32 devices in a mesh: blk: 8 (over z, y), req: 4 (over x, core).
Axes of the slice: x: 2, y: 2, z: 4, core: 2. Of those that a mesh axis runs over, the one named last changes fastest.
Arguments:
- tokens_in: bfloat16 [4, 1024, 1792], P('req', 'blk'), may hold values from -6 to 6
- query_weight: bfloat16 [1792, 256], replicated, may hold values from -0.125 to 0.125
- key_weight: bfloat16 [1792, 256], replicated, may hold values from -0.125 to 0.125
- value_weight: bfloat16 [1792, 1792], replicated, may hold values from -0.125 to 0.125
- conv_weight: float32 [3, 1792], replicated, may hold values from -3 to 3
- prompt_lengths: int32 [4], P('req'), may hold values from 512 to 1024, as said below
- decode_map: int32 [4], P('req'), may hold values from 0 to 3, each once
Outputs:
- mixed: bfloat16 [4, 1024, 1792], P('req', 'blk')
- decode_state: float32 [4, 273, 1792], P('req', None, 'blk')
- decode_norm: float32 [4, 273, 16], P('req')
The draws below stay inside these ranges and needn't reach their ends.
Inputs may be any that keep to these rules, and one draw needn't show every extreme that they name: `prompt_lengths`: some prompt has exactly 1024 live tokens. `decode_map`: each decode slot receives exactly one prompt.
All inputs are finite; a program needn't handle non-finite values.
Results may differ from the reference program's by a relative error of at most 0.0057.
Values may be sent and summed in bfloat16 or wider, within the bound.
No kernel may reach another device: no remote copies, remote signals or barrier semaphores. Data moves between devices by JAX's collectives and lax.ppermute only.
A program may use at most 384 MiB of HBM per device.

```python
import math
import jax
import jax.numpy as jnp
from jax import lax

D = 1792
HEADS = 16
FEAT = 16
CONV = 3
HV = 112
EXPAND = 273
LEN = 1024
PROMPTS = 4


def draw_prompt_lengths(key, part):
    lengths = jax.random.randint(key, (PROMPTS,), LEN // 2, LEN + 1)
    chosen = jax.random.randint(jax.random.fold_in(key, 1), (), 0, PROMPTS)
    return jnp.where(jnp.arange(PROMPTS) == chosen, LEN, lengths).astype(jnp.int32)


def block_scale(rng, shape, split, least, largest):
    loudness, own = 1.0, jax.random.fold_in(rng, 6)
    for position, blocks in split:
        steps = jnp.exp(jax.random.uniform(jax.random.fold_in(own, position), (blocks,), jnp.float32, least / len(split), largest / len(split)))
        loudness = loudness * jnp.repeat(steps, shape[position] // blocks).reshape([-1 if axis == position else 1 for axis in range(len(shape))])
    return loudness


def centred(own_key, shape, width, most, cuts=(), kind=jnp.bfloat16):
    array = jax.random.normal(own_key, shape, jnp.float32) * width
    if len(cuts) > 0:
        array = block_scale(own_key, shape, cuts, -0.22, 0.18) * array
    return jnp.clip(array, min=-most, max=most).astype(kind)


def setup_inputs(seed: int = 0) -> dict:
    seeds = jax.random.split(jax.random.key(seed), 8)
    tokens_in = centred(seeds[0], (PROMPTS, LEN, D), 1.0, 6.0, ((0, 4), (1, 8)))
    query_weight = centred(seeds[1], (D, HEADS * FEAT), D ** -0.5, 0.125)
    key_weight = centred(seeds[2], (D, HEADS * FEAT), D ** -0.5, 0.125)
    value_weight = centred(seeds[3], (D, D), D ** -0.5, 0.125)
    conv_weight = centred(seeds[4], (CONV, D), 0.6, 3.0, (), jnp.float32)
    prompt_lengths = draw_prompt_lengths(jax.random.fold_in(seeds[7], 71), 0)
    decode_map = jax.random.permutation(seeds[6], PROMPTS).astype(jnp.int32)
    return {"tokens_in": tokens_in, "query_weight": query_weight, "key_weight": key_weight, "value_weight": value_weight, "conv_weight": conv_weight, "prompt_lengths": prompt_lengths, "decode_map": decode_map}


def features(x):
    half = x * FEAT ** (-0.25)
    outer = half[..., :, None] * half[..., None, :]
    flat = outer.reshape(outer.shape[:-2] + (FEAT * FEAT,)) * math.sqrt(0.5)
    ones = jnp.ones(x.shape[:-1] + (1,), jnp.float32)
    return jnp.concatenate([ones, half, flat], -1)

def reference(tokens_in, query_weight, key_weight, value_weight, conv_weight, prompt_lengths, decode_map):
    block = math.gcd(LEN, 512)
    count = LEN // block
    hi = lax.Precision.HIGHEST
    outs = []
    state_out = jnp.zeros((PROMPTS, EXPAND, D), jnp.float32)
    norm_out = jnp.zeros((PROMPTS, EXPAND, HEADS), jnp.float32)
    causal = jnp.arange(block)[:, None] >= jnp.arange(block)[None, :]
    for prompt in range(PROMPTS):
        inputs = tokens_in[prompt]
        queries = jnp.dot(inputs, query_weight, preferred_element_type=jnp.float32).reshape(LEN, HEADS, FEAT)
        keys = jnp.dot(inputs, key_weight, preferred_element_type=jnp.float32).reshape(LEN, HEADS, FEAT)
        values = jnp.dot(inputs, value_weight, preferred_element_type=jnp.float32).astype(jnp.bfloat16)
        padded = jnp.concatenate([jnp.zeros((CONV - 1, D), jnp.float32), values.astype(jnp.float32)], 0)
        conv = jnp.zeros((LEN, D), jnp.float32)
        for tap in range(CONV):
            conv = conv + conv_weight[tap][None, :] * padded[CONV - 1 - tap:CONV - 1 - tap + LEN]
        conv_v = conv.astype(jnp.bfloat16).astype(jnp.float32).reshape(LEN, HEADS, HV)
        live = (jnp.arange(LEN, dtype=jnp.int32) < prompt_lengths[prompt]).astype(jnp.float32)

        def step(carry, pieces):
            state, norm = carry
            qb, kb, cb, lb = pieces
            pq = features(qb)
            pk = features(kb) * lb[:, None, None]
            scores = jnp.einsum('thf,shf->hts', pq, pk, precision=hi) * causal[None]
            num = jnp.einsum('hts,shc->thc', scores, cb, precision=hi) + jnp.einsum('thf,fhc->thc', pq, state, precision=hi)
            den = lax.optimization_barrier(jnp.sum(scores, -1)).T + jnp.einsum('thf,fh->th', pq, norm, precision=hi) + (1.0 - lb)[:, None]
            result = jnp.where(lb[:, None, None] > 0, num / den[..., None], 0.0)
            state = state + jnp.einsum('thf,thc->fhc', pk, cb, precision=hi)
            norm = norm + lax.optimization_barrier(jnp.sum(pk, 0)).T
            return ((state, norm), result)
        init = (jnp.zeros((EXPAND, HEADS, HV), jnp.float32), jnp.zeros((EXPAND, HEADS), jnp.float32))
        pieces = (queries.reshape(count, block, HEADS, FEAT), keys.reshape(count, block, HEADS, FEAT), conv_v.reshape(count, block, HEADS, HV), live.reshape(count, block))
        (state, norm), results = lax.scan(step, init, pieces)
        outs.append(results.reshape(LEN, D).astype(jnp.bfloat16))
        slot = decode_map[prompt]
        state_out = state_out.at[slot].set(state.reshape(EXPAND, D))
        norm_out = norm_out.at[slot].set(norm)
    return (jnp.stack(outs, 0), state_out, norm_out)
```

```python
import functools
import math

import jax
import jax.numpy as jnp
import numpy as np
from jax import lax
from jax.experimental import pallas as pl
from jax.experimental.pallas import tpu as pltpu
from jax.sharding import PartitionSpec as P

HEADS = 16
FEAT = 16
CONV = 3

GROUP = 4
SYM = 160
LANES = 128
SUMS = 48
INFO = 34
f32 = jnp.float32
bf16 = jnp.bfloat16
NT = (((1,), (1,)), ((), ()))
NN = (((1,), (0,)), ((), ()))


def dot(a, b, dims=NN):
    return lax.dot_general(a, b, dims, preferred_element_type=f32)


def iota(shape, axis):
    return lax.broadcasted_iota(jnp.int32, shape, axis)


def symmetric(y, scale_square):
    twice = jnp.concatenate([y, y], 0)
    rows = [y * y * scale_square] + [y * twice[o : o + FEAT] for o in range(1, 8)]
    rest = jnp.where(iota((8, y.shape[1]), 0) == 0, 1.0, 0.0)
    return jnp.concatenate(rows + [y, y[:8] * y[8:], rest], 0)


def project_kernel(
    length, x, wq, wk, wv, conv, o0, o1, o2, o3, taps, wv_v, wqk_v, vt, qkt, taps_v, sems
):
    rows = x.shape[0]
    width = wv.shape[1]
    keyed = wq.shape[1]
    tile = 256
    copies = [
        pltpu.make_async_copy(wk, wqk_v.at[1], sems.at[0]),
        pltpu.make_async_copy(wq, wqk_v.at[0], sems.at[1]),
    ]
    for j in range(width // tile):
        cut = pl.ds(j * tile, tile)
        copies.append(pltpu.make_async_copy(wv.at[:, cut], wv_v.at[:, cut], sems.at[2 + j]))
    for copy in copies:
        copy.start()
    place = lax.axis_index("blk")
    mine = lax.rem(place, GROUP)
    padded = jnp.concatenate([conv[...], jnp.zeros((8 - CONV, width), f32)], 0)
    for j in range(width // LANES):
        taps_v[j * LANES : (j + 1) * LANES, :] = padded[:, j * LANES : (j + 1) * LANES].T
    half = width // 2
    slab = half // GROUP
    taps[0:slab, :] = taps_v[pl.ds(pl.multiple_of(slab * mine, 32), slab), :]
    taps[slab : 2 * slab, :] = taps_v[pl.ds(pl.multiple_of(half + slab * mine, 32), slab), :]
    inputs = x[...]
    for j, copy in enumerate(copies):
        copy.wait()
        if j < 2:
            got = dot(inputs, wqk_v[1 - j])
            qkt[1 - j] = got.T.astype(bf16)
        else:
            at = (j - 2) * tile
            got = dot(inputs, wv_v[:, at : at + tile])
            vt[at : at + tile, :] = got.T.astype(bf16)
    alive = (place * rows + iota((1, rows), 1) < length[0]).astype(f32)
    keys = (qkt[1].astype(f32) * alive).astype(bf16)
    gram = dot(keys, keys, NT)
    same = iota((keyed, keyed), 0) // FEAT == iota((keyed, keyed), 1) // FEAT
    pick = (lax.rem(iota((FEAT, keyed), 1), FEAT) == iota((FEAT, keyed), 0)).astype(bf16)
    folded = dot(pick, jnp.where(same, gram, 0.0).astype(bf16))
    plain = dot(jnp.ones((8, rows), bf16), keys, NT)
    third = jnp.concatenate(
        [plain[0:1, :LANES], plain[0:1, LANES:], jnp.zeros((FEAT - 2, LANES), f32)], 0
    )
    sums = jnp.concatenate([folded[:, :LANES], folded[:, LANES:], third], 0).astype(bf16)
    part = keyed // 2 // GROUP
    for s, out in enumerate((o0, o1, o2, o3)):
        dest = mine ^ s
        out[0:slab, :] = vt[pl.ds(pl.multiple_of(slab * dest, 32), slab), :]
        out[slab : 2 * slab, :] = vt[pl.ds(pl.multiple_of(half + slab * dest, 32), slab), :]
        at = 2 * slab
        for which in (1, 0):
            for base in (0, keyed // 2):
                start = pl.multiple_of(base + part * dest, 32)
                out[at : at + part, :] = qkt[which, pl.ds(start, part), :]
                at += part
        out[at : at + SUMS, :] = sums


def project(length, x, wq, wk, wv, conv):
    rows, width = x.shape
    keyed = wq.shape[1]
    total = (width + 2 * keyed) // GROUP + SUMS
    payload = jax.ShapeDtypeStruct((total, rows), bf16)
    taps = jax.ShapeDtypeStruct((width // GROUP, 8), f32)
    vmem = pl.BlockSpec(memory_space=pltpu.VMEM)
    hbm = pl.BlockSpec(memory_space=pl.ANY)
    return pl.pallas_call(
        project_kernel,
        out_shape=[payload] * 4 + [taps],
        in_specs=[pl.BlockSpec(memory_space=pltpu.SMEM), vmem, hbm, hbm, hbm, vmem],
        out_specs=[vmem] * 5,
        scratch_shapes=[
            pltpu.VMEM((width, width), bf16),
            pltpu.VMEM((2, width, keyed), bf16),
            pltpu.VMEM((width, rows), bf16),
            pltpu.VMEM((2, keyed, rows), bf16),
            pltpu.VMEM((width, 8), f32),
            pltpu.SemaphoreType.DMA((2 + width // 256,)),
        ],
        compiler_params=pltpu.CompilerParams(vmem_limit_bytes=40 * 2**20),
        cost_estimate=pl.CostEstimate(
            flops=2 * rows * width * (width + 2 * keyed),
            bytes_accessed=2 * width * (width + 2 * keyed),
            transcendentals=0,
        ),
    )(length, x, wq, wk, wv, conv)


def state_kernel(length, p0, p1, p2, p3, taps, aug, qk, state, held):
    rows = p0.shape[1]
    place = lax.axis_index("blk")
    mine, group = lax.rem(place, GROUP), place // GROUP
    values = p0.shape[0] - SUMS - 2 * HEADS // GROUP * FEAT
    local = HEADS // GROUP
    size = values // local
    tokens = GROUP * rows
    for s, ref in enumerate((p0, p1, p2, p3)):
        held[mine ^ s] = ref[0 : held.shape[1], :]
    sums = p0[held.shape[1] :, :].astype(f32) + p1[held.shape[1] :, :].astype(f32)
    sums += p2[held.shape[1] :, :].astype(f32) + p3[held.shape[1] :, :].astype(f32)
    state[local * SYM :, :] = sums.astype(bf16)
    for b in range(GROUP):
        qk[:, b * rows : (b + 1) * rows] = held[b, values:, :]
    alive = (group * tokens + iota((1, tokens), 1) < length[0]).astype(f32)
    token = iota((FEAT, tokens), 1)
    row = iota((FEAT, tokens), 0)
    marks = (row == 0) | ((row == 1) & (token == 0)) | ((row == 2) & (token == 1))
    marks = jnp.where(marks, alive, 0.0).astype(bf16)
    lane = iota((size, rows), 1)
    last = iota((FEAT, rows), 0)
    ends = iota((FEAT, rows), 1)
    ends = ((last == 9) & (ends == rows - 1)) | ((last == 10) & (ends == rows - 2))
    ends = ends.astype(bf16)
    for h in range(local):
        cut = slice(h * size, (h + 1) * size)
        tap = [jnp.broadcast_to(taps[cut, t : t + 1], (size, rows)) for t in range(CONV)]
        before = [jnp.zeros((size, rows), f32)] * 2
        pieces = []
        for b in range(GROUP):
            now = held[b, cut, :].astype(f32)
            rolled = [pltpu.roll(now, 1, 1), pltpu.roll(now, 2, 1)]
            one = jnp.where(lane < 1, before[0], rolled[0])
            two = jnp.where(lane < 2, before[1], rolled[1])
            before = rolled
            mixed = tap[0] * now + tap[1] * one + tap[2] * two
            live = alive[:, b * rows : (b + 1) * rows]
            pieces.append(jnp.where(live > 0, mixed, 0.0).astype(bf16))
        aug_h = jnp.concatenate([jnp.concatenate(pieces, 1), marks], 0)
        aug[h] = aug_h
        y = qk[h * FEAT : (h + 1) * FEAT, :].astype(f32) * FEAT ** (-0.25)
        own = dot(symmetric(y, 1.0).astype(bf16), aug_h, NT)
        edge = dot(ends, held[GROUP - 1, h * size : h * size + LANES, :], NT)
        state[h * SYM : h * SYM + 144, :] = own[:144].astype(bf16)
        state[h * SYM + 144 : (h + 1) * SYM, :] = (own[144:] + edge).astype(bf16)


def group_state(length, payloads, taps):
    total, rows = payloads[0].shape
    local = HEADS // GROUP
    vmem = pl.BlockSpec(memory_space=pltpu.VMEM)
    tokens = GROUP * rows
    return pl.pallas_call(
        state_kernel,
        out_shape=[
            jax.ShapeDtypeStruct((local, LANES, tokens), bf16),
            jax.ShapeDtypeStruct((2 * local * FEAT, tokens), bf16),
            jax.ShapeDtypeStruct((local * SYM + SUMS, LANES), bf16),
        ],
        in_specs=[pl.BlockSpec(memory_space=pltpu.SMEM)] + [vmem] * 5,
        out_specs=[vmem] * 3,
        scratch_shapes=[pltpu.VMEM((GROUP, total - SUMS, rows), bf16)],
        compiler_params=pltpu.CompilerParams(vmem_limit_bytes=32 * 2**20),
        cost_estimate=pl.CostEstimate(flops=200_000_000, bytes_accessed=2_000_000, transcendentals=0),
    )(length, *payloads, taps)


def local_kernel(aug, qk, num):
    local, _, tokens = aug.shape
    keyed = local * FEAT
    half = tokens // 2
    keys = qk[0:keyed, :].astype(f32).T.astype(bf16)
    queries = qk[keyed:, :]
    head = iota((keyed, tokens), 0) // FEAT
    causal = iota((half, half), 0) <= iota((half, half), 1)

    def scores(d):
        return 1.0 + d * (0.25 + d * 0.03125)

    for h in range(local):
        only = jnp.where(head == h, queries, jnp.zeros_like(queries))
        first = scores(dot(keys[:half], only[:, :half]))
        first = jnp.where(causal, first, 0.0).astype(bf16)
        num[h, :, 0:half] = dot(aug[h, :, 0:half], first)
        lower = scores(dot(keys[half:], only[:, half:]))
        lower = jnp.where(causal, lower, 0.0).astype(bf16)
        upper = scores(dot(keys[:half], only[:, half:])).astype(bf16)
        num[h, :, half:] = dot(aug[h, :, 0:half], upper) + dot(aug[h, :, half:], lower)


def local_part(aug, qk):
    local, _, tokens = aug.shape
    vmem = pl.BlockSpec(memory_space=pltpu.VMEM)
    return pl.pallas_call(
        local_kernel,
        out_shape=jax.ShapeDtypeStruct(aug.shape, f32),
        in_specs=[vmem] * 2,
        out_specs=vmem,
        compiler_params=pltpu.CompilerParams(vmem_limit_bytes=32 * 2**20),
        cost_estimate=pl.CostEstimate(
            flops=4 * local * tokens * tokens * LANES, bytes_accessed=2_000_000, transcendentals=0
        ),
    )(aug, qk)


def finish_kernel(length, slot, num, own, got, qk, taps, r0, r1, r2, r3, route, scr, tot):
    local, _, tokens = num.shape
    rows = tokens // GROUP
    size = taps.shape[0] // local
    keyed = local * FEAT
    place = lax.axis_index("blk")
    mine, group = lax.rem(place, GROUP), place // GROUP
    upper = group == 1
    weight = jnp.where(upper, 1.0, 0.0)
    alive = group * tokens + iota((1, tokens), 1) < length[0]
    first = (iota((size, LANES), 1) == 0) & upper
    aux = iota((LANES - size, SYM), 0)
    for h in range(local):
        here = own[h * SYM : (h + 1) * SYM, :].astype(f32).T
        there = got[h * SYM : (h + 1) * SYM, :].astype(f32).T
        low = jnp.where(upper, there, here)
        high = jnp.where(upper, here, there)
        tap = taps[h * size : (h + 1) * size, :]
        last, second = low[:size, 153:154], low[:size, 154:155]
        change0 = tap[:, 1:2] * last + tap[:, 2:3] * second
        change1 = tap[:, 2:3] * last
        key0, key1 = high[size + 1 : size + 2, :], high[size + 2 : size + 3, :]
        body = low[:size] + change0 * key0 + change1 * key1
        tail = jnp.where(aux == 2, key1, low[size:])
        prior = jnp.concatenate([body, tail], 0)
        tot[h] = jnp.concatenate([body + high[:size], low[size:] + high[size:]], 0)
        y = qk[keyed + h * FEAT : keyed + (h + 1) * FEAT, :].astype(f32) * FEAT ** (-0.25)
        feats = symmetric(y, 0.5).astype(bf16)
        all_num = num[h] + weight * dot(prior.astype(bf16), feats)
        den = jnp.where(alive, all_num[size : size + 1, :], 1.0)
        inverse = jnp.where(alive, 1.0 / den, 0.0)
        top = all_num[:size]
        extra = all_num[size + 2 : size + 3, 0:1]
        edge = top[:, :LANES] - jnp.where(first, change1 * extra, 0.0)
        top = jnp.concatenate([edge, top[:, LANES:]], 1)
        result = (top * inverse).astype(bf16)
        for b in range(GROUP):
            scr[b, h * size : (h + 1) * size, :] = result[:, b * rows : (b + 1) * rows]
    for s, out in enumerate((r0, r1, r2, r3)):
        out[...] = scr[mine ^ s]
    chosen = local // 2
    for c in range(chosen):
        final = jnp.where(upper, tot[chosen + c], tot[c])
        route[c * SYM : (c + 1) * SYM, :] = final.T.astype(bf16)
    sums = own[local * SYM :, :].astype(f32) + got[local * SYM :, :].astype(f32)
    r, c = iota(sums.shape, 0), iota(sums.shape, 1)
    count = length[0]
    sums = jnp.where((r == INFO) & (c == 0), slot[0].astype(f32), sums)
    sums = jnp.where((r == INFO) & (c == 1), (count // 256).astype(f32), sums)
    sums = jnp.where((r == INFO) & (c == 2), lax.rem(count, 256).astype(f32), sums)
    route[chosen * SYM :, :] = sums.astype(bf16)


def finish(length, slot, num, own, got, qk, taps):
    local, _, tokens = num.shape
    rows = tokens // GROUP
    width = taps.shape[0]
    vmem = pl.BlockSpec(memory_space=pltpu.VMEM)
    smem = pl.BlockSpec(memory_space=pltpu.SMEM)
    result = jax.ShapeDtypeStruct((width, rows), bf16)
    return pl.pallas_call(
        finish_kernel,
        out_shape=[result] * 4 + [jax.ShapeDtypeStruct((local // 2 * SYM + SUMS, LANES), bf16)],
        in_specs=[smem, smem] + [vmem] * 5,
        out_specs=[vmem] * 5,
        scratch_shapes=[
            pltpu.VMEM((GROUP, width, rows), bf16),
            pltpu.VMEM((local, LANES, SYM), f32),
        ],
        compiler_params=pltpu.CompilerParams(vmem_limit_bytes=32 * 2**20),
        cost_estimate=pl.CostEstimate(flops=100_000_000, bytes_accessed=2_000_000, transcendentals=0),
    )(length, slot, num, own, got, qk, taps)


def place_kernel(r0, r1, r2, r3, mixed, scr):
    width = scr.shape[0]
    mine = lax.rem(lax.axis_index("blk"), GROUP)
    half = width // 2
    slab = half // GROUP
    for s, ref in enumerate((r0, r1, r2, r3)):
        dest = mine ^ s
        scr[pl.ds(pl.multiple_of(slab * dest, 32), slab), :] = ref[0:slab, :]
        scr[pl.ds(pl.multiple_of(half + slab * dest, 32), slab), :] = ref[slab:, :]
    for j in range(width // LANES):
        cut = slice(j * LANES, (j + 1) * LANES)
        mixed[0, :, cut] = scr[cut, :].astype(f32).T.astype(bf16)


def place_tokens(results):
    part, rows = results[0].shape
    width = part * GROUP
    vmem = pl.BlockSpec(memory_space=pltpu.VMEM)
    return pl.pallas_call(
        place_kernel,
        out_shape=jax.ShapeDtypeStruct((1, rows, width), bf16),
        in_specs=[vmem] * 4,
        out_specs=vmem,
        scratch_shapes=[pltpu.VMEM((width, rows), bf16)],
        compiler_params=pltpu.CompilerParams(vmem_limit_bytes=32 * 2**20),
        cost_estimate=pl.CostEstimate(flops=1000, bytes_accessed=1_000_000, transcendentals=0),
    )(*results)


def expand_kernel(near, far, spread, state, norm):
    me = lax.axis_index("req").astype(f32)
    heads = (near.shape[1] - SUMS) // SYM
    info = heads * SYM + INFO
    kept = jnp.zeros(near.shape[1:], f32)
    for ref in (near, far):
        for c in range(2):
            kept += jnp.where(ref[c, info : info + 1, 0:1].astype(f32) == me, ref[c].astype(f32), 0.0)
    size = state.shape[2] // heads
    expand = state.shape[1]
    scale = jnp.where(iota((expand, LANES), 0) > FEAT, math.sqrt(0.5), 1.0)
    for c in range(heads):
        whole = dot(spread[...], kept[c * SYM : (c + 1) * SYM].astype(bf16)) * scale
        state[0, :, c * size : (c + 1) * size] = whole[:, :size]
    sums = kept[heads * SYM :]
    keyed = HEADS * FEAT
    products = jnp.concatenate([sums[:FEAT], sums[FEAT : 2 * FEAT]], 1)
    plain = jnp.concatenate([sums[2 * FEAT : 2 * FEAT + 1], sums[2 * FEAT + 1 : 2 * FEAT + 2]], 1)
    big = jnp.concatenate(
        [jnp.broadcast_to(plain * FEAT ** (-0.25), (FEAT, keyed))]
        + [products * FEAT ** (-0.5)] * FEAT,
        0,
    )
    r, j = iota(big.shape, 0), iota(big.shape, 1)
    entry = jnp.where(r < FEAT, r, r // FEAT - 1)
    big = jnp.where(lax.rem(j, FEAT) == entry, big, 0.0)
    gather = (iota((keyed, HEADS), 0) // FEAT == iota((keyed, HEADS), 1)).astype(bf16)
    rest = dot(big.astype(bf16), gather)
    rest = rest * jnp.where(iota(rest.shape, 0) >= FEAT, math.sqrt(0.5), 1.0)
    count = sums[INFO : INFO + 1, 1:2] * 256.0 + sums[INFO : INFO + 1, 2:3]
    norm[0, 0:1, :] = jnp.broadcast_to(count, (1, HEADS))
    norm[0, 1:expand, :] = rest


def spread_rows():
    table = np.zeros((1 + FEAT + FEAT * FEAT, SYM), np.float32)
    table[0, 152] = 1
    for a in range(FEAT):
        table[1 + a, 128 + a] = 1
        for b in range(FEAT):
            o = (b - a) % FEAT
            at = o * FEAT + a if o < 8 else (144 + min(a, b) if o == 8 else (FEAT - o) * FEAT + b)
            table[1 + FEAT + a * FEAT + b, at] = 1
    return table


def expand_state(near, far, columns):
    vmem = pl.BlockSpec(memory_space=pltpu.VMEM)
    spread = jnp.asarray(spread_rows(), bf16)
    expand = spread.shape[0]
    return pl.pallas_call(
        expand_kernel,
        out_shape=[
            jax.ShapeDtypeStruct((1, expand, columns), f32),
            jax.ShapeDtypeStruct((1, expand, HEADS), f32),
        ],
        in_specs=[vmem] * 3,
        out_specs=[vmem] * 2,
        compiler_params=pltpu.CompilerParams(vmem_limit_bytes=32 * 2**20),
        cost_estimate=pl.CostEstimate(flops=40_000_000, bytes_accessed=1_000_000, transcendentals=0),
    )(near, far, spread)


def swap(array, axis, by):
    return lax.ppermute(array, axis, [(i, i ^ by) for i in range(lax.axis_size(axis))])


def two_groups(
    tokens_in, query_weight, key_weight, value_weight, conv_weight, prompt_lengths, decode_map
):
    width = tokens_in.shape[2]
    *payloads, taps = project(
        prompt_lengths, tokens_in[0], query_weight, key_weight, value_weight, conv_weight
    )
    payloads = [payloads[0]] + [swap(payloads[s], "blk", s) for s in (1, 2, 3)]
    aug, qk, own = group_state(prompt_lengths, payloads, taps)
    got = swap(own, "blk", GROUP)
    num = local_part(aug, qk)
    *results, route = finish(prompt_lengths, decode_map, num, own, got, qk, taps)
    results = [results[0]] + [swap(results[s], "blk", s) for s in (1, 2, 3)]
    near = jnp.stack([route, swap(route, "req", 2)])
    far = swap(near, "req", 1)
    mixed = place_tokens(results)
    state, norm = expand_state(near, far, width // lax.axis_size("blk"))
    return (mixed, state, norm)


def from_behind(array, axis, by):
    devices = lax.axis_size(axis)
    pairs = [(i, i + by) for i in range(devices) if 0 <= i + by < devices]
    return lax.ppermute(array, axis, pairs)


def entering(part, axis, combine, identity):
    place = lax.axis_index(axis)
    gathered = jax.tree.map(lambda a: lax.all_gather(a, axis), part)
    state = jax.tree.map(lambda a, e: jnp.zeros_like(a) + jnp.asarray(e, a.dtype), part, identity)

    def one(turn, state):
        return combine(
            state, jax.tree.map(lambda a: lax.dynamic_index_in_dim(a, turn, 0, False), gathered)
        )

    return lax.fori_loop(0, place, one, state)


def features_last(x):
    half = x * FEAT ** (-0.25)
    outer = half[:, :, None, :] * half[:, None, :, :]
    flat = outer.reshape(half.shape[0], FEAT * FEAT, half.shape[2]) * math.sqrt(0.5)
    ones = jnp.ones((half.shape[0], 1, half.shape[2]), jnp.float32)
    return jnp.concatenate([ones, half, flat], 1)


def add_pair(earlier, later):
    return (earlier[0] + later[0], earlier[1] + later[1])


def route_slot(pair, decode_map):
    groups = lax.axis_size("req")
    slots = (jnp.arange(groups, dtype=jnp.int32) == decode_map[0]).astype(jnp.float32)
    sent = (slots[:, None, None] * pair[0][None], slots[:, None, None] * pair[1][None])
    got = (
        lax.all_to_all(sent[0], "req", split_axis=0, concat_axis=0, tiled=True),
        lax.all_to_all(sent[1], "req", split_axis=0, concat_axis=0, tiled=True),
    )
    return (jnp.sum(got[0], 0), jnp.sum(got[1], 0))


def reduce_blocks(pair):
    return (
        lax.psum_scatter(pair[0], "blk", scatter_dimension=1, tiled=True),
        lax.psum_scatter(pair[1], "blk", scatter_dimension=1, tiled=True),
    )


def any_blocks(
    tokens_in, query_weight, key_weight, value_weight, conv_weight, prompt_lengths, decode_map
):
    rows = tokens_in.shape[1]
    width = tokens_in.shape[2]
    blocks = lax.axis_size("blk")
    head_size = width // HEADS
    hi = lax.Precision.HIGHEST
    inputs = tokens_in[0]
    queries = jnp.einsum(
        "dk,td->kt", query_weight, inputs, preferred_element_type=jnp.float32
    ).reshape(HEADS, FEAT, rows)
    keys = jnp.einsum("dk,td->kt", key_weight, inputs, preferred_element_type=jnp.float32).reshape(
        HEADS, FEAT, rows
    )
    values = jnp.dot(inputs, value_weight, preferred_element_type=jnp.float32).astype(jnp.bfloat16)
    earlier = from_behind(values[rows - (CONV - 1) :], "blk", 1)
    extended = jnp.concatenate([earlier, values], 0).astype(jnp.float32)
    conv = jnp.zeros((rows, width), jnp.float32)
    for tap in range(CONV):
        conv = conv + conv_weight[tap][None, :] * extended[CONV - 1 - tap : CONV - 1 - tap + rows]
    conv_t = conv.astype(jnp.bfloat16).astype(jnp.float32).T.reshape(HEADS, head_size, rows)
    start = lax.axis_index("blk") * rows
    live = (start + jnp.arange(rows, dtype=jnp.int32) < prompt_lengths[0]).astype(jnp.float32)
    feat_q = features_last(queries)
    feat_k = features_last(keys) * live[None, None, :]
    own_state = jnp.einsum("hft,hct->hfc", feat_k, conv_t, precision=hi)
    own_norm = jnp.sum(feat_k, 2)
    zero_state = jnp.zeros_like(own_state)
    zero_norm = jnp.zeros_like(own_norm)
    prior_state, prior_norm = entering(
        (own_state, own_norm), "blk", add_pair, (zero_state, zero_norm)
    )
    causal = (jnp.arange(rows)[:, None] >= jnp.arange(rows)[None, :]).astype(jnp.float32)
    scores = jnp.einsum("hft,hfs->hts", feat_q, feat_k, precision=hi) * causal[None]
    num = jnp.einsum("hts,hcs->hct", scores, conv_t, precision=hi) + jnp.einsum(
        "hft,hfc->hct", feat_q, prior_state, precision=hi
    )
    den = (
        jnp.sum(scores, -1)
        + jnp.einsum("hft,hf->ht", feat_q, prior_norm, precision=hi)
        + (1.0 - live)[None, :]
    )
    result = jnp.where(live[None, None, :] > 0, num / den[:, None, :], 0.0)
    mixed = result.reshape(width, rows).T.reshape(1, rows, width).astype(jnp.bfloat16)
    state_flat = jnp.transpose(own_state, (1, 0, 2)).reshape(own_state.shape[1], width)
    pair = (state_flat, jnp.tile(own_norm.T, (1, blocks)))
    final = route_slot(reduce_blocks(pair), decode_map)
    return (mixed, final[0][None], final[1][None])


def solution(mesh):
    def on_device(*args):
        rows = args[0].shape[1]
        if mesh.shape["blk"] == 2 * GROUP and mesh.shape["req"] == 4 and rows == LANES:
            return two_groups(*args)
        return any_blocks(*args)

    return jax.shard_map(
        on_device,
        mesh=mesh,
        in_specs=(P("req", "blk", None), P(), P(), P(), P(), P("req"), P("req")),
        out_specs=(P("req", "blk", None), P("req", None, "blk"), P("req", None, None)),
        check_vma=False,
    )
```

```python
import functools
import math

import jax
import jax.numpy as jnp
import numpy as np
from jax import lax
from jax.experimental import pallas as pl
from jax.experimental.pallas import tpu as pltpu
from jax.sharding import PartitionSpec as P

HEADS = 16
FEAT = 16
CONV = 3

GROUP = 4
SYM = 160
LANES = 128
INFO = 159
LOCAL = HEADS // GROUP // 2
f32 = jnp.float32
bf16 = jnp.bfloat16
NT = (((1,), (1,)), ((), ()))
NN = (((1,), (0,)), ((), ()))


def dot(a, b, dims=NN):
    return lax.dot_general(a, b, dims, preferred_element_type=f32)


def iota(shape, axis):
    return lax.broadcasted_iota(jnp.int32, shape, axis)


def symmetric(y, scale_square):
    twice = jnp.concatenate([y, y], 0)
    rows = [y * y * scale_square] + [y * twice[o : o + FEAT] for o in range(1, 8)]
    rest = jnp.where(iota((8, y.shape[1]), 0) == 0, 1.0, 0.0)
    return jnp.concatenate(rows + [y, y[:8] * y[8:], rest], 0)


def call(kernel, outs, scratch, limit, flops, moved, args, spaces=(), after=()):
    vmem = pl.BlockSpec(memory_space=pltpu.VMEM)
    given = [pl.BlockSpec(memory_space=space) for space in spaces]
    if after:
        body, plain = kernel, len(args)

        def kernel(*refs):
            body(*refs[:plain], *refs[plain + len(after) :])

    return pl.pallas_call(
        kernel,
        out_shape=[jax.ShapeDtypeStruct(shape, dtype) for shape, dtype in outs],
        in_specs=given
        + [vmem] * (len(args) - len(given))
        + [pl.BlockSpec(memory_space=pl.ANY)] * len(after),
        out_specs=[vmem] * len(outs),
        scratch_shapes=scratch,
        compiler_params=pltpu.CompilerParams(vmem_limit_bytes=int(limit * 2**20)),
        cost_estimate=pl.CostEstimate(flops=flops, bytes_accessed=moved, transcendentals=0),
    )(*args, *after)


TILES = (384, 512)


def key_sums(keys):
    keyed, rows = keys.shape
    gram = dot(keys, keys, NT)
    same = iota((keyed, keyed), 0) // FEAT == iota((keyed, keyed), 1) // FEAT
    entry, lane = iota((FEAT, keyed), 0), iota((FEAT, keyed), 1)
    pick = (lax.rem(lane, FEAT) == entry).astype(bf16)
    folded = dot(pick, jnp.where(same, gram, 0.0).astype(bf16))
    plain = dot(jnp.ones((8, rows), bf16), keys, NT)
    mirror = lax.rem(entry - lax.rem(lane, FEAT) + FEAT, FEAT) == 9
    return jnp.where(mirror, plain[0:1], folded).astype(bf16)


def project_kernel(half, *refs):
    x, wq, wk, wv = refs[:4]
    refs = refs[4:]
    if half:
        length, early, o0, o1, o2, o3 = refs[:6]
        refs = refs[6:]
    else:
        o0, o1, o2, o3, early = refs[:5]
        refs = refs[5:]
    x_v, wqk_v, wv_v, vt, qkt, sems = refs[:6]
    rows = x.shape[1]
    width = wv.shape[1] // 2
    keyed = wq.shape[1] // 2
    get_x = pltpu.make_async_copy(x.at[0], x_v, sems.at[0])
    keyed_cut = pl.ds(half * keyed, keyed)
    get_k = pltpu.make_async_copy(wk.at[:, keyed_cut], wqk_v.at[:, pl.ds(0, keyed)], sems.at[1])
    get_q = pltpu.make_async_copy(wq.at[:, keyed_cut], wqk_v.at[:, pl.ds(keyed, keyed)], sems.at[2])
    copies, at = [], 0
    for j, tile in enumerate(TILES):
        source = wv.at[:, pl.ds(half * width + at, tile)]
        copies.append(pltpu.make_async_copy(source, wv_v.at[:, pl.ds(at, tile)], sems.at[3 + j]))
        at += tile
    for copy in (get_x, get_k, get_q, *copies):
        copy.start()
    place = lax.axis_index("blk")
    mine = lax.rem(place, GROUP)
    slab = width // GROUP
    get_x.wait()
    get_k.wait()
    get_q.wait()
    inputs = x_v[...]
    qkt[...] = dot(inputs, wqk_v[...]).T.astype(bf16)
    at = 0
    for tile, copy in zip(TILES, copies):
        copy.wait()
        vt[at : at + tile, :] = dot(inputs, wv_v[:, at : at + tile]).T.astype(bf16)
        at += tile
    part = keyed // GROUP
    for s, out in enumerate((o0, o1, o2, o3)):
        dest = mine ^ s
        out[0:slab, :] = vt[pl.ds(pl.multiple_of(slab * dest, 32), slab), :]
        for base, at in ((0, slab), (keyed, slab + part)):
            start = pl.multiple_of(base + part * dest, 32)
            out[at : at + part, :] = qkt[pl.ds(start, part), :]
    if not half:
        early[...] = qkt[0:keyed, :]
        return
    alive = place * rows + iota((1, rows), 1) < length[...]
    alive = jnp.where(alive, 1.0, 0.0).astype(bf16)
    sums = [key_sums(early[...] * alive), key_sums(qkt[0:keyed, :] * alive)]
    for out in (o0, o1, o2, o3):
        out[slab + 2 * part :, :] = jnp.concatenate(sums, 0)


def project(half, x, wq, wk, wv, *others):
    _, rows, width = x.shape
    keyed = wq.shape[1]
    total = (width + 2 * keyed) // GROUP // 2 + (2 * FEAT if half else 0)
    outs = [((total, rows), bf16)] * GROUP
    scratch = [
        pltpu.VMEM((rows, width), bf16),
        pltpu.VMEM((width, keyed), bf16),
        pltpu.VMEM((width, width // 2), bf16),
        pltpu.VMEM((width // 2, rows), bf16),
        pltpu.VMEM((keyed, rows), bf16),
        pltpu.SemaphoreType.DMA((3 + len(TILES),)),
    ]
    if not half:
        outs.append(((keyed // 2, rows), bf16))
    flops = rows * width * (width + 2 * keyed)
    kernel = functools.partial(project_kernel, half)
    limit = LIMIT_B if half else LIMIT_A
    args = [x, wq, wk, wv, *others]
    return call(kernel, outs, scratch, limit, flops, flops // rows, args, [pltpu.HBM] * 4)


LIMIT_A = 53.6
LIMIT_B = 16


def own_taps(conv, mine, taps, taps_v):
    full = conv.shape[1]
    padded = jnp.concatenate([conv[...], jnp.zeros((8 - CONV, full), f32)], 0)
    for j in range(full // LANES):
        taps_v[j * LANES : (j + 1) * LANES, :] = padded[:, j * LANES : (j + 1) * LANES].T
    slab = full // 2 // GROUP
    for half in range(2):
        start = pl.multiple_of(full // 2 * half + slab * mine, 32)
        taps[half * slab : (half + 1) * slab, :] = taps_v[pl.ds(start, slab), :]


def state_kernel(half, *refs):
    length, p0, p1, p2, p3 = refs[:5]
    if half:
        taps, aug, qk, state, held = refs[5:]
    else:
        conv, aug, qk, state, taps, held, taps_v = refs[5:]
        own_taps(conv, lax.rem(lax.axis_index("blk"), GROUP), taps, taps_v)
    rows = p0.shape[1]
    place = lax.axis_index("blk")
    mine, group = lax.rem(place, GROUP), place // GROUP
    kept = held.shape[1]
    size = kept // LOCAL - 2 * FEAT
    values = LOCAL * size
    tokens = GROUP * rows
    for s, ref in enumerate((p0, p1, p2, p3)):
        held[mine ^ s] = ref[0:kept, :]
    if half:
        sums = p0[kept:, :].astype(f32) + p1[kept:, :].astype(f32)
        sums += p2[kept:, :].astype(f32) + p3[kept:, :].astype(f32)
        state[LOCAL * SYM :, :] = sums.astype(bf16)
    for b in range(GROUP):
        qk[:, b * rows : (b + 1) * rows] = held[b, values:, :]
    alive = (group * tokens + iota((1, tokens), 1) < length[...]).astype(f32)
    token = iota((FEAT, tokens), 1)
    row = iota((FEAT, tokens), 0)
    marks = (row == 0) | ((row == 1) & (token == 0)) | ((row == 2) & (token == 1))
    marks = jnp.where(marks, alive, 0.0).astype(bf16)
    lane = iota((size, rows), 1)
    last = iota((FEAT, rows), 0)
    ends = iota((FEAT, rows), 1)
    ends = ((last == 9) & (ends == rows - 1)) | ((last == 10) & (ends == rows - 2))
    ends = ends.astype(bf16)
    for h in range(LOCAL):
        cut = slice(h * size, (h + 1) * size)
        first = (half * LOCAL + h) * size
        tap = taps[first : first + size, :]
        tap = [jnp.broadcast_to(tap[:, t : t + 1], (size, rows)) for t in range(CONV)]
        before = [jnp.zeros((size, rows), f32)] * 2
        pieces = []
        for b in range(GROUP):
            now = held[b, cut, :].astype(f32)
            rolled = [pltpu.roll(now, 1, 1), pltpu.roll(now, 2, 1)]
            one = jnp.where(lane < 1, before[0], rolled[0])
            two = jnp.where(lane < 2, before[1], rolled[1])
            before = rolled
            mixed = tap[0] * now + tap[1] * one + tap[2] * two
            live = alive[:, b * rows : (b + 1) * rows]
            pieces.append(jnp.where(live > 0, mixed, 0.0).astype(bf16))
        aug_h = jnp.concatenate([jnp.concatenate(pieces, 1), marks], 0)
        aug[h] = aug_h
        y = qk[h * FEAT : (h + 1) * FEAT, :].astype(f32) * FEAT ** (-0.25)
        own = dot(symmetric(y, 1.0).astype(bf16), aug_h, NT)
        edge = dot(ends, held[GROUP - 1, h * size : h * size + LANES, :], NT)
        state[h * SYM : h * SYM + 144, :] = own[:144].astype(bf16)
        state[h * SYM + 144 : (h + 1) * SYM, :] = (own[144:] + edge).astype(bf16)


def group_state(half, length, payloads, taps, after):
    total, rows = payloads[0].shape
    tokens = GROUP * rows
    extra = 2 * FEAT if half else 0
    outs = [
        ((LOCAL, LANES, tokens), bf16),
        ((2 * LOCAL * FEAT, tokens), bf16),
        ((LOCAL * SYM + extra, LANES), bf16),
    ]
    scratch = [pltpu.VMEM((GROUP, total - extra, rows), bf16)]
    if not half:
        width = taps.shape[1]
        outs.append(((width // GROUP, 8), f32))
        scratch.append(pltpu.VMEM((width, 8), f32))
    kernel = functools.partial(state_kernel, half)
    args = [length, *payloads, taps]
    return call(kernel, outs, scratch, 32, 100_000_000, 1_000_000, args, after=after)


def local_kernel(aug, qk, num):
    _, _, tokens = aug.shape
    keyed = LOCAL * FEAT
    half = tokens // 2
    keys = qk[0:keyed, :].astype(f32).T.astype(bf16)
    queries = qk[keyed:, :]
    head = iota((keyed, tokens), 0) // FEAT
    causal = iota((half, half), 0) <= iota((half, half), 1)

    def scores(d):
        return 1.0 + d * (0.25 + d * 0.03125)

    for h in range(LOCAL):
        only = jnp.where(head == h, queries, jnp.zeros_like(queries))
        first = scores(dot(keys[:half], only[:, :half]))
        first = jnp.where(causal, first, 0.0).astype(bf16)
        num[h, :, 0:half] = dot(aug[h, :, 0:half], first)
        lower = scores(dot(keys[half:], only[:, half:]))
        lower = jnp.where(causal, lower, 0.0).astype(bf16)
        upper = scores(dot(keys[:half], only[:, half:])).astype(bf16)
        num[h, :, half:] = dot(aug[h, :, 0:half], upper) + dot(aug[h, :, half:], lower)


def local_part(aug, qk, flops, after):
    _, _, tokens = aug.shape
    return call(local_kernel, [(aug.shape, f32)], [], 32, flops, 1000, [aug, qk], after=after)[0]


def finish_kernel(half, *refs):
    length, slot, num, own, got, qk, taps = refs[:7]
    refs = refs[7:]
    if half:
        other, *firsts = refs[:5]
        refs = refs[5:]
    r0, r1, r2, r3, route, scr = refs
    _, _, tokens = num.shape
    rows = tokens // GROUP
    size = taps.shape[0] // 2 // LOCAL
    keyed = LOCAL * FEAT
    place = lax.axis_index("blk")
    mine, group = lax.rem(place, GROUP), place // GROUP
    upper = group == 1
    weight = jnp.where(upper, 1.0, 0.0)
    alive = group * tokens + iota((1, tokens), 1) < length[...]
    first = (iota((size, LANES), 1) == 0) & upper
    aux = iota((LANES - size, SYM), 0)
    finals = []
    for h in range(LOCAL):
        here = own[h * SYM : (h + 1) * SYM, :].astype(f32).T
        there = got[h * SYM : (h + 1) * SYM, :].astype(f32).T
        low = jnp.where(upper, there, here)
        high = jnp.where(upper, here, there)
        at = (half * LOCAL + h) * size
        tap = taps[at : at + size, :]
        last, second = low[:size, 153:154], low[:size, 154:155]
        change0 = tap[:, 1:2] * last + tap[:, 2:3] * second
        change1 = tap[:, 2:3] * last
        key0, key1 = high[size + 1 : size + 2, :], high[size + 2 : size + 3, :]
        body = low[:size] + change0 * key0 + change1 * key1
        tail = jnp.where(aux == 2, key1, low[size:])
        prior = jnp.concatenate([body, tail], 0)
        finals.append(jnp.concatenate([body + high[:size], low[size:] + high[size:]], 0))
        y = qk[keyed + h * FEAT : keyed + (h + 1) * FEAT, :].astype(f32) * FEAT ** (-0.25)
        feats = symmetric(y, 0.5).astype(bf16)
        all_num = num[h] + weight * dot(prior.astype(bf16), feats)
        den = jnp.where(alive, all_num[size : size + 1, :], 1.0)
        inverse = jnp.where(alive, 1.0 / den, 0.0)
        top = all_num[:size]
        extra = all_num[size + 2 : size + 3, 0:1]
        edge = top[:, :LANES] - jnp.where(first, change1 * extra, 0.0)
        top = jnp.concatenate([edge, top[:, LANES:]], 1)
        result = (top * inverse).astype(bf16)
        for b in range(GROUP):
            scr[b, h * size : (h + 1) * size, :] = result[:, b * rows : (b + 1) * rows]
    for s, out in enumerate((r0, r1, r2, r3)):
        if half:
            out[0 : LOCAL * size, :] = firsts[s][...]
        out[half * LOCAL * size :, :] = scr[mine ^ s]
    if not half:
        for c in range(LOCAL):
            route[c * SYM : (c + 1) * SYM, :] = finals[c].T.astype(bf16)
        return
    count = length[...]
    for c in range(LOCAL):
        final = jnp.where(upper, finals[c].T, other[c * SYM : (c + 1) * SYM, :].astype(f32))
        if c == 0:
            row, lane = iota(final.shape, 0), iota(final.shape, 1)
            info = (slot[...], lax.shift_right_logical(count, 8), count & 255)
            for at, value in enumerate(info):
                final = jnp.where((row == INFO) & (lane == at), value.astype(f32), final)
        route[c * SYM : (c + 1) * SYM, :] = final.astype(bf16)
    sums = own[LOCAL * SYM :, :].astype(f32) + got[LOCAL * SYM :, :].astype(f32)
    route[LOCAL * SYM :, :] = sums.astype(bf16)


def finish(half, length, slot, num, own, got, qk, taps, other):
    _, _, tokens = num.shape
    rows = tokens // GROUP
    width = taps.shape[0] // 2
    outs = [(((1 + half) * width, rows), bf16)] * GROUP + [(own.shape, bf16)]
    scratch = [pltpu.VMEM((GROUP, width, rows), bf16)]
    args = [length, slot, num, own, got, qk, taps] + other
    kernel = functools.partial(finish_kernel, half)
    return call(kernel, outs, scratch, 32, 50_000_000, 20_000_000, args)


def place_kernel(r0, r1, r2, r3, mixed, scr):
    width = scr.shape[0]
    mine = lax.rem(lax.axis_index("blk"), GROUP)
    half = width // 2
    slab = half // GROUP
    for s, ref in enumerate((r0, r1, r2, r3)):
        start = pl.multiple_of(slab * (mine ^ s), 32)
        scr[pl.ds(start, slab), :] = ref[0:slab, :]
        scr[pl.ds(pl.multiple_of(half + start, 32), slab), :] = ref[slab:, :]
    for j in range(width // LANES):
        cut = slice(j * LANES, (j + 1) * LANES)
        mixed[0, :, cut] = scr[cut, :].astype(f32).T.astype(bf16)


def place_tokens(results, after):
    part, rows = results[0].shape
    width = part * GROUP
    outs = [((1, rows, width), bf16)]
    scratch = [pltpu.VMEM((width, rows), bf16)]
    return call(place_kernel, outs, scratch, 32, 1000, 1_000_000, results, after=after)[0]


def hand_on_kernel(own, got, out):
    other = (lax.axis_index("req") ^ 1).astype(f32)
    kept = jnp.zeros(out.shape, f32)
    for ref in (own, got):
        here = ref[INFO : INFO + 1, 0:1].astype(f32) == other
        kept += jnp.where(here, ref[...].astype(f32), 0.0)
    out[...] = kept.astype(bf16)


def hand_on(own, got, after):
    args = [own, got]
    return call(hand_on_kernel, [(own.shape, bf16)], [], 32, 1000, 300_000, args, after=after)[0]


def expand_kernel(c0, c1, c2, spread, state, norm):
    me = lax.axis_index("req").astype(f32)
    kept = jnp.zeros(c0.shape, f32)
    for ref in (c0, c1, c2):
        here = ref[INFO : INFO + 1, 0:1].astype(f32) == me
        kept += jnp.where(here, ref[...].astype(f32), 0.0)
    size = state.shape[2] // LOCAL
    expand = state.shape[0]
    scale = jnp.where(iota((expand, LANES), 0) > FEAT, math.sqrt(0.5), 1.0)
    wholes = []
    for c in range(LOCAL):
        whole = dot(spread[...], kept[c * SYM : (c + 1) * SYM].astype(bf16)) * scale
        wholes.append(whole[:, :size])
    state[...] = jnp.concatenate(wholes, 1).reshape(state.shape)
    sums = kept[LOCAL * SYM :]
    keyed = HEADS * FEAT
    sums = jnp.concatenate([sums[:FEAT], sums[FEAT:]], 1)
    plain = jnp.concatenate([sums[9:], sums[:9]], 0) * FEAT ** (-0.25)
    products = sums * FEAT ** (-0.5)
    b = iota((FEAT, keyed), 0)
    entry = lax.rem(iota((FEAT, keyed), 1), FEAT)
    big = [jnp.where(entry == b, plain, 0.0)]
    for a in range(FEAT):
        mirror = b == (a + 9) % FEAT
        row = jnp.where(mirror, products[a : a + 1], products)
        big.append(jnp.where(entry == jnp.where(mirror, b, a), row, 0.0))
    big = jnp.concatenate(big, 0)
    gather = (iota((keyed, HEADS), 0) // FEAT == iota((keyed, HEADS), 1)).astype(bf16)
    rest = dot(big.astype(bf16), gather)
    rest = rest * jnp.where(iota(rest.shape, 0) >= FEAT, math.sqrt(0.5), 1.0)
    info = kept[INFO : INFO + 1]
    count = info[:, 1:2] * 256.0 + info[:, 2:3]
    norm[0] = jnp.concatenate([jnp.broadcast_to(count, (1, HEADS)), rest], 0).T


def spread_rows():
    table = np.zeros((1 + FEAT + FEAT * FEAT, SYM), np.float32)
    table[0, 152] = 1
    for a in range(FEAT):
        table[1 + a, 128 + a] = 1
        for b in range(FEAT):
            o = (b - a) % FEAT
            at = o * FEAT + a if o < 8 else (144 + min(a, b) if o == 8 else (FEAT - o) * FEAT + b)
            table[1 + FEAT + a * FEAT + b, at] = 1
    return table


def expand_state(candidates, columns):
    spread = jnp.asarray(spread_rows(), bf16)
    expand = spread.shape[0]
    outs = [((expand, 1, columns), f32), ((1, HEADS, expand), f32)]
    return call(expand_kernel, outs, [], 32, 40_000_000, 1_000_000, [*candidates, spread])


def swap(array, axis, by):
    return lax.ppermute(array, axis, [(i, i ^ by) for i in range(lax.axis_size(axis))])


def two_groups(
    tokens_in, query_weight, key_weight, value_weight, conv_weight, prompt_lengths, decode_map
):
    width = tokens_in.shape[2]
    length, slot = prompt_lengths.reshape(1, 1), decode_map.reshape(1, 1)
    given = (tokens_in, query_weight, key_weight, value_weight)
    *parts, early = project(0, *given)
    sent = [[parts[0]] + [swap(parts[s], "blk", s) for s in (1, 2, 3)]]
    parts = project(1, *given, length, early)
    sent.append([parts[0]] + [swap(parts[s], "blk", s) for s in (1, 2, 3)])
    *first, taps = group_state(0, length, sent[0], conv_weight, [])
    second = group_state(1, length, sent[1], taps, [first[2]])
    got = [swap(held[2], "blk", GROUP) for held in (first, second)]
    aug, qk, own = first
    num = local_part(aug, qk, 1000, [second[2]])
    early = finish(0, length, slot, num, own, got[0], qk, taps, [])
    aug, qk, own = second
    num = local_part(aug, qk, 5_000_000_000, [early[4]])
    *parts, total = finish(1, length, slot, num, own, got[1], qk, taps, [early[4], *early[:4]])
    results = [parts[0]] + [swap(parts[s], "blk", s) for s in (1, 2, 3)]
    beside = swap(total, "req", 2)
    theirs = swap(hand_on(total, beside, results[1:2]), "req", 1)
    state, norm = expand_state([total, beside, theirs], width // lax.axis_size("blk"))
    mixed = place_tokens(results, [theirs])
    return (mixed, jnp.swapaxes(state, 0, 1), jnp.swapaxes(norm, 1, 2))


def from_behind(array, axis, by):
    devices = lax.axis_size(axis)
    pairs = [(i, i + by) for i in range(devices) if 0 <= i + by < devices]
    return lax.ppermute(array, axis, pairs)


def entering(part, axis, combine, identity):
    place = lax.axis_index(axis)
    gathered = jax.tree.map(lambda a: lax.all_gather(a, axis), part)
    state = jax.tree.map(lambda a, e: jnp.zeros_like(a) + jnp.asarray(e, a.dtype), part, identity)

    def one(turn, state):
        return combine(
            state, jax.tree.map(lambda a: lax.dynamic_index_in_dim(a, turn, 0, False), gathered)
        )

    return lax.fori_loop(0, place, one, state)


def features_last(x):
    half = x * FEAT ** (-0.25)
    outer = half[:, :, None, :] * half[:, None, :, :]
    flat = outer.reshape(half.shape[0], FEAT * FEAT, half.shape[2]) * math.sqrt(0.5)
    ones = jnp.ones((half.shape[0], 1, half.shape[2]), jnp.float32)
    return jnp.concatenate([ones, half, flat], 1)


def add_pair(earlier, later):
    return (earlier[0] + later[0], earlier[1] + later[1])


def route_slot(pair, decode_map):
    groups = lax.axis_size("req")
    slots = (jnp.arange(groups, dtype=jnp.int32) == decode_map[0]).astype(jnp.float32)
    sent = (slots[:, None, None] * pair[0][None], slots[:, None, None] * pair[1][None])
    got = (
        lax.all_to_all(sent[0], "req", split_axis=0, concat_axis=0, tiled=True),
        lax.all_to_all(sent[1], "req", split_axis=0, concat_axis=0, tiled=True),
    )
    return (jnp.sum(got[0], 0), jnp.sum(got[1], 0))


def reduce_blocks(pair):
    return (
        lax.psum_scatter(pair[0], "blk", scatter_dimension=1, tiled=True),
        lax.psum_scatter(pair[1], "blk", scatter_dimension=1, tiled=True),
    )


def any_blocks(
    tokens_in, query_weight, key_weight, value_weight, conv_weight, prompt_lengths, decode_map
):
    rows = tokens_in.shape[1]
    width = tokens_in.shape[2]
    blocks = lax.axis_size("blk")
    head_size = width // HEADS
    hi = lax.Precision.HIGHEST
    inputs = tokens_in[0]
    queries = jnp.einsum(
        "dk,td->kt", query_weight, inputs, preferred_element_type=jnp.float32
    ).reshape(HEADS, FEAT, rows)
    keys = jnp.einsum("dk,td->kt", key_weight, inputs, preferred_element_type=jnp.float32).reshape(
        HEADS, FEAT, rows
    )
    values = jnp.dot(inputs, value_weight, preferred_element_type=jnp.float32).astype(jnp.bfloat16)
    earlier = from_behind(values[rows - (CONV - 1) :], "blk", 1)
    extended = jnp.concatenate([earlier, values], 0).astype(jnp.float32)
    conv = jnp.zeros((rows, width), jnp.float32)
    for tap in range(CONV):
        conv = conv + conv_weight[tap][None, :] * extended[CONV - 1 - tap : CONV - 1 - tap + rows]
    conv_t = conv.astype(jnp.bfloat16).astype(jnp.float32).T.reshape(HEADS, head_size, rows)
    start = lax.axis_index("blk") * rows
    live = (start + jnp.arange(rows, dtype=jnp.int32) < prompt_lengths[0]).astype(jnp.float32)
    feat_q = features_last(queries)
    feat_k = features_last(keys) * live[None, None, :]
    own_state = jnp.einsum("hft,hct->hfc", feat_k, conv_t, precision=hi)
    own_norm = jnp.sum(feat_k, 2)
    zero_state = jnp.zeros_like(own_state)
    zero_norm = jnp.zeros_like(own_norm)
    prior_state, prior_norm = entering(
        (own_state, own_norm), "blk", add_pair, (zero_state, zero_norm)
    )
    causal = (jnp.arange(rows)[:, None] >= jnp.arange(rows)[None, :]).astype(jnp.float32)
    scores = jnp.einsum("hft,hfs->hts", feat_q, feat_k, precision=hi) * causal[None]
    num = jnp.einsum("hts,hcs->hct", scores, conv_t, precision=hi) + jnp.einsum(
        "hft,hfc->hct", feat_q, prior_state, precision=hi
    )
    den = (
        jnp.sum(scores, -1)
        + jnp.einsum("hft,hf->ht", feat_q, prior_norm, precision=hi)
        + (1.0 - live)[None, :]
    )
    result = jnp.where(live[None, None, :] > 0, num / den[:, None, :], 0.0)
    mixed = result.reshape(width, rows).T.reshape(1, rows, width).astype(jnp.bfloat16)
    state_flat = jnp.transpose(own_state, (1, 0, 2)).reshape(own_state.shape[1], width)
    pair = (state_flat, jnp.tile(own_norm.T, (1, blocks)))
    final = route_slot(reduce_blocks(pair), decode_map)
    return (mixed, final[0][None], final[1][None])


def solution(mesh):
    def on_device(*args):
        rows = args[0].shape[1]
        if mesh.shape["blk"] == 2 * GROUP and mesh.shape["req"] == 4 and rows == LANES:
            return two_groups(*args)
        return any_blocks(*args)

    return jax.shard_map(
        on_device,
        mesh=mesh,
        in_specs=(P("req", "blk", None), P(), P(), P(), P(), P("req"), P("req")),
        out_specs=(P("req", "blk", None), P("req", None, "blk"), P("req", None, None)),
        check_vma=False,
    )
```

```python
import functools
import math

import jax
import jax.numpy as jnp
import numpy as np
from jax import lax
from jax.experimental import pallas as pl
from jax.experimental.pallas import tpu as pltpu
from jax.sharding import PartitionSpec as P

HEADS = 16
FEAT = 16
CONV = 3

GROUP = 4
SYM = 160
LANES = 128
INFO = 159
LOCAL = HEADS // GROUP // 2
ORDER = (0, 3, 2, 1)
f32 = jnp.float32
bf16 = jnp.bfloat16
NT = (((1,), (1,)), ((), ()))
NN = (((1,), (0,)), ((), ()))


def dot(a, b, dims=NN):
    return lax.dot_general(a, b, dims, preferred_element_type=f32)


def iota(shape, axis):
    return lax.broadcasted_iota(jnp.int32, shape, axis)


def symmetric(y, scale_square):
    twice = jnp.concatenate([y, y], 0)
    rows = [y * y * scale_square] + [y * twice[o : o + FEAT] for o in range(1, 8)]
    rest = jnp.where(iota((8, y.shape[1]), 0) == 0, 1.0, 0.0)
    return jnp.concatenate(rows + [y, y[:8] * y[8:], rest], 0)


def call(kernel, outs, scratch, limit, flops, moved, args, spaces=(), after=()):
    vmem = pl.BlockSpec(memory_space=pltpu.VMEM)
    given = [pl.BlockSpec(memory_space=space) for space in spaces]
    if after:
        body, plain = kernel, len(args)

        def kernel(*refs):
            body(*refs[:plain], *refs[plain + len(after) :])

    return pl.pallas_call(
        kernel,
        out_shape=[jax.ShapeDtypeStruct(shape, dtype) for shape, dtype in outs],
        in_specs=given
        + [vmem] * (len(args) - len(given))
        + [pl.BlockSpec(memory_space=pl.ANY)] * len(after),
        out_specs=[vmem] * len(outs),
        scratch_shapes=scratch,
        compiler_params=pltpu.CompilerParams(vmem_limit_bytes=int(limit * 2**20)),
        cost_estimate=pl.CostEstimate(flops=flops, bytes_accessed=moved, transcendentals=0),
    )(*args, *after)


TILES = (384, 512)


def key_sums(keys):
    keyed, rows = keys.shape
    gram = dot(keys, keys, NT)
    same = iota((keyed, keyed), 0) // FEAT == iota((keyed, keyed), 1) // FEAT
    entry, lane = iota((FEAT, keyed), 0), iota((FEAT, keyed), 1)
    pick = (lax.rem(lane, FEAT) == entry).astype(bf16)
    folded = dot(pick, jnp.where(same, gram, 0.0).astype(bf16))
    plain = dot(jnp.ones((8, rows), bf16), keys, NT)
    mirror = lax.rem(entry - lax.rem(lane, FEAT) + FEAT, FEAT) == 9
    return jnp.where(mirror, plain[0:1], folded).astype(bf16)


def project_kernel(half, *refs):
    x, wq, wk, wv = refs[:4]
    refs = refs[4:]
    if half:
        length, early, o0, o1, o2, o3 = refs[:6]
        refs = refs[6:]
    else:
        o0, o1, o2, o3, early = refs[:5]
        refs = refs[5:]
    x_v, wqk_v, wv_v, vt, qkt, sems = refs[:6]
    rows = x.shape[1]
    width = wv.shape[1] // 2
    keyed = wq.shape[1] // 2
    get_x = pltpu.make_async_copy(x.at[0], x_v, sems.at[0])
    keyed_cut = pl.ds(half * keyed, keyed)
    get_k = pltpu.make_async_copy(wk.at[:, keyed_cut], wqk_v.at[:, pl.ds(0, keyed)], sems.at[1])
    get_q = pltpu.make_async_copy(wq.at[:, keyed_cut], wqk_v.at[:, pl.ds(keyed, keyed)], sems.at[2])
    copies, at = [], 0
    for j, tile in enumerate(TILES):
        source = wv.at[:, pl.ds(half * width + at, tile)]
        copies.append(pltpu.make_async_copy(source, wv_v.at[:, pl.ds(at, tile)], sems.at[3 + j]))
        at += tile
    for copy in (get_x, get_k, get_q, *copies):
        copy.start()
    place = lax.axis_index("blk")
    mine = lax.rem(place, GROUP)
    slab = width // GROUP
    get_x.wait()
    get_k.wait()
    get_q.wait()
    inputs = x_v[...]
    qkt[...] = dot(inputs, wqk_v[...]).T.astype(bf16)
    at = 0
    for tile, copy in zip(TILES, copies):
        copy.wait()
        vt[at : at + tile, :] = dot(inputs, wv_v[:, at : at + tile]).T.astype(bf16)
        at += tile
    part = keyed // GROUP
    for s, out in zip(ORDER, (o0, o1, o2, o3)):
        dest = mine ^ s
        out[0:slab, :] = vt[pl.ds(pl.multiple_of(slab * dest, 32), slab), :]
        for base, at in ((0, slab), (keyed, slab + part)):
            start = pl.multiple_of(base + part * dest, 32)
            out[at : at + part, :] = qkt[pl.ds(start, part), :]
    if not half:
        early[...] = qkt[0:keyed, :]
        return
    alive = place * rows + iota((1, rows), 1) < length[...]
    alive = jnp.where(alive, 1.0, 0.0).astype(bf16)
    sums = [key_sums(early[...] * alive), key_sums(qkt[0:keyed, :] * alive)]
    for out in (o0, o1, o2, o3):
        out[slab + 2 * part :, :] = jnp.concatenate(sums, 0)


def project(half, x, wq, wk, wv, *others):
    _, rows, width = x.shape
    keyed = wq.shape[1]
    total = (width + 2 * keyed) // GROUP // 2 + (2 * FEAT if half else 0)
    outs = [((total, rows), bf16)] * GROUP
    scratch = [
        pltpu.VMEM((rows, width), bf16),
        pltpu.VMEM((width, keyed), bf16),
        pltpu.VMEM((width, width // 2), bf16),
        pltpu.VMEM((width // 2, rows), bf16),
        pltpu.VMEM((keyed, rows), bf16),
        pltpu.SemaphoreType.DMA((3 + len(TILES),)),
    ]
    if not half:
        outs.append(((keyed // 2, rows), bf16))
    flops = rows * width * (width + 2 * keyed)
    kernel = functools.partial(project_kernel, half)
    limit = LIMIT_B if half else LIMIT_A
    args = [x, wq, wk, wv, *others]
    return call(kernel, outs, scratch, limit, flops, flops // rows, args, [pltpu.HBM] * 4)


LIMIT_A = 53.6
LIMIT_B = 16


def own_taps(conv, mine, taps, taps_v):
    half = conv.shape[1] // 2
    slab = half // GROUP
    wide = taps_v.shape[0]
    start = jnp.minimum(slab * mine // LANES * LANES, half - wide)
    inside = pl.multiple_of(slab * mine - start, 32)
    for h in range(2):
        cut = conv[:, pl.ds(pl.multiple_of(half * h + start, LANES), wide)]
        padded = jnp.concatenate([cut, jnp.zeros((8 - CONV, wide), f32)], 0)
        for j in range(wide // LANES):
            rows = slice(j * LANES, (j + 1) * LANES)
            taps_v[rows, :] = padded[:, rows].T
        taps[h * slab : (h + 1) * slab, :] = taps_v[pl.ds(inside, slab), :]


def state_kernel(half, *refs):
    length, p0, p1, p2, p3 = refs[:5]
    if half:
        taps, aug, qk, state, held = refs[5:]
    else:
        conv, aug, qk, state, taps, held, taps_v = refs[5:]
        own_taps(conv, lax.rem(lax.axis_index("blk"), GROUP), taps, taps_v)
    rows = p0.shape[1]
    place = lax.axis_index("blk")
    mine, group = lax.rem(place, GROUP), place // GROUP
    kept = held.shape[1]
    size = kept // LOCAL - 2 * FEAT
    values = LOCAL * size
    tokens = GROUP * rows
    for s, ref in zip(ORDER, (p0, p1, p2, p3)):
        held[mine ^ s] = ref[0:kept, :]
    if half:
        sums = p0[kept:, :].astype(f32) + p1[kept:, :].astype(f32)
        sums += p2[kept:, :].astype(f32) + p3[kept:, :].astype(f32)
        state[LOCAL * SYM :, :] = sums.astype(bf16)
    for b in range(GROUP):
        qk[:, b * rows : (b + 1) * rows] = held[b, values:, :]
    alive = (group * tokens + iota((1, tokens), 1) < length[...]).astype(f32)
    token = iota((FEAT, tokens), 1)
    row = iota((FEAT, tokens), 0)
    marks = (row == 0) | ((row == 1) & (token == 0)) | ((row == 2) & (token == 1))
    marks = jnp.where(marks, alive, 0.0).astype(bf16)
    lane = iota((size, rows), 1)
    last = iota((FEAT, rows), 0)
    ends = iota((FEAT, rows), 1)
    ends = ((last == 9) & (ends == rows - 1)) | ((last == 10) & (ends == rows - 2))
    ends = ends.astype(bf16)
    for h in range(LOCAL):
        cut = slice(h * size, (h + 1) * size)
        first = (half * LOCAL + h) * size
        tap = taps[first : first + size, :]
        tap = [jnp.broadcast_to(tap[:, t : t + 1], (size, rows)) for t in range(CONV)]
        before = [jnp.zeros((size, rows), f32)] * 2
        pieces = []
        for b in range(GROUP):
            now = held[b, cut, :].astype(f32)
            rolled = [pltpu.roll(now, 1, 1), pltpu.roll(now, 2, 1)]
            one = jnp.where(lane < 1, before[0], rolled[0])
            two = jnp.where(lane < 2, before[1], rolled[1])
            before = rolled
            mixed = tap[0] * now + tap[1] * one + tap[2] * two
            live = alive[:, b * rows : (b + 1) * rows]
            pieces.append(jnp.where(live > 0, mixed, 0.0).astype(bf16))
        aug_h = jnp.concatenate([jnp.concatenate(pieces, 1), marks], 0)
        aug[h] = aug_h
        y = qk[h * FEAT : (h + 1) * FEAT, :].astype(f32) * FEAT ** (-0.25)
        own = dot(symmetric(y, 1.0).astype(bf16), aug_h, NT)
        edge = dot(ends, held[GROUP - 1, h * size : h * size + LANES, :], NT)
        state[h * SYM : h * SYM + 144, :] = own[:144].astype(bf16)
        state[h * SYM + 144 : (h + 1) * SYM, :] = (own[144:] + edge).astype(bf16)


def group_state(half, length, payloads, taps, after):
    total, rows = payloads[0].shape
    tokens = GROUP * rows
    extra = 2 * FEAT if half else 0
    outs = [
        ((LOCAL, LANES, tokens), bf16),
        ((2 * LOCAL * FEAT, tokens), bf16),
        ((LOCAL * SYM + extra, LANES), bf16),
    ]
    scratch = [pltpu.VMEM((GROUP, total - extra, rows), bf16)]
    if not half:
        slab = taps.shape[1] // GROUP
        outs.append(((slab, 8), f32))
        scratch.append(pltpu.VMEM(((slab // 2 // LANES + 2) * LANES, 8), f32))
    kernel = functools.partial(state_kernel, half)
    args = [length, *payloads, taps]
    return call(kernel, outs, scratch, 32, 100_000_000, 1_000_000, args, after=after)


def local_kernel(aug, qk, num):
    _, _, tokens = aug.shape
    keyed = LOCAL * FEAT
    half = tokens // 2
    keys = qk[0:keyed, :].astype(f32).T.astype(bf16)
    queries = qk[keyed:, :]
    head = iota((keyed, tokens), 0) // FEAT
    causal = iota((half, half), 0) <= iota((half, half), 1)

    def scores(d):
        return 1.0 + d * (0.25 + d * 0.03125)

    for h in range(LOCAL):
        only = jnp.where(head == h, queries, jnp.zeros_like(queries))
        first = scores(dot(keys[:half], only[:, :half]))
        first = jnp.where(causal, first, 0.0).astype(bf16)
        num[h, :, 0:half] = dot(aug[h, :, 0:half], first)
        lower = scores(dot(keys[half:], only[:, half:]))
        lower = jnp.where(causal, lower, 0.0).astype(bf16)
        upper = scores(dot(keys[:half], only[:, half:])).astype(bf16)
        num[h, :, half:] = dot(aug[h, :, 0:half], upper) + dot(aug[h, :, half:], lower)


def local_part(aug, qk, flops, after):
    _, _, tokens = aug.shape
    return call(local_kernel, [(aug.shape, f32)], [], 32, flops, 1000, [aug, qk], after=after)[0]


def finish_kernel(half, *refs):
    length, slot, num, own, got, qk, taps = refs[:7]
    refs = refs[7:]
    if half:
        other, *firsts = refs[:5]
        refs = refs[5:]
    r0, r1, r2, r3, route, scr = refs
    _, _, tokens = num.shape
    rows = tokens // GROUP
    size = taps.shape[0] // 2 // LOCAL
    keyed = LOCAL * FEAT
    place = lax.axis_index("blk")
    mine, group = lax.rem(place, GROUP), place // GROUP
    upper = group == 1
    weight = jnp.where(upper, 1.0, 0.0)
    alive = group * tokens + iota((1, tokens), 1) < length[...]
    first = (iota((size, LANES), 1) == 0) & upper
    aux = iota((LANES - size, SYM), 0)
    finals = []
    for h in range(LOCAL):
        here = own[h * SYM : (h + 1) * SYM, :].astype(f32).T
        there = got[h * SYM : (h + 1) * SYM, :].astype(f32).T
        low = jnp.where(upper, there, here)
        high = jnp.where(upper, here, there)
        at = (half * LOCAL + h) * size
        tap = taps[at : at + size, :]
        last, second = low[:size, 153:154], low[:size, 154:155]
        change0 = tap[:, 1:2] * last + tap[:, 2:3] * second
        change1 = tap[:, 2:3] * last
        key0, key1 = high[size + 1 : size + 2, :], high[size + 2 : size + 3, :]
        body = low[:size] + change0 * key0 + change1 * key1
        tail = jnp.where(aux == 2, key1, low[size:])
        prior = jnp.concatenate([body, tail], 0)
        finals.append(jnp.concatenate([body + high[:size], low[size:] + high[size:]], 0))
        y = qk[keyed + h * FEAT : keyed + (h + 1) * FEAT, :].astype(f32) * FEAT ** (-0.25)
        feats = symmetric(y, 0.5).astype(bf16)
        all_num = num[h] + weight * dot(prior.astype(bf16), feats)
        den = jnp.where(alive, all_num[size : size + 1, :], 1.0)
        inverse = jnp.where(alive, 1.0 / den, 0.0)
        top = all_num[:size]
        extra = all_num[size + 2 : size + 3, 0:1]
        edge = top[:, :LANES] - jnp.where(first, change1 * extra, 0.0)
        top = jnp.concatenate([edge, top[:, LANES:]], 1)
        result = (top * inverse).astype(bf16)
        for b in range(GROUP):
            scr[b, h * size : (h + 1) * size, :] = result[:, b * rows : (b + 1) * rows]
    for j, (s, out) in enumerate(zip(ORDER, (r0, r1, r2, r3))):
        if half:
            out[0 : LOCAL * size, :] = firsts[j][...]
        out[half * LOCAL * size :, :] = scr[mine ^ s]
    if not half:
        for c in range(LOCAL):
            route[c * SYM : (c + 1) * SYM, :] = finals[c].T.astype(bf16)
        return
    count = length[...]
    for c in range(LOCAL):
        final = jnp.where(upper, finals[c].T, other[c * SYM : (c + 1) * SYM, :].astype(f32))
        if c == 0:
            row, lane = iota(final.shape, 0), iota(final.shape, 1)
            values = (slot[...], lax.shift_right_logical(count, 8), count & 255)
            for at, value in enumerate(values):
                final = jnp.where((row == INFO) & (lane == at), value.astype(f32), final)
        route[c * SYM : (c + 1) * SYM, :] = final.astype(bf16)
    sums = own[LOCAL * SYM :, :].astype(f32) + got[LOCAL * SYM :, :].astype(f32)
    route[LOCAL * SYM :, :] = sums.astype(bf16)


def finish(half, length, slot, num, own, got, qk, taps, other):
    _, _, tokens = num.shape
    rows = tokens // GROUP
    width = taps.shape[0] // 2
    outs = [(((1 + half) * width, rows), bf16)] * GROUP + [(own.shape, bf16)]
    scratch = [pltpu.VMEM((GROUP, width, rows), bf16)]
    args = [length, slot, num, own, got, qk, taps] + other
    kernel = functools.partial(finish_kernel, half)
    return call(kernel, outs, scratch, 32, 50_000_000, 20_000_000, args)


def place_kernel(r0, r1, r2, r3, mixed, scr):
    width = scr.shape[0]
    mine = lax.rem(lax.axis_index("blk"), GROUP)
    half = width // 2
    slab = half // GROUP
    for s, ref in zip(ORDER, (r0, r1, r2, r3)):
        start = pl.multiple_of(slab * (mine ^ s), 32)
        scr[pl.ds(start, slab), :] = ref[0:slab, :]
        scr[pl.ds(pl.multiple_of(half + start, 32), slab), :] = ref[slab:, :]
    for j in range(width // LANES):
        cut = slice(j * LANES, (j + 1) * LANES)
        mixed[0, :, cut] = scr[cut, :].T


def place_tokens(results, after):
    part, rows = results[0].shape
    width = part * GROUP
    outs = [((1, rows, width), bf16)]
    scratch = [pltpu.VMEM((width, rows), bf16)]
    return call(place_kernel, outs, scratch, 32, 1000, 1_000_000, results, after=after)[0]


ROUTE = (2, 1)


def hand_on_kernel(own, got, out):
    other = (lax.axis_index("req") ^ ROUTE[1]).astype(f32)
    kept = jnp.zeros(out.shape, f32)
    for ref in (own, got):
        here = ref[INFO : INFO + 1, 0:1].astype(f32) == other
        kept += jnp.where(here, ref[...].astype(f32), 0.0)
    out[...] = kept.astype(bf16)


def hand_on(own, got, after):
    args = [own, got]
    return call(hand_on_kernel, [(own.shape, bf16)], [], 32, 1000, 300_000, args, after=after)[0]


def expand_kernel(c0, c1, c2, spread, state, norm):
    me = lax.axis_index("req").astype(f32)
    kept = jnp.zeros(c0.shape, f32)
    for ref in (c0, c1, c2):
        here = ref[INFO : INFO + 1, 0:1].astype(f32) == me
        kept += jnp.where(here, ref[...].astype(f32), 0.0)
    size = state.shape[2] // LOCAL
    expand = state.shape[0]
    scale = jnp.where(iota((expand, LANES), 0) > FEAT, math.sqrt(0.5), 1.0)
    wholes = []
    for c in range(LOCAL):
        whole = dot(spread[...], kept[c * SYM : (c + 1) * SYM].astype(bf16)) * scale
        wholes.append(whole[:, :size])
    state[...] = jnp.concatenate(wholes, 1).reshape(state.shape)
    sums = kept[LOCAL * SYM :]
    keyed = HEADS * FEAT
    sums = jnp.concatenate([sums[:FEAT], sums[FEAT:]], 1)
    plain = jnp.concatenate([sums[9:], sums[:9]], 0) * FEAT ** (-0.25)
    products = sums * FEAT ** (-0.5)
    b = iota((FEAT, keyed), 0)
    entry = lax.rem(iota((FEAT, keyed), 1), FEAT)
    big = [jnp.where(entry == b, plain, 0.0)]
    for a in range(FEAT):
        mirror = b == (a + 9) % FEAT
        row = jnp.where(mirror, products[a : a + 1], products)
        big.append(jnp.where(entry == jnp.where(mirror, b, a), row, 0.0))
    big = jnp.concatenate(big, 0)
    gather = (iota((keyed, HEADS), 0) // FEAT == iota((keyed, HEADS), 1)).astype(bf16)
    rest = dot(big.astype(bf16), gather)
    rest = rest * jnp.where(iota(rest.shape, 0) >= FEAT, math.sqrt(0.5), 1.0)
    info = kept[INFO : INFO + 1]
    count = info[:, 1:2] * 256.0 + info[:, 2:3]
    norm[0] = jnp.concatenate([jnp.broadcast_to(count, (1, HEADS)), rest], 0).T


def spread_rows():
    table = np.zeros((1 + FEAT + FEAT * FEAT, SYM), np.float32)
    table[0, 152] = 1
    for a in range(FEAT):
        table[1 + a, 128 + a] = 1
        for b in range(FEAT):
            o = (b - a) % FEAT
            at = o * FEAT + a if o < 8 else (144 + min(a, b) if o == 8 else (FEAT - o) * FEAT + b)
            table[1 + FEAT + a * FEAT + b, at] = 1
    return table


def expand_state(candidates, columns):
    spread = jnp.asarray(spread_rows(), bf16)
    expand = spread.shape[0]
    outs = [((expand, 1, columns), f32), ((1, HEADS, expand), f32)]
    return call(expand_kernel, outs, [], 32, 40_000_000, 1_000_000, [*candidates, spread])


def across(arrays):
    return [swap(array, "blk", s) if s else array for s, array in zip(ORDER, arrays)]


def swap(array, axis, by):
    return lax.ppermute(array, axis, [(i, i ^ by) for i in range(lax.axis_size(axis))])


def two_groups(
    tokens_in, query_weight, key_weight, value_weight, conv_weight, prompt_lengths, decode_map
):
    width = tokens_in.shape[2]
    given = (tokens_in, query_weight, key_weight, value_weight)
    length, slot = prompt_lengths.reshape(1, 1), decode_map.reshape(1, 1)
    *parts, early = project(0, *given)
    sent = [across(parts)]
    parts = project(1, *given, length, early)
    sent.append(across(parts))
    *first, taps = group_state(0, length, sent[0], conv_weight, [])
    second = group_state(1, length, sent[1], taps, [first[2]])
    got = [swap(held[2], "blk", GROUP) for held in (first, second)]
    aug, qk, own = first
    num = local_part(aug, qk, 1000, [second[2]])
    early = finish(0, length, slot, num, own, got[0], qk, taps, [])
    aug, qk, own = second
    num = local_part(aug, qk, 5_000_000_000, [early[4]])
    *parts, total = finish(1, length, slot, num, own, got[1], qk, taps, [early[4], *early[:4]])
    results = across(parts)
    beside = swap(total, "req", ROUTE[0])
    theirs = swap(hand_on(total, beside, results[1:2]), "req", ROUTE[1])
    state, norm = expand_state([total, beside, theirs], width // lax.axis_size("blk"))
    mixed = place_tokens(results, [theirs])
    return (mixed, jnp.swapaxes(state, 0, 1), jnp.swapaxes(norm, 1, 2))


def from_behind(array, axis, by):
    devices = lax.axis_size(axis)
    pairs = [(i, i + by) for i in range(devices) if 0 <= i + by < devices]
    return lax.ppermute(array, axis, pairs)


def entering(part, axis, combine, identity):
    place = lax.axis_index(axis)
    gathered = jax.tree.map(lambda a: lax.all_gather(a, axis), part)
    state = jax.tree.map(lambda a, e: jnp.zeros_like(a) + jnp.asarray(e, a.dtype), part, identity)

    def one(turn, state):
        return combine(
            state, jax.tree.map(lambda a: lax.dynamic_index_in_dim(a, turn, 0, False), gathered)
        )

    return lax.fori_loop(0, place, one, state)


def features_last(x):
    half = x * FEAT ** (-0.25)
    outer = half[:, :, None, :] * half[:, None, :, :]
    flat = outer.reshape(half.shape[0], FEAT * FEAT, half.shape[2]) * math.sqrt(0.5)
    ones = jnp.ones((half.shape[0], 1, half.shape[2]), jnp.float32)
    return jnp.concatenate([ones, half, flat], 1)


def add_pair(earlier, later):
    return (earlier[0] + later[0], earlier[1] + later[1])


def route_slot(pair, decode_map):
    groups = lax.axis_size("req")
    slots = (jnp.arange(groups, dtype=jnp.int32) == decode_map[0]).astype(jnp.float32)
    sent = (slots[:, None, None] * pair[0][None], slots[:, None, None] * pair[1][None])
    got = (
        lax.all_to_all(sent[0], "req", split_axis=0, concat_axis=0, tiled=True),
        lax.all_to_all(sent[1], "req", split_axis=0, concat_axis=0, tiled=True),
    )
    return (jnp.sum(got[0], 0), jnp.sum(got[1], 0))


def reduce_blocks(pair):
    return (
        lax.psum_scatter(pair[0], "blk", scatter_dimension=1, tiled=True),
        lax.psum_scatter(pair[1], "blk", scatter_dimension=1, tiled=True),
    )


def any_blocks(
    tokens_in, query_weight, key_weight, value_weight, conv_weight, prompt_lengths, decode_map
):
    rows = tokens_in.shape[1]
    width = tokens_in.shape[2]
    blocks = lax.axis_size("blk")
    head_size = width // HEADS
    hi = lax.Precision.HIGHEST
    inputs = tokens_in[0]
    queries = jnp.einsum(
        "dk,td->kt", query_weight, inputs, preferred_element_type=jnp.float32
    ).reshape(HEADS, FEAT, rows)
    keys = jnp.einsum("dk,td->kt", key_weight, inputs, preferred_element_type=jnp.float32).reshape(
        HEADS, FEAT, rows
    )
    values = jnp.dot(inputs, value_weight, preferred_element_type=jnp.float32).astype(jnp.bfloat16)
    earlier = from_behind(values[rows - (CONV - 1) :], "blk", 1)
    extended = jnp.concatenate([earlier, values], 0).astype(jnp.float32)
    conv = jnp.zeros((rows, width), jnp.float32)
    for tap in range(CONV):
        conv = conv + conv_weight[tap][None, :] * extended[CONV - 1 - tap : CONV - 1 - tap + rows]
    conv_t = conv.astype(jnp.bfloat16).astype(jnp.float32).T.reshape(HEADS, head_size, rows)
    start = lax.axis_index("blk") * rows
    live = (start + jnp.arange(rows, dtype=jnp.int32) < prompt_lengths[0]).astype(jnp.float32)
    feat_q = features_last(queries)
    feat_k = features_last(keys) * live[None, None, :]
    own_state = jnp.einsum("hft,hct->hfc", feat_k, conv_t, precision=hi)
    own_norm = jnp.sum(feat_k, 2)
    zero_state = jnp.zeros_like(own_state)
    zero_norm = jnp.zeros_like(own_norm)
    prior_state, prior_norm = entering(
        (own_state, own_norm), "blk", add_pair, (zero_state, zero_norm)
    )
    causal = (jnp.arange(rows)[:, None] >= jnp.arange(rows)[None, :]).astype(jnp.float32)
    scores = jnp.einsum("hft,hfs->hts", feat_q, feat_k, precision=hi) * causal[None]
    num = jnp.einsum("hts,hcs->hct", scores, conv_t, precision=hi) + jnp.einsum(
        "hft,hfc->hct", feat_q, prior_state, precision=hi
    )
    den = (
        jnp.sum(scores, -1)
        + jnp.einsum("hft,hf->ht", feat_q, prior_norm, precision=hi)
        + (1.0 - live)[None, :]
    )
    result = jnp.where(live[None, None, :] > 0, num / den[:, None, :], 0.0)
    mixed = result.reshape(width, rows).T.reshape(1, rows, width).astype(jnp.bfloat16)
    state_flat = jnp.transpose(own_state, (1, 0, 2)).reshape(own_state.shape[1], width)
    pair = (state_flat, jnp.tile(own_norm.T, (1, blocks)))
    final = route_slot(reduce_blocks(pair), decode_map)
    return (mixed, final[0][None], final[1][None])


def solution(mesh):
    def on_device(*args):
        rows = args[0].shape[1]
        if mesh.shape["blk"] == 2 * GROUP and mesh.shape["req"] == 4 and rows == LANES:
            return two_groups(*args)
        return any_blocks(*args)

    return jax.shard_map(
        on_device,
        mesh=mesh,
        in_specs=(P("req", "blk", None), P(), P(), P(), P(), P("req"), P("req")),
        out_specs=(P("req", "blk", None), P("req", None, "blk"), P("req", None, None)),
        check_vma=False,
    )
```

```python
import functools
import math

import jax
import jax.numpy as jnp
import numpy as np
from jax import lax
from jax.experimental import pallas as pl
from jax.experimental.pallas import tpu as pltpu
from jax.sharding import PartitionSpec as P

HEADS = 16
FEAT = 16
CONV = 3

GROUP = 4
SYM = 160
LANES = 128
REST = SYM - LANES
EDGE, KEYS = 25, 27
INFO = 31
LOCAL = HEADS // GROUP // 2
ORDER = (0, 3, 2, 1)
f32 = jnp.float32
bf16 = jnp.bfloat16
NT = (((1,), (1,)), ((), ()))
NN = (((1,), (0,)), ((), ()))


def dot(a, b, dims=NN):
    return lax.dot_general(a, b, dims, preferred_element_type=f32)


def iota(shape, axis):
    return lax.broadcasted_iota(jnp.int32, shape, axis)


def symmetric(y, scale_square):
    twice = jnp.concatenate([y, y], 0)
    rows = [y * y * scale_square] + [y * twice[o : o + FEAT] for o in range(1, 8)]
    rest = jnp.where(iota((8, y.shape[1]), 0) == 0, 1.0, 0.0)
    return jnp.concatenate(rows + [y, y[:8] * y[8:], rest], 0)


def call(kernel, outs, scratch, limit, flops, moved, args, spaces=(), after=()):
    vmem = pl.BlockSpec(memory_space=pltpu.VMEM)
    given = [pl.BlockSpec(memory_space=space) for space in spaces]
    if after:
        body, plain = kernel, len(args)

        def kernel(*refs):
            body(*refs[:plain], *refs[plain + len(after) :])

    return pl.pallas_call(
        kernel,
        out_shape=[jax.ShapeDtypeStruct(shape, dtype) for shape, dtype in outs],
        in_specs=given
        + [vmem] * (len(args) - len(given))
        + [pl.BlockSpec(memory_space=pl.ANY)] * len(after),
        out_specs=[vmem] * len(outs),
        scratch_shapes=scratch,
        compiler_params=pltpu.CompilerParams(vmem_limit_bytes=int(limit * 2**20)),
        cost_estimate=pl.CostEstimate(flops=flops, bytes_accessed=moved, transcendentals=0),
    )(*args, *after)


TILES = (384, 512)


def key_sums(keys):
    keyed, rows = keys.shape
    gram = dot(keys, keys, NT)
    same = iota((keyed, keyed), 0) // FEAT == iota((keyed, keyed), 1) // FEAT
    entry, lane = iota((FEAT, keyed), 0), iota((FEAT, keyed), 1)
    pick = (lax.rem(lane, FEAT) == entry).astype(bf16)
    folded = dot(pick, jnp.where(same, gram, 0.0).astype(bf16))
    plain = dot(jnp.ones((8, rows), bf16), keys, NT)
    mirror = lax.rem(entry - lax.rem(lane, FEAT) + FEAT, FEAT) == 9
    return jnp.where(mirror, plain[0:1], folded).astype(bf16)


def project_kernel(half, *refs):
    x, wq, wk, wv = refs[:4]
    refs = refs[4:]
    if half:
        length, early, o0, o1, o2, o3 = refs[:6]
        refs = refs[6:]
    else:
        o0, o1, o2, o3, early = refs[:5]
        refs = refs[5:]
    x_v, wqk_v, wv_v, vt, qkt, sems = refs[:6]
    rows = x.shape[1]
    width = wv.shape[1] // 2
    keyed = wq.shape[1] // 2
    get_x = pltpu.make_async_copy(x.at[0], x_v, sems.at[0])
    keyed_cut = pl.ds(half * keyed, keyed)
    get_k = pltpu.make_async_copy(wk.at[:, keyed_cut], wqk_v.at[:, pl.ds(0, keyed)], sems.at[1])
    get_q = pltpu.make_async_copy(wq.at[:, keyed_cut], wqk_v.at[:, pl.ds(keyed, keyed)], sems.at[2])
    copies, at = [], 0
    for j, tile in enumerate(TILES):
        source = wv.at[:, pl.ds(half * width + at, tile)]
        copies.append(pltpu.make_async_copy(source, wv_v.at[:, pl.ds(at, tile)], sems.at[3 + j]))
        at += tile
    for copy in (get_x, get_k, get_q, *copies):
        copy.start()
    place = lax.axis_index("blk")
    mine = lax.rem(place, GROUP)
    slab = width // GROUP
    get_x.wait()
    get_k.wait()
    get_q.wait()
    inputs = x_v[...]
    qkt[...] = dot(inputs, wqk_v[...]).T.astype(bf16)
    at = 0
    for tile, copy in zip(TILES, copies):
        copy.wait()
        vt[at : at + tile, :] = dot(inputs, wv_v[:, at : at + tile]).T.astype(bf16)
        at += tile
    part = keyed // GROUP
    for s, out in zip(ORDER, (o0, o1, o2, o3)):
        dest = mine ^ s
        out[0:slab, :] = vt[pl.ds(pl.multiple_of(slab * dest, 32), slab), :]
        for base, at in ((0, slab), (keyed, slab + part)):
            start = pl.multiple_of(base + part * dest, 32)
            out[at : at + part, :] = qkt[pl.ds(start, part), :]
    if not half:
        early[...] = qkt[0:keyed, :]
        return
    alive = place * rows + iota((1, rows), 1) < length[...]
    alive = jnp.where(alive, 1.0, 0.0).astype(bf16)
    sums = [key_sums(early[...] * alive), key_sums(qkt[0:keyed, :] * alive)]
    for out in (o0, o1, o2, o3):
        out[slab + 2 * part :, :] = jnp.concatenate(sums, 0)


def project(half, x, wq, wk, wv, *others):
    _, rows, width = x.shape
    keyed = wq.shape[1]
    total = (width + 2 * keyed) // GROUP // 2 + (2 * FEAT if half else 0)
    outs = [((total, rows), bf16)] * GROUP
    scratch = [
        pltpu.VMEM((rows, width), bf16),
        pltpu.VMEM((width, keyed), bf16),
        pltpu.VMEM((width, width // 2), bf16),
        pltpu.VMEM((width // 2, rows), bf16),
        pltpu.VMEM((keyed, rows), bf16),
        pltpu.SemaphoreType.DMA((3 + len(TILES),)),
    ]
    if not half:
        outs.append(((keyed // 2, rows), bf16))
    flops = rows * width * (width + 2 * keyed)
    kernel = functools.partial(project_kernel, half)
    limit = LIMIT_B if half else LIMIT_A
    args = [x, wq, wk, wv, *others]
    return call(kernel, outs, scratch, limit, flops, flops // rows, args, [pltpu.HBM] * 4)


LIMIT_A = 53.6
LIMIT_B = 16


def own_taps(conv, mine, taps, taps_v):
    half = conv.shape[1] // 2
    slab = half // GROUP
    wide = taps_v.shape[0]
    start = jnp.minimum(slab * mine // LANES * LANES, half - wide)
    inside = pl.multiple_of(slab * mine - start, 32)
    for h in range(2):
        cut = conv[:, pl.ds(pl.multiple_of(half * h + start, LANES), wide)]
        padded = jnp.concatenate([cut, jnp.zeros((8 - CONV, wide), f32)], 0)
        for j in range(wide // LANES):
            rows = slice(j * LANES, (j + 1) * LANES)
            taps_v[rows, :] = padded[:, rows].T
        taps[h * slab : (h + 1) * slab, :] = taps_v[pl.ds(inside, slab), :]


def state_kernel(half, *refs):
    length, p0, p1, p2, p3 = refs[:5]
    if half:
        taps, aug, qk, state, held = refs[5:]
    else:
        conv, aug, qk, state, taps, held, taps_v = refs[5:]
        own_taps(conv, lax.rem(lax.axis_index("blk"), GROUP), taps, taps_v)
    rows = p0.shape[1]
    place = lax.axis_index("blk")
    mine, group = lax.rem(place, GROUP), place // GROUP
    kept = held.shape[1]
    size = kept // LOCAL - 2 * FEAT
    values = LOCAL * size
    tokens = GROUP * rows
    for s, ref in zip(ORDER, (p0, p1, p2, p3)):
        held[mine ^ s] = ref[0:kept, :]
    if half:
        sums = p0[kept:, :].astype(f32) + p1[kept:, :].astype(f32)
        sums += p2[kept:, :].astype(f32) + p3[kept:, :].astype(f32)
        state[LOCAL * (size + REST) :, :] = sums.astype(bf16)
    for b in range(GROUP):
        qk[:, b * rows : (b + 1) * rows] = held[b, values:, :]
    alive = (group * tokens + iota((1, tokens), 1) < length[...]).astype(f32)
    token = iota((FEAT, tokens), 1)
    row = iota((FEAT, tokens), 0)
    marks = (row == 0) | ((row == 1) & (token == 0)) | ((row == 2) & (token == 1))
    marks = jnp.where(marks, alive, 0.0).astype(bf16)
    lane = iota((size, rows), 1)
    last = iota((REST, rows), 0)
    ends = iota((REST, rows), 1)
    ends = ((last == EDGE) & (ends == rows - 1)) | ((last == EDGE + 1) & (ends == rows - 2))
    ends = ends.astype(bf16)
    step = size + REST
    for h in range(LOCAL):
        cut = slice(h * size, (h + 1) * size)
        first = (half * LOCAL + h) * size
        tap = taps[first : first + size, :]
        tap = [jnp.broadcast_to(tap[:, t : t + 1], (size, rows)) for t in range(CONV)]
        before = [jnp.zeros((size, rows), f32)] * 2
        pieces = []
        for b in range(GROUP):
            now = held[b, cut, :].astype(f32)
            rolled = [pltpu.roll(now, 1, 1), pltpu.roll(now, 2, 1)]
            one = jnp.where(lane < 1, before[0], rolled[0])
            two = jnp.where(lane < 2, before[1], rolled[1])
            before = rolled
            mixed = tap[0] * now + tap[1] * one + tap[2] * two
            live = alive[:, b * rows : (b + 1) * rows]
            pieces.append(jnp.where(live > 0, mixed, 0.0).astype(bf16))
        aug_h = jnp.concatenate([jnp.concatenate(pieces, 1), marks], 0)
        aug[h] = aug_h
        y = qk[h * FEAT : (h + 1) * FEAT, :].astype(f32) * FEAT ** (-0.25)
        feats = symmetric(y, 1.0).astype(bf16)
        own = dot(aug_h, feats, NT)
        keys = pltpu.roll(own[size : size + 8, :LANES], KEYS % 8, 0)
        keys = jnp.concatenate([jnp.zeros((KEYS // 8 * 8, LANES), f32), keys], 0)
        edge = dot(ends, held[GROUP - 1, h * size : h * size + LANES, :], NT)
        rest = own[:, LANES:].T + edge + keys
        state[h * step : h * step + size, :] = own[:size, :LANES].astype(bf16)
        state[h * step + size : (h + 1) * step, :] = rest.astype(bf16)


def group_state(half, length, payloads, taps, after):
    total, rows = payloads[0].shape
    tokens = GROUP * rows
    extra = 2 * FEAT if half else 0
    outs = [
        ((LOCAL, LANES, tokens), bf16),
        ((2 * LOCAL * FEAT, tokens), bf16),
        (((total - extra) // LOCAL * LOCAL + extra, LANES), bf16),
    ]
    scratch = [pltpu.VMEM((GROUP, total - extra, rows), bf16)]
    if not half:
        slab = taps.shape[1] // GROUP
        outs.append(((slab, 8), f32))
        scratch.append(pltpu.VMEM(((slab // 2 // LANES + 2) * LANES, 8), f32))
    kernel = functools.partial(state_kernel, half)
    args = [length, *payloads, taps]
    return call(kernel, outs, scratch, 32, 100_000_000, 1_000_000, args, after=after)


def local_kernel(aug, qk, num):
    _, _, tokens = aug.shape
    keyed = LOCAL * FEAT
    half = tokens // 2
    keys = qk[0:keyed, :].astype(f32).T.astype(bf16)
    queries = qk[keyed:, :]
    head = iota((keyed, tokens), 0) // FEAT
    causal = iota((half, half), 0) <= iota((half, half), 1)

    def scores(d):
        return 1.0 + d * (0.25 + d * 0.03125)

    for h in range(LOCAL):
        only = jnp.where(head == h, queries, jnp.zeros_like(queries))
        first = scores(dot(keys[:half], only[:, :half]))
        first = jnp.where(causal, first, 0.0).astype(bf16)
        num[h, :, 0:half] = dot(aug[h, :, 0:half], first)
        lower = scores(dot(keys[half:], only[:, half:]))
        lower = jnp.where(causal, lower, 0.0).astype(bf16)
        upper = scores(dot(keys[:half], only[:, half:])).astype(bf16)
        num[h, :, half:] = dot(aug[h, :, 0:half], upper) + dot(aug[h, :, half:], lower)


def local_part(aug, qk, flops, after):
    _, _, tokens = aug.shape
    return call(local_kernel, [(aug.shape, f32)], [], 32, flops, 1000, [aug, qk], after=after)[0]


def finish_kernel(half, *refs):
    if half:
        slot, *refs = refs
    length, num, own, got, qk, taps = refs[:6]
    refs = refs[6:]
    if half:
        other, *firsts = refs[:5]
        refs = refs[5:]
    r0, r1, r2, r3, route, scr = refs
    _, _, tokens = num.shape
    rows = tokens // GROUP
    size = taps.shape[0] // 2 // LOCAL
    keyed = LOCAL * FEAT
    place = lax.axis_index("blk")
    mine, group = lax.rem(place, GROUP), place // GROUP
    upper = group == 1
    weight = jnp.where(upper, 1.0, 0.0)
    alive = group * tokens + iota((1, tokens), 1) < length[...]
    first = (iota((size, LANES), 1) == 0) & upper
    aux = iota((LANES - size, SYM), 0)
    step = size + REST

    def whole(ref, h):
        rest = ref[h * step + size : (h + 1) * step, :].astype(f32)
        tail = [rest[KEYS : KEYS + 3], jnp.zeros((LANES - size - 3, LANES), f32)]
        main = [ref[h * step : h * step + size, :].astype(f32), *tail]
        return jnp.concatenate([jnp.concatenate(main, 0), rest.T], 1)

    finals = []
    for h in range(LOCAL):
        here, there = whole(own, h), whole(got, h)
        low = jnp.where(upper, there, here)
        high = jnp.where(upper, here, there)
        at = (half * LOCAL + h) * size
        tap = taps[at : at + size, :]
        last, second = low[:size, 153:154], low[:size, 154:155]
        change0 = tap[:, 1:2] * last + tap[:, 2:3] * second
        change1 = tap[:, 2:3] * last
        key0, key1 = high[size + 1 : size + 2, :], high[size + 2 : size + 3, :]
        body = low[:size] + change0 * key0 + change1 * key1
        tail = jnp.where(aux == 2, key1, low[size:])
        prior = jnp.concatenate([body, tail], 0)
        finals.append(jnp.concatenate([body + high[:size], low[size:] + high[size:]], 0))
        y = qk[keyed + h * FEAT : keyed + (h + 1) * FEAT, :].astype(f32) * FEAT ** (-0.25)
        feats = symmetric(y, 0.5).astype(bf16)
        all_num = num[h] + weight * dot(prior.astype(bf16), feats)
        den = jnp.where(alive, all_num[size : size + 1, :], 1.0)
        inverse = jnp.where(alive, 1.0 / den, 0.0)
        top = all_num[:size]
        extra = all_num[size + 2 : size + 3, 0:1]
        edge = top[:, :LANES] - jnp.where(first, change1 * extra, 0.0)
        top = jnp.concatenate([edge, top[:, LANES:]], 1)
        result = (top * inverse).astype(bf16)
        for b in range(GROUP):
            scr[b, h * size : (h + 1) * size, :] = result[:, b * rows : (b + 1) * rows]
    for j, (s, out) in enumerate(zip(ORDER, (r0, r1, r2, r3))):
        if half:
            out[0 : LOCAL * size, :] = firsts[j][...]
        out[half * LOCAL * size :, :] = scr[mine ^ s]
    if not half:
        for c in range(LOCAL):
            route[c * step : c * step + size, :] = finals[c][:size, :LANES].astype(bf16)
            route[c * step + size : (c + 1) * step, :] = finals[c][:, LANES:].T.astype(bf16)
        return
    count = length[...]
    for c in range(LOCAL):
        cut = slice(c * step, c * step + size)
        final = jnp.where(upper, finals[c][:size, :LANES], other[cut, :].astype(f32))
        route[cut, :] = final.astype(bf16)
        cut = slice(c * step + size, (c + 1) * step)
        final = jnp.where(upper, finals[c][:, LANES:].T, other[cut, :].astype(f32))
        if c == 0:
            row, lane = iota(final.shape, 0), iota(final.shape, 1)
            values = (slot[0], lax.shift_right_logical(count, 8), count & 255)
            for at, value in enumerate(values):
                final = jnp.where((row == INFO) & (lane == at), value.astype(f32), final)
        route[cut, :] = final.astype(bf16)
    sums = own[LOCAL * step :, :].astype(f32) + got[LOCAL * step :, :].astype(f32)
    route[LOCAL * step :, :] = sums.astype(bf16)


def finish(half, length, slot, num, own, got, qk, taps, other):
    _, _, tokens = num.shape
    rows = tokens // GROUP
    width = taps.shape[0] // 2
    outs = [(((1 + half) * width, rows), bf16)] * GROUP + [(own.shape, bf16)]
    scratch = [pltpu.VMEM((GROUP, width, rows), bf16)]
    args = [slot] * half + [length, num, own, got, qk, taps] + other
    kernel = functools.partial(finish_kernel, half)
    return call(kernel, outs, scratch, 32, 50_000_000, 20_000_000, args, [pltpu.SMEM] * half)


def place_kernel(r0, r1, r2, r3, mixed, scr, turned, sems):
    width = scr.shape[0]
    mine = lax.rem(lax.axis_index("blk"), GROUP)
    half = width // 2
    slab = half // GROUP
    for s, ref in zip(ORDER, (r0, r1, r2, r3)):
        start = pl.multiple_of(slab * (mine ^ s), 32)
        scr[pl.ds(start, slab), :] = ref[0:slab, :]
        scr[pl.ds(pl.multiple_of(half + start, 32), slab), :] = ref[slab:, :]
    copies = []
    for j in range(width // LANES):
        cut = slice(j * LANES, (j + 1) * LANES)
        turned[:, cut] = scr[cut, :].T
        if j % 2:
            cut = pl.ds((j - 1) * LANES, 2 * LANES)
            copies.append(
                pltpu.make_async_copy(turned.at[:, cut], mixed.at[0, :, cut], sems.at[j // 2])
            )
            copies[-1].start()
    for copy in copies:
        copy.wait()


def place_tokens(results, after):
    part, rows = results[0].shape
    width = part * GROUP

    def kernel(*refs):
        place_kernel(*refs[:GROUP], *refs[GROUP + len(after) :])

    vmem, hbm = (pl.BlockSpec(memory_space=space) for space in (pltpu.VMEM, pl.ANY))
    return pl.pallas_call(
        kernel,
        out_shape=jax.ShapeDtypeStruct((1, rows, width), bf16),
        in_specs=[vmem] * GROUP + [hbm] * len(after),
        out_specs=hbm,
        scratch_shapes=[
            pltpu.VMEM((width, rows), bf16),
            pltpu.VMEM((rows, width), bf16),
            pltpu.SemaphoreType.DMA((width // LANES // 2,)),
        ],
        compiler_params=pltpu.CompilerParams(vmem_limit_bytes=32 * 2**20),
        cost_estimate=pl.CostEstimate(flops=1000, bytes_accessed=1_000_000, transcendentals=0),
    )(*results, *after)


ROUTE = (2, 1)


def hand_on_kernel(own, got, out):
    other = (lax.axis_index("req") ^ ROUTE[1]).astype(f32)
    kept = jnp.zeros(out.shape, f32)
    for ref in (own, got):
        at = (ref.shape[0] - 2 * FEAT) // LOCAL - REST + INFO
        here = ref[at : at + 1, 0:1].astype(f32) == other
        kept += jnp.where(here, ref[...].astype(f32), 0.0)
    out[...] = kept.astype(bf16)


def hand_on(own, got, after):
    args = [own, got]
    return call(hand_on_kernel, [(own.shape, bf16)], [], 32, 1000, 300_000, args, after=after)[0]


def expand_kernel(c0, c1, c2, spread, state, norm):
    me = lax.axis_index("req").astype(f32)
    kept = jnp.zeros(c0.shape, f32)
    step = (c0.shape[0] - 2 * FEAT) // LOCAL
    at = step - REST + INFO
    for ref in (c0, c1, c2):
        here = ref[at : at + 1, 0:1].astype(f32) == me
        kept += jnp.where(here, ref[...].astype(f32), 0.0)
    size = state.shape[2] // LOCAL
    expand = state.shape[0]
    scale = jnp.where(iota((expand, size), 0) > FEAT, math.sqrt(0.5), 1.0)
    wholes = []
    for c in range(LOCAL):
        main = kept[c * step : c * step + size].astype(bf16)
        rest = kept[c * step + size : (c + 1) * step].astype(bf16)
        whole = dot(spread[:, :LANES], main, NT) + dot(spread[:, LANES:], rest)[:, :size]
        wholes.append(whole * scale)
    state[...] = jnp.concatenate(wholes, 1).reshape(state.shape)
    sums = kept[LOCAL * step :]
    keyed = HEADS * FEAT
    sums = jnp.concatenate([sums[:FEAT], sums[FEAT:]], 1)
    plain = jnp.concatenate([sums[9:], sums[:9]], 0) * FEAT ** (-0.25)
    products = sums * FEAT ** (-0.5)
    b = iota((FEAT, keyed), 0)
    entry = lax.rem(iota((FEAT, keyed), 1), FEAT)
    big = [jnp.where(entry == b, plain, 0.0)]
    for a in range(FEAT):
        mirror = b == (a + 9) % FEAT
        row = jnp.where(mirror, products[a : a + 1], products)
        big.append(jnp.where(entry == jnp.where(mirror, b, a), row, 0.0))
    big = jnp.concatenate(big, 0)
    gather = (iota((keyed, HEADS), 0) // FEAT == iota((keyed, HEADS), 1)).astype(bf16)
    rest = dot(big.astype(bf16), gather)
    rest = rest * jnp.where(iota(rest.shape, 0) >= FEAT, math.sqrt(0.5), 1.0)
    info = kept[at : at + 1]
    count = info[:, 1:2] * 256.0 + info[:, 2:3]
    norm[0] = jnp.concatenate([jnp.broadcast_to(count, (1, HEADS)), rest], 0).T


def spread_rows():
    table = np.zeros((1 + FEAT + FEAT * FEAT, SYM), np.float32)
    table[0, 152] = 1
    for a in range(FEAT):
        table[1 + a, 128 + a] = 1
        for b in range(FEAT):
            o = (b - a) % FEAT
            at = o * FEAT + a if o < 8 else (144 + min(a, b) if o == 8 else (FEAT - o) * FEAT + b)
            table[1 + FEAT + a * FEAT + b, at] = 1
    return table


def expand_state(candidates, columns):
    spread = jnp.asarray(spread_rows(), bf16)
    expand = spread.shape[0]
    outs = [((expand, 1, columns), f32), ((1, HEADS, expand), f32)]
    return call(expand_kernel, outs, [], 32, 40_000_000, 1_000_000, [*candidates, spread])


def across(arrays):
    return [swap(array, "blk", s) if s else array for s, array in zip(ORDER, arrays)]


def swap(array, axis, by):
    return lax.ppermute(array, axis, [(i, i ^ by) for i in range(lax.axis_size(axis))])


def two_groups(
    tokens_in, query_weight, key_weight, value_weight, conv_weight, prompt_lengths, decode_map
):
    width = tokens_in.shape[2]
    given = (tokens_in, query_weight, key_weight, value_weight)
    length, slot = prompt_lengths.reshape(1, 1), decode_map
    *parts, early = project(0, *given)
    sent = [across(parts)]
    parts = project(1, *given, length, early)
    sent.append(across(parts))
    *first, taps = group_state(0, length, sent[0], conv_weight, [])
    second = group_state(1, length, sent[1], taps, [first[2]])
    got = [swap(held[2], "blk", GROUP) for held in (first, second)]
    aug, qk, own = first
    num = local_part(aug, qk, 1000, [second[2]])
    early = finish(0, length, slot, num, own, got[0], qk, taps, [])
    aug, qk, own = second
    num = local_part(aug, qk, 5_000_000_000, [early[4]])
    *parts, total = finish(1, length, slot, num, own, got[1], qk, taps, [early[4], *early[:4]])
    results = across(parts)
    beside = swap(total, "req", ROUTE[0])
    theirs = swap(hand_on(total, beside, []), "req", ROUTE[1])
    state, norm = expand_state([total, beside, theirs], width // lax.axis_size("blk"))
    mixed = place_tokens(results, [theirs])
    return (mixed, jnp.swapaxes(state, 0, 1), jnp.swapaxes(norm, 1, 2))


def from_behind(array, axis, by):
    devices = lax.axis_size(axis)
    pairs = [(i, i + by) for i in range(devices) if 0 <= i + by < devices]
    return lax.ppermute(array, axis, pairs)


def entering(part, axis, combine, identity):
    place = lax.axis_index(axis)
    gathered = jax.tree.map(lambda a: lax.all_gather(a, axis), part)
    state = jax.tree.map(lambda a, e: jnp.zeros_like(a) + jnp.asarray(e, a.dtype), part, identity)

    def one(turn, state):
        return combine(
            state, jax.tree.map(lambda a: lax.dynamic_index_in_dim(a, turn, 0, False), gathered)
        )

    return lax.fori_loop(0, place, one, state)


def features_last(x):
    half = x * FEAT ** (-0.25)
    outer = half[:, :, None, :] * half[:, None, :, :]
    flat = outer.reshape(half.shape[0], FEAT * FEAT, half.shape[2]) * math.sqrt(0.5)
    ones = jnp.ones((half.shape[0], 1, half.shape[2]), jnp.float32)
    return jnp.concatenate([ones, half, flat], 1)


def add_pair(earlier, later):
    return (earlier[0] + later[0], earlier[1] + later[1])


def route_slot(pair, decode_map):
    groups = lax.axis_size("req")
    slots = (jnp.arange(groups, dtype=jnp.int32) == decode_map[0]).astype(jnp.float32)
    sent = (slots[:, None, None] * pair[0][None], slots[:, None, None] * pair[1][None])
    got = (
        lax.all_to_all(sent[0], "req", split_axis=0, concat_axis=0, tiled=True),
        lax.all_to_all(sent[1], "req", split_axis=0, concat_axis=0, tiled=True),
    )
    return (jnp.sum(got[0], 0), jnp.sum(got[1], 0))


def reduce_blocks(pair):
    return (
        lax.psum_scatter(pair[0], "blk", scatter_dimension=1, tiled=True),
        lax.psum_scatter(pair[1], "blk", scatter_dimension=1, tiled=True),
    )


def any_blocks(
    tokens_in, query_weight, key_weight, value_weight, conv_weight, prompt_lengths, decode_map
):
    rows = tokens_in.shape[1]
    width = tokens_in.shape[2]
    blocks = lax.axis_size("blk")
    head_size = width // HEADS
    hi = lax.Precision.HIGHEST
    inputs = tokens_in[0]
    queries = jnp.einsum(
        "dk,td->kt", query_weight, inputs, preferred_element_type=jnp.float32
    ).reshape(HEADS, FEAT, rows)
    keys = jnp.einsum("dk,td->kt", key_weight, inputs, preferred_element_type=jnp.float32).reshape(
        HEADS, FEAT, rows
    )
    values = jnp.dot(inputs, value_weight, preferred_element_type=jnp.float32).astype(jnp.bfloat16)
    earlier = from_behind(values[rows - (CONV - 1) :], "blk", 1)
    extended = jnp.concatenate([earlier, values], 0).astype(jnp.float32)
    conv = jnp.zeros((rows, width), jnp.float32)
    for tap in range(CONV):
        conv = conv + conv_weight[tap][None, :] * extended[CONV - 1 - tap : CONV - 1 - tap + rows]
    conv_t = conv.astype(jnp.bfloat16).astype(jnp.float32).T.reshape(HEADS, head_size, rows)
    start = lax.axis_index("blk") * rows
    live = (start + jnp.arange(rows, dtype=jnp.int32) < prompt_lengths[0]).astype(jnp.float32)
    feat_q = features_last(queries)
    feat_k = features_last(keys) * live[None, None, :]
    own_state = jnp.einsum("hft,hct->hfc", feat_k, conv_t, precision=hi)
    own_norm = jnp.sum(feat_k, 2)
    zero_state = jnp.zeros_like(own_state)
    zero_norm = jnp.zeros_like(own_norm)
    prior_state, prior_norm = entering(
        (own_state, own_norm), "blk", add_pair, (zero_state, zero_norm)
    )
    causal = (jnp.arange(rows)[:, None] >= jnp.arange(rows)[None, :]).astype(jnp.float32)
    scores = jnp.einsum("hft,hfs->hts", feat_q, feat_k, precision=hi) * causal[None]
    num = jnp.einsum("hts,hcs->hct", scores, conv_t, precision=hi) + jnp.einsum(
        "hft,hfc->hct", feat_q, prior_state, precision=hi
    )
    den = (
        jnp.sum(scores, -1)
        + jnp.einsum("hft,hf->ht", feat_q, prior_norm, precision=hi)
        + (1.0 - live)[None, :]
    )
    result = jnp.where(live[None, None, :] > 0, num / den[:, None, :], 0.0)
    mixed = result.reshape(width, rows).T.reshape(1, rows, width).astype(jnp.bfloat16)
    state_flat = jnp.transpose(own_state, (1, 0, 2)).reshape(own_state.shape[1], width)
    pair = (state_flat, jnp.tile(own_norm.T, (1, blocks)))
    final = route_slot(reduce_blocks(pair), decode_map)
    return (mixed, final[0][None], final[1][None])


def solution(mesh):
    def on_device(*args):
        rows = args[0].shape[1]
        if mesh.shape["blk"] == 2 * GROUP and mesh.shape["req"] == 4 and rows == LANES:
            return two_groups(*args)
        return any_blocks(*args)

    return jax.shard_map(
        on_device,
        mesh=mesh,
        in_specs=(P("req", "blk", None), P(), P(), P(), P(), P("req"), P("req")),
        out_specs=(P("req", "blk", None), P("req", None, "blk"), P("req", None, None)),
        check_vma=False,
    )
```

```python
import functools
import math

import jax
import jax.numpy as jnp
import numpy as np
from jax import lax
from jax.experimental import pallas as pl
from jax.experimental.pallas import tpu as pltpu
from jax.sharding import PartitionSpec as P

HEADS = 16
FEAT = 16
CONV = 3

GROUP = 4
SYM = 160
LANES = 128
REST = SYM - LANES
EDGE, KEYS = 25, 27
INFO = 31
LOCAL = HEADS // GROUP // 2
ORDER = (0, 3, 2, 1)
f32 = jnp.float32
bf16 = jnp.bfloat16
NT = (((1,), (1,)), ((), ()))
NN = (((1,), (0,)), ((), ()))


def dot(a, b, dims=NN):
    return lax.dot_general(a, b, dims, preferred_element_type=f32)


def iota(shape, axis):
    return lax.broadcasted_iota(jnp.int32, shape, axis)


def symmetric(y, scale_square):
    twice = jnp.concatenate([y, y], 0)
    rows = [y * y * scale_square] + [y * twice[o : o + FEAT] for o in range(1, 8)]
    rest = jnp.where(iota((8, y.shape[1]), 0) == 0, 1.0, 0.0)
    return jnp.concatenate(rows + [y, y[:8] * y[8:], rest], 0)


def call(kernel, outs, scratch, limit, flops, moved, args, spaces=(), after=()):
    vmem = pl.BlockSpec(memory_space=pltpu.VMEM)
    given = [pl.BlockSpec(memory_space=space) for space in spaces]
    if after:
        body, plain = kernel, len(args)

        def kernel(*refs):
            body(*refs[:plain], *refs[plain + len(after) :])

    return pl.pallas_call(
        kernel,
        out_shape=[jax.ShapeDtypeStruct(shape, dtype) for shape, dtype in outs],
        in_specs=given
        + [vmem] * (len(args) - len(given))
        + [pl.BlockSpec(memory_space=pl.ANY)] * len(after),
        out_specs=[vmem] * len(outs),
        scratch_shapes=scratch,
        compiler_params=pltpu.CompilerParams(vmem_limit_bytes=int(limit * 2**20)),
        cost_estimate=pl.CostEstimate(flops=flops, bytes_accessed=moved, transcendentals=0),
    )(*args, *after)


TILES = (384, 512)
TILES_B = (896,)


def key_sums(keys):
    keyed, rows = keys.shape
    gram = dot(keys, keys, NT)
    same = iota((keyed, keyed), 0) // FEAT == iota((keyed, keyed), 1) // FEAT
    entry, lane = iota((FEAT, keyed), 0), iota((FEAT, keyed), 1)
    pick = (lax.rem(lane, FEAT) == entry).astype(bf16)
    folded = dot(pick, jnp.where(same, gram, 0.0).astype(bf16))
    plain = dot(jnp.ones((8, rows), bf16), keys, NT)
    mirror = lax.rem(entry - lax.rem(lane, FEAT) + FEAT, FEAT) == 9
    return jnp.where(mirror, plain[0:1], folded).astype(bf16)


def project_kernel(half, *refs):
    x, wq, wk, wv = refs[:4]
    refs = refs[4:]
    if half:
        length, early, o0, o1, o2, o3 = refs[:6]
        refs = refs[6:]
    else:
        o0, o1, o2, o3, early = refs[:5]
        refs = refs[5:]
    rows = x.shape[1]
    width = wv.shape[1] // 2
    keyed = wq.shape[1] // 2
    place = lax.axis_index("blk")
    mine = lax.rem(place, GROUP)
    slab = width // GROUP
    if half:
        vt, qkt = refs
        inputs = x[0]
        both = jnp.concatenate([wk[:, keyed:], wq[:, keyed:]], 1)
        qkt[...] = dot(inputs, both).T.astype(bf16)
        at = 0
        for tile in TILES_B:
            weights = wv[:, width + at : width + at + tile]
            vt[at : at + tile, :] = dot(inputs, weights).T.astype(bf16)
            at += tile
    else:
        vt, qkt, x_v, wqk_v, wv_v, sems = refs
        first, second = pl.ds(0, keyed), pl.ds(keyed, keyed)
        needed = [
            pltpu.make_async_copy(x.at[0], x_v, sems.at[0]),
            pltpu.make_async_copy(wk.at[:, first], wqk_v.at[:, first], sems.at[1]),
            pltpu.make_async_copy(wq.at[:, first], wqk_v.at[:, second], sems.at[2]),
        ]
        copies, at = [], 0
        for j, tile in enumerate(TILES):
            cut = pl.ds(at, tile)
            copies.append(pltpu.make_async_copy(wv.at[:, cut], wv_v.at[:, cut], sems.at[3 + j]))
            at += tile
        for copy in (*needed, *copies):
            copy.start()
        for copy in needed:
            copy.wait()
        inputs = x_v[...]
        qkt[...] = dot(inputs, wqk_v[...]).T.astype(bf16)
        at = 0
        for tile, copy in zip(TILES, copies):
            copy.wait()
            vt[at : at + tile, :] = dot(inputs, wv_v[:, at : at + tile]).T.astype(bf16)
            at += tile
    part = keyed // GROUP
    for s, out in zip(ORDER, (o0, o1, o2, o3)):
        dest = mine ^ s
        out[0:slab, :] = vt[pl.ds(pl.multiple_of(slab * dest, 32), slab), :]
        for base, at in ((0, slab), (keyed, slab + part)):
            start = pl.multiple_of(base + part * dest, 32)
            out[at : at + part, :] = qkt[pl.ds(start, part), :]
    if not half:
        early[...] = qkt[0:keyed, :]
        return
    alive = place * rows + iota((1, rows), 1) < length[...]
    alive = jnp.where(alive, 1.0, 0.0).astype(bf16)
    sums = [key_sums(early[...] * alive), key_sums(qkt[0:keyed, :] * alive)]
    for out in (o0, o1, o2, o3):
        out[slab + 2 * part :, :] = jnp.concatenate(sums, 0)


def project(half, x, wq, wk, wv, *others):
    _, rows, width = x.shape
    keyed = wq.shape[1]
    total = (width + 2 * keyed) // GROUP // 2 + (2 * FEAT if half else 0)
    outs = [((total, rows), bf16)] * GROUP
    scratch = [pltpu.VMEM((width // 2, rows), bf16), pltpu.VMEM((keyed, rows), bf16)]
    if not half:
        outs.append(((keyed // 2, rows), bf16))
        scratch += [
            pltpu.VMEM((rows, width), bf16),
            pltpu.VMEM((width, keyed), bf16),
            pltpu.VMEM((width, width // 2), bf16),
            pltpu.SemaphoreType.DMA((3 + len(TILES),)),
        ]
    flops = rows * width * (width + 2 * keyed)
    kernel = functools.partial(project_kernel, half)
    limit = LIMIT_B if half else LIMIT_A
    args = [x, wq, wk, wv, *others]
    return call(kernel, outs, scratch, limit, flops, flops // rows, args, [] if half else [pltpu.HBM] * 4)


LIMIT_A = 53.6
LIMIT_B = 16


def own_taps(conv, mine, taps, taps_v):
    half = conv.shape[1] // 2
    slab = half // GROUP
    wide = taps_v.shape[0]
    start = jnp.minimum(slab * mine // LANES * LANES, half - wide)
    inside = pl.multiple_of(slab * mine - start, 32)
    for h in range(2):
        cut = conv[:, pl.ds(pl.multiple_of(half * h + start, LANES), wide)]
        padded = jnp.concatenate([cut, jnp.zeros((8 - CONV, wide), f32)], 0)
        for j in range(wide // LANES):
            rows = slice(j * LANES, (j + 1) * LANES)
            taps_v[rows, :] = padded[:, rows].T
        taps[h * slab : (h + 1) * slab, :] = taps_v[pl.ds(inside, slab), :]


def state_kernel(half, *refs):
    length, p0, p1, p2, p3 = refs[:5]
    if half:
        taps, aug, qk, state, held = refs[5:]
    else:
        conv, aug, qk, state, taps, held, taps_v = refs[5:]
        own_taps(conv, lax.rem(lax.axis_index("blk"), GROUP), taps, taps_v)
    rows = p0.shape[1]
    place = lax.axis_index("blk")
    mine, group = lax.rem(place, GROUP), place // GROUP
    kept = held.shape[1]
    size = kept // LOCAL - 2 * FEAT
    values = LOCAL * size
    tokens = GROUP * rows
    for s, ref in zip(ORDER, (p0, p1, p2, p3)):
        held[mine ^ s] = ref[0:kept, :]
    if half:
        sums = p0[kept:, :].astype(f32) + p1[kept:, :].astype(f32)
        sums += p2[kept:, :].astype(f32) + p3[kept:, :].astype(f32)
        state[LOCAL * (size + REST) :, :] = sums.astype(bf16)
    for b in range(GROUP):
        qk[:, b * rows : (b + 1) * rows] = held[b, values:, :]
    alive = (group * tokens + iota((1, tokens), 1) < length[...]).astype(f32)
    token = iota((FEAT, tokens), 1)
    row = iota((FEAT, tokens), 0)
    marks = (row == 0) | ((row == 1) & (token == 0)) | ((row == 2) & (token == 1))
    marks = jnp.where(marks, alive, 0.0).astype(bf16)
    lane = iota((size, rows), 1)
    last = iota((REST, rows), 0)
    ends = iota((REST, rows), 1)
    ends = ((last == EDGE) & (ends == rows - 1)) | ((last == EDGE + 1) & (ends == rows - 2))
    ends = ends.astype(bf16)
    step = size + REST
    for h in range(LOCAL):
        cut = slice(h * size, (h + 1) * size)
        first = (half * LOCAL + h) * size
        tap = taps[first : first + size, :]
        tap = [jnp.broadcast_to(tap[:, t : t + 1], (size, rows)) for t in range(CONV)]
        before = [jnp.zeros((size, rows), f32)] * 2
        pieces = []
        for b in range(GROUP):
            now = held[b, cut, :].astype(f32)
            rolled = [pltpu.roll(now, 1, 1), pltpu.roll(now, 2, 1)]
            one = jnp.where(lane < 1, before[0], rolled[0])
            two = jnp.where(lane < 2, before[1], rolled[1])
            before = rolled
            mixed = tap[0] * now + tap[1] * one + tap[2] * two
            live = alive[:, b * rows : (b + 1) * rows]
            pieces.append(jnp.where(live > 0, mixed, 0.0).astype(bf16))
        aug_h = jnp.concatenate([jnp.concatenate(pieces, 1), marks], 0)
        aug[h] = aug_h
        y = qk[h * FEAT : (h + 1) * FEAT, :].astype(f32) * FEAT ** (-0.25)
        feats = symmetric(y, 1.0).astype(bf16)
        own = dot(aug_h, feats, NT)
        keys = pltpu.roll(own[size : size + 8, :LANES], KEYS % 8, 0)
        keys = jnp.concatenate([jnp.zeros((KEYS // 8 * 8, LANES), f32), keys], 0)
        edge = dot(ends, held[GROUP - 1, h * size : h * size + LANES, :], NT)
        rest = own[:, LANES:].T + edge + keys
        state[h * step : h * step + size, :] = own[:size, :LANES].astype(bf16)
        state[h * step + size : (h + 1) * step, :] = rest.astype(bf16)


def group_state(half, length, payloads, taps, after):
    total, rows = payloads[0].shape
    tokens = GROUP * rows
    extra = 2 * FEAT if half else 0
    outs = [
        ((LOCAL, LANES, tokens), bf16),
        ((2 * LOCAL * FEAT, tokens), bf16),
        (((total - extra) // LOCAL * LOCAL + extra, LANES), bf16),
    ]
    scratch = [pltpu.VMEM((GROUP, total - extra, rows), bf16)]
    if not half:
        slab = taps.shape[1] // GROUP
        outs.append(((slab, 8), f32))
        scratch.append(pltpu.VMEM(((slab // 2 // LANES + 2) * LANES, 8), f32))
    kernel = functools.partial(state_kernel, half)
    args = [length, *payloads, taps]
    return call(kernel, outs, scratch, 32, 100_000_000, 1_000_000, args, after=after)


def local_kernel(aug, qk, num):
    _, _, tokens = aug.shape
    keyed = LOCAL * FEAT
    half = tokens // 2
    keys = qk[0:keyed, :].astype(f32).T.astype(bf16)
    queries = qk[keyed:, :]
    head = iota((keyed, tokens), 0) // FEAT
    causal = iota((half, half), 0) <= iota((half, half), 1)

    def scores(d):
        return 1.0 + d * (0.25 + d * 0.03125)

    for h in range(LOCAL):
        only = jnp.where(head == h, queries, jnp.zeros_like(queries))
        first = scores(dot(keys[:half], only[:, :half]))
        first = jnp.where(causal, first, 0.0).astype(bf16)
        num[h, :, 0:half] = dot(aug[h, :, 0:half], first)
        lower = scores(dot(keys[half:], only[:, half:]))
        lower = jnp.where(causal, lower, 0.0).astype(bf16)
        upper = scores(dot(keys[:half], only[:, half:])).astype(bf16)
        num[h, :, half:] = dot(aug[h, :, 0:half], upper) + dot(aug[h, :, half:], lower)


def local_part(aug, qk, flops, after):
    _, _, tokens = aug.shape
    return call(local_kernel, [(aug.shape, f32)], [], 32, flops, 1000, [aug, qk], after=after)[0]


def finish_kernel(half, *refs):
    if half:
        slot, *refs = refs
    length, num, own, got, qk, taps = refs[:6]
    refs = refs[6:]
    if half:
        other, *firsts = refs[:5]
        refs = refs[5:]
    r0, r1, r2, r3, route, scr = refs
    _, _, tokens = num.shape
    rows = tokens // GROUP
    size = taps.shape[0] // 2 // LOCAL
    keyed = LOCAL * FEAT
    place = lax.axis_index("blk")
    mine, group = lax.rem(place, GROUP), place // GROUP
    upper = group == 1
    weight = jnp.where(upper, 1.0, 0.0)
    alive = group * tokens + iota((1, tokens), 1) < length[...]
    first = (iota((size, LANES), 1) == 0) & upper
    aux = iota((LANES - size, SYM), 0)
    step = size + REST

    def whole(ref, h):
        rest = ref[h * step + size : (h + 1) * step, :].astype(f32)
        tail = [rest[KEYS : KEYS + 3], jnp.zeros((LANES - size - 3, LANES), f32)]
        main = [ref[h * step : h * step + size, :].astype(f32), *tail]
        return jnp.concatenate([jnp.concatenate(main, 0), rest.T], 1)

    finals = []
    for h in range(LOCAL):
        here, there = whole(own, h), whole(got, h)
        low = jnp.where(upper, there, here)
        high = jnp.where(upper, here, there)
        at = (half * LOCAL + h) * size
        tap = taps[at : at + size, :]
        last, second = low[:size, 153:154], low[:size, 154:155]
        change0 = tap[:, 1:2] * last + tap[:, 2:3] * second
        change1 = tap[:, 2:3] * last
        key0, key1 = high[size + 1 : size + 2, :], high[size + 2 : size + 3, :]
        body = low[:size] + change0 * key0 + change1 * key1
        tail = jnp.where(aux == 2, key1, low[size:])
        prior = jnp.concatenate([body, tail], 0)
        finals.append(jnp.concatenate([body + high[:size], low[size:] + high[size:]], 0))
        y = qk[keyed + h * FEAT : keyed + (h + 1) * FEAT, :].astype(f32) * FEAT ** (-0.25)
        feats = symmetric(y, 0.5).astype(bf16)
        all_num = num[h] + weight * dot(prior.astype(bf16), feats)
        den = jnp.where(alive, all_num[size : size + 1, :], 1.0)
        inverse = jnp.where(alive, 1.0 / den, 0.0)
        top = all_num[:size]
        extra = all_num[size + 2 : size + 3, 0:1]
        edge = top[:, :LANES] - jnp.where(first, change1 * extra, 0.0)
        top = jnp.concatenate([edge, top[:, LANES:]], 1)
        result = (top * inverse).astype(bf16)
        for b in range(GROUP):
            scr[b, h * size : (h + 1) * size, :] = result[:, b * rows : (b + 1) * rows]
    for j, (s, out) in enumerate(zip(ORDER, (r0, r1, r2, r3))):
        if half:
            out[0 : LOCAL * size, :] = firsts[j][...]
        out[half * LOCAL * size :, :] = scr[mine ^ s]
    if not half:
        for c in range(LOCAL):
            route[c * step : c * step + size, :] = finals[c][:size, :LANES].astype(bf16)
            route[c * step + size : (c + 1) * step, :] = finals[c][:, LANES:].T.astype(bf16)
        return
    count = length[...]
    for c in range(LOCAL):
        cut = slice(c * step, c * step + size)
        final = jnp.where(upper, finals[c][:size, :LANES], other[cut, :].astype(f32))
        route[cut, :] = final.astype(bf16)
        cut = slice(c * step + size, (c + 1) * step)
        final = jnp.where(upper, finals[c][:, LANES:].T, other[cut, :].astype(f32))
        if c == 0:
            row, lane = iota(final.shape, 0), iota(final.shape, 1)
            values = (slot[0], lax.shift_right_logical(count, 8), count & 255)
            for at, value in enumerate(values):
                final = jnp.where((row == INFO) & (lane == at), value.astype(f32), final)
        route[cut, :] = final.astype(bf16)
    sums = own[LOCAL * step :, :].astype(f32) + got[LOCAL * step :, :].astype(f32)
    route[LOCAL * step :, :] = sums.astype(bf16)


def finish(half, length, slot, num, own, got, qk, taps, other):
    _, _, tokens = num.shape
    rows = tokens // GROUP
    width = taps.shape[0] // 2
    outs = [(((1 + half) * width, rows), bf16)] * GROUP + [(own.shape, bf16)]
    scratch = [pltpu.VMEM((GROUP, width, rows), bf16)]
    args = [slot] * half + [length, num, own, got, qk, taps] + other
    kernel = functools.partial(finish_kernel, half)
    return call(kernel, outs, scratch, 32, 50_000_000, 20_000_000, args, [pltpu.SMEM] * half)


def place_kernel(r0, r1, r2, r3, mixed, scr, turned, sems):
    width = scr.shape[0]
    mine = lax.rem(lax.axis_index("blk"), GROUP)
    half = width // 2
    slab = half // GROUP
    for s, ref in zip(ORDER, (r0, r1, r2, r3)):
        start = pl.multiple_of(slab * (mine ^ s), 32)
        scr[pl.ds(start, slab), :] = ref[0:slab, :]
        scr[pl.ds(pl.multiple_of(half + start, 32), slab), :] = ref[slab:, :]
    copies = []
    for j in range(width // LANES):
        cut = slice(j * LANES, (j + 1) * LANES)
        turned[:, cut] = scr[cut, :].T
        if j % 2:
            cut = pl.ds((j - 1) * LANES, 2 * LANES)
            copies.append(
                pltpu.make_async_copy(turned.at[:, cut], mixed.at[0, :, cut], sems.at[j // 2])
            )
            copies[-1].start()
    for copy in copies:
        copy.wait()


def place_tokens(results, after):
    part, rows = results[0].shape
    width = part * GROUP

    def kernel(*refs):
        place_kernel(*refs[:GROUP], *refs[GROUP + len(after) :])

    vmem, hbm = (pl.BlockSpec(memory_space=space) for space in (pltpu.VMEM, pl.ANY))
    return pl.pallas_call(
        kernel,
        out_shape=jax.ShapeDtypeStruct((1, rows, width), bf16),
        in_specs=[vmem] * GROUP + [hbm] * len(after),
        out_specs=hbm,
        scratch_shapes=[
            pltpu.VMEM((width, rows), bf16),
            pltpu.VMEM((rows, width), bf16),
            pltpu.SemaphoreType.DMA((width // LANES // 2,)),
        ],
        compiler_params=pltpu.CompilerParams(vmem_limit_bytes=32 * 2**20),
        cost_estimate=pl.CostEstimate(flops=1000, bytes_accessed=1_000_000, transcendentals=0),
    )(*results, *after)


ROUTE = (2, 1)


def hand_on_kernel(own, got, out):
    other = (lax.axis_index("req") ^ ROUTE[1]).astype(f32)
    kept = jnp.zeros(out.shape, f32)
    step = (own.shape[0] - 2 * FEAT) // LOCAL
    for ref in (own, got):
        here = ref[step - FEAT : step, :].astype(f32)[INFO % FEAT :, 0:1] == other
        kept += jnp.where(here, ref[...].astype(f32), 0.0)
    out[...] = kept.astype(bf16)


def hand_on(own, got, after):
    args = [own, got]
    return call(hand_on_kernel, [(own.shape, bf16)], [], 32, 1000, 300_000, args, after=after)[0]


def expand_kernel(c0, c1, c2, spread, state, norm):
    me = lax.axis_index("req").astype(f32)
    kept = jnp.zeros(c0.shape, f32)
    step = (c0.shape[0] - 2 * FEAT) // LOCAL
    at = step - REST + INFO
    for ref in (c0, c1, c2):
        here = ref[step - FEAT : step, :].astype(f32)[INFO % FEAT :, 0:1] == me
        kept += jnp.where(here, ref[...].astype(f32), 0.0)
    size = state.shape[2] // LOCAL
    expand = state.shape[0]
    scale = jnp.where(iota((expand, size), 0) > FEAT, math.sqrt(0.5), 1.0)
    wholes = []
    for c in range(LOCAL):
        main = kept[c * step : c * step + size].astype(bf16)
        rest = kept[c * step + size : (c + 1) * step].astype(bf16)
        whole = dot(spread[:, :LANES], main, NT) + dot(spread[:, LANES:], rest)[:, :size]
        wholes.append(whole * scale)
    state[...] = jnp.concatenate(wholes, 1).reshape(state.shape)
    sums = kept[LOCAL * step :]
    keyed = HEADS * FEAT
    sums = jnp.concatenate([sums[:FEAT], sums[FEAT:]], 1)
    plain = jnp.concatenate([sums[9:], sums[:9]], 0) * FEAT ** (-0.25)
    products = sums * FEAT ** (-0.5)
    b = iota((FEAT, keyed), 0)
    entry = lax.rem(iota((FEAT, keyed), 1), FEAT)
    big = [jnp.where(entry == b, plain, 0.0)]
    for a in range(FEAT):
        mirror = b == (a + 9) % FEAT
        row = jnp.where(mirror, products[a : a + 1], products)
        big.append(jnp.where(entry == jnp.where(mirror, b, a), row, 0.0))
    big = jnp.concatenate(big, 0)
    gather = (iota((keyed, HEADS), 0) // FEAT == iota((keyed, HEADS), 1)).astype(bf16)
    rest = dot(big.astype(bf16), gather)
    rest = rest * jnp.where(iota(rest.shape, 0) >= FEAT, math.sqrt(0.5), 1.0)
    info = kept[at : at + 1]
    count = info[:, 1:2] * 256.0 + info[:, 2:3]
    norm[0] = jnp.concatenate([jnp.broadcast_to(count, (1, HEADS)), rest], 0).T


def spread_rows():
    table = np.zeros((1 + FEAT + FEAT * FEAT, SYM), np.float32)
    table[0, 152] = 1
    for a in range(FEAT):
        table[1 + a, 128 + a] = 1
        for b in range(FEAT):
            o = (b - a) % FEAT
            at = o * FEAT + a if o < 8 else (144 + min(a, b) if o == 8 else (FEAT - o) * FEAT + b)
            table[1 + FEAT + a * FEAT + b, at] = 1
    return table


def expand_state(candidates, columns):
    spread = jnp.asarray(spread_rows(), bf16)
    expand = spread.shape[0]
    outs = [((expand, 1, columns), f32), ((1, HEADS, expand), f32)]
    return call(expand_kernel, outs, [], 32, 40_000_000, 1_000_000, [*candidates, spread])


def across(arrays):
    return [swap(array, "blk", s) if s else array for s, array in zip(ORDER, arrays)]


def swap(array, axis, by):
    return lax.ppermute(array, axis, [(i, i ^ by) for i in range(lax.axis_size(axis))])


def two_groups(
    tokens_in, query_weight, key_weight, value_weight, conv_weight, prompt_lengths, decode_map
):
    width = tokens_in.shape[2]
    given = (tokens_in, query_weight, key_weight, value_weight)
    length, slot = prompt_lengths.reshape(1, 1), decode_map
    *parts, early = project(0, *given)
    sent = [across(parts)]
    parts = project(1, *given, length, early)
    sent.append(across(parts))
    *first, taps = group_state(0, length, sent[0], conv_weight, [])
    second = group_state(1, length, sent[1], taps, [first[2]])
    got = [swap(held[2], "blk", GROUP) for held in (first, second)]
    aug, qk, own = first
    num = local_part(aug, qk, 1000, [second[2]])
    early = finish(0, length, slot, num, own, got[0], qk, taps, [])
    aug, qk, own = second
    num = local_part(aug, qk, 5_000_000_000, [early[4]])
    *parts, total = finish(1, length, slot, num, own, got[1], qk, taps, [early[4], *early[:4]])
    results = across(parts)
    beside = swap(total, "req", ROUTE[0])
    theirs = swap(hand_on(total, beside, []), "req", ROUTE[1])
    state, norm = expand_state([total, beside, theirs], width // lax.axis_size("blk"))
    mixed = place_tokens(results, [theirs])
    return (mixed, jnp.swapaxes(state, 0, 1), jnp.swapaxes(norm, 1, 2))


def from_behind(array, axis, by):
    devices = lax.axis_size(axis)
    pairs = [(i, i + by) for i in range(devices) if 0 <= i + by < devices]
    return lax.ppermute(array, axis, pairs)


def entering(part, axis, combine, identity):
    place = lax.axis_index(axis)
    gathered = jax.tree.map(lambda a: lax.all_gather(a, axis), part)
    state = jax.tree.map(lambda a, e: jnp.zeros_like(a) + jnp.asarray(e, a.dtype), part, identity)

    def one(turn, state):
        return combine(
            state, jax.tree.map(lambda a: lax.dynamic_index_in_dim(a, turn, 0, False), gathered)
        )

    return lax.fori_loop(0, place, one, state)


def features_last(x):
    half = x * FEAT ** (-0.25)
    outer = half[:, :, None, :] * half[:, None, :, :]
    flat = outer.reshape(half.shape[0], FEAT * FEAT, half.shape[2]) * math.sqrt(0.5)
    ones = jnp.ones((half.shape[0], 1, half.shape[2]), jnp.float32)
    return jnp.concatenate([ones, half, flat], 1)


def add_pair(earlier, later):
    return (earlier[0] + later[0], earlier[1] + later[1])


def route_slot(pair, decode_map):
    groups = lax.axis_size("req")
    slots = (jnp.arange(groups, dtype=jnp.int32) == decode_map[0]).astype(jnp.float32)
    sent = (slots[:, None, None] * pair[0][None], slots[:, None, None] * pair[1][None])
    got = (
        lax.all_to_all(sent[0], "req", split_axis=0, concat_axis=0, tiled=True),
        lax.all_to_all(sent[1], "req", split_axis=0, concat_axis=0, tiled=True),
    )
    return (jnp.sum(got[0], 0), jnp.sum(got[1], 0))


def reduce_blocks(pair):
    return (
        lax.psum_scatter(pair[0], "blk", scatter_dimension=1, tiled=True),
        lax.psum_scatter(pair[1], "blk", scatter_dimension=1, tiled=True),
    )


def any_blocks(
    tokens_in, query_weight, key_weight, value_weight, conv_weight, prompt_lengths, decode_map
):
    rows = tokens_in.shape[1]
    width = tokens_in.shape[2]
    blocks = lax.axis_size("blk")
    head_size = width // HEADS
    hi = lax.Precision.HIGHEST
    inputs = tokens_in[0]
    queries = jnp.einsum(
        "dk,td->kt", query_weight, inputs, preferred_element_type=jnp.float32
    ).reshape(HEADS, FEAT, rows)
    keys = jnp.einsum("dk,td->kt", key_weight, inputs, preferred_element_type=jnp.float32).reshape(
        HEADS, FEAT, rows
    )
    values = jnp.dot(inputs, value_weight, preferred_element_type=jnp.float32).astype(jnp.bfloat16)
    earlier = from_behind(values[rows - (CONV - 1) :], "blk", 1)
    extended = jnp.concatenate([earlier, values], 0).astype(jnp.float32)
    conv = jnp.zeros((rows, width), jnp.float32)
    for tap in range(CONV):
        conv = conv + conv_weight[tap][None, :] * extended[CONV - 1 - tap : CONV - 1 - tap + rows]
    conv_t = conv.astype(jnp.bfloat16).astype(jnp.float32).T.reshape(HEADS, head_size, rows)
    start = lax.axis_index("blk") * rows
    live = (start + jnp.arange(rows, dtype=jnp.int32) < prompt_lengths[0]).astype(jnp.float32)
    feat_q = features_last(queries)
    feat_k = features_last(keys) * live[None, None, :]
    own_state = jnp.einsum("hft,hct->hfc", feat_k, conv_t, precision=hi)
    own_norm = jnp.sum(feat_k, 2)
    zero_state = jnp.zeros_like(own_state)
    zero_norm = jnp.zeros_like(own_norm)
    prior_state, prior_norm = entering(
        (own_state, own_norm), "blk", add_pair, (zero_state, zero_norm)
    )
    causal = (jnp.arange(rows)[:, None] >= jnp.arange(rows)[None, :]).astype(jnp.float32)
    scores = jnp.einsum("hft,hfs->hts", feat_q, feat_k, precision=hi) * causal[None]
    num = jnp.einsum("hts,hcs->hct", scores, conv_t, precision=hi) + jnp.einsum(
        "hft,hfc->hct", feat_q, prior_state, precision=hi
    )
    den = (
        jnp.sum(scores, -1)
        + jnp.einsum("hft,hf->ht", feat_q, prior_norm, precision=hi)
        + (1.0 - live)[None, :]
    )
    result = jnp.where(live[None, None, :] > 0, num / den[:, None, :], 0.0)
    mixed = result.reshape(width, rows).T.reshape(1, rows, width).astype(jnp.bfloat16)
    state_flat = jnp.transpose(own_state, (1, 0, 2)).reshape(own_state.shape[1], width)
    pair = (state_flat, jnp.tile(own_norm.T, (1, blocks)))
    final = route_slot(reduce_blocks(pair), decode_map)
    return (mixed, final[0][None], final[1][None])


def solution(mesh):
    def on_device(*args):
        rows = args[0].shape[1]
        if mesh.shape["blk"] == 2 * GROUP and mesh.shape["req"] == 4 and rows == LANES:
            return two_groups(*args)
        return any_blocks(*args)

    return jax.shard_map(
        on_device,
        mesh=mesh,
        in_specs=(P("req", "blk", None), P(), P(), P(), P(), P("req"), P("req")),
        out_specs=(P("req", "blk", None), P("req", None, "blk"), P("req", None, None)),
        check_vma=False,
    )
```

```python
import functools
import math

import jax
import jax.numpy as jnp
import numpy as np
from jax import lax
from jax.experimental import pallas as pl
from jax.experimental.pallas import tpu as pltpu
from jax.sharding import PartitionSpec as P

HEADS = 16
FEAT = 16
CONV = 3

GROUP = 4
SYM = 160
LANES = 128
REST = SYM - LANES
EDGE, KEYS = 25, 27
INFO = 31
LOCAL = HEADS // GROUP // 2
ORDER = (0, 3, 2, 1)
RETURN = (0, 3, 1, 2)
f32 = jnp.float32
bf16 = jnp.bfloat16
NT = (((1,), (1,)), ((), ()))
NN = (((1,), (0,)), ((), ()))


def dot(a, b, dims=NN):
    return lax.dot_general(a, b, dims, preferred_element_type=f32)


def iota(shape, axis):
    return lax.broadcasted_iota(jnp.int32, shape, axis)


def symmetric(y, scale_square):
    twice = jnp.concatenate([y, y], 0)
    rows = [y * y * scale_square] + [y * twice[o : o + FEAT] for o in range(1, 8)]
    rest = jnp.where(iota((8, y.shape[1]), 0) == 0, 1.0, 0.0)
    return jnp.concatenate(rows + [y, y[:8] * y[8:], rest], 0)


def call(kernel, outs, scratch, limit, flops, moved, args, spaces=(), after=()):
    vmem = pl.BlockSpec(memory_space=pltpu.VMEM)
    given = [pl.BlockSpec(memory_space=space) for space in spaces]
    if after:
        body, plain = kernel, len(args)

        def kernel(*refs):
            body(*refs[:plain], *refs[plain + len(after) :])

    return pl.pallas_call(
        kernel,
        out_shape=[jax.ShapeDtypeStruct(shape, dtype) for shape, dtype in outs],
        in_specs=given
        + [vmem] * (len(args) - len(given))
        + [pl.BlockSpec(memory_space=pl.ANY)] * len(after),
        out_specs=[vmem] * len(outs),
        scratch_shapes=scratch,
        compiler_params=pltpu.CompilerParams(vmem_limit_bytes=int(limit * 2**20)),
        cost_estimate=pl.CostEstimate(flops=flops, bytes_accessed=moved, transcendentals=0),
    )(*args, *after)


TILES = (384, 512)
TILES_B = (896,)


def key_sums(keys):
    keyed, rows = keys.shape
    gram = dot(keys, keys, NT)
    same = iota((keyed, keyed), 0) // FEAT == iota((keyed, keyed), 1) // FEAT
    entry, lane = iota((FEAT, keyed), 0), iota((FEAT, keyed), 1)
    pick = (lax.rem(lane, FEAT) == entry).astype(bf16)
    folded = dot(pick, jnp.where(same, gram, 0.0).astype(bf16))
    plain = dot(jnp.ones((8, rows), bf16), keys, NT)
    mirror = lax.rem(entry - lax.rem(lane, FEAT) + FEAT, FEAT) == 9
    return jnp.where(mirror, plain[0:1], folded).astype(bf16)


def project_kernel(half, *refs):
    x, wq, wk, wv = refs[:4]
    refs = refs[4:]
    if half:
        length, early, o0, o1, o2, o3 = refs[:6]
        refs = refs[6:]
    else:
        o0, o1, o2, o3, early = refs[:5]
        refs = refs[5:]
    rows = x.shape[1]
    width = wv.shape[1] // 2
    keyed = wq.shape[1] // 2
    place = lax.axis_index("blk")
    mine = lax.rem(place, GROUP)
    slab = width // GROUP
    if half:
        vt, qkt = refs
        inputs = x[0]
        both = jnp.concatenate([wk[:, keyed:], wq[:, keyed:]], 1)
        qkt[...] = dot(inputs, both).T.astype(bf16)
        at = 0
        for tile in TILES_B:
            weights = wv[:, width + at : width + at + tile]
            vt[at : at + tile, :] = dot(inputs, weights).T.astype(bf16)
            at += tile
    else:
        vt, qkt, x_v, wqk_v, wv_v, sems = refs
        first, second = pl.ds(0, keyed), pl.ds(keyed, keyed)
        needed = [
            pltpu.make_async_copy(x.at[0], x_v, sems.at[0]),
            pltpu.make_async_copy(wk.at[:, first], wqk_v.at[:, first], sems.at[1]),
            pltpu.make_async_copy(wq.at[:, first], wqk_v.at[:, second], sems.at[2]),
        ]
        copies, at = [], 0
        for j, tile in enumerate(TILES):
            cut = pl.ds(at, tile)
            copies.append(pltpu.make_async_copy(wv.at[:, cut], wv_v.at[:, cut], sems.at[3 + j]))
            at += tile
        for copy in (*needed, *copies):
            copy.start()
        for copy in needed:
            copy.wait()
        inputs = x_v[...]
        qkt[...] = dot(inputs, wqk_v[...]).T.astype(bf16)
        at = 0
        for tile, copy in zip(TILES, copies):
            copy.wait()
            vt[at : at + tile, :] = dot(inputs, wv_v[:, at : at + tile]).T.astype(bf16)
            at += tile
    part = keyed // GROUP
    for s, out in zip(ORDER, (o0, o1, o2, o3)):
        dest = mine ^ s
        out[0:slab, :] = vt[pl.ds(pl.multiple_of(slab * dest, 32), slab), :]
        for base, at in ((0, slab), (keyed, slab + part)):
            start = pl.multiple_of(base + part * dest, 32)
            out[at : at + part, :] = qkt[pl.ds(start, part), :]
    if not half:
        early[...] = qkt[0:keyed, :]
        return
    alive = place * rows + iota((1, rows), 1) < length[...]
    alive = jnp.where(alive, 1.0, 0.0).astype(bf16)
    sums = [key_sums(early[...] * alive), key_sums(qkt[0:keyed, :] * alive)]
    for out in (o0, o1, o2, o3):
        out[slab + 2 * part :, :] = jnp.concatenate(sums, 0)


def project(half, x, wq, wk, wv, *others):
    _, rows, width = x.shape
    keyed = wq.shape[1]
    total = (width + 2 * keyed) // GROUP // 2 + (2 * FEAT if half else 0)
    outs = [((total, rows), bf16)] * GROUP
    scratch = [pltpu.VMEM((width // 2, rows), bf16), pltpu.VMEM((keyed, rows), bf16)]
    if not half:
        outs.append(((keyed // 2, rows), bf16))
        scratch += [
            pltpu.VMEM((rows, width), bf16),
            pltpu.VMEM((width, keyed), bf16),
            pltpu.VMEM((width, width // 2), bf16),
            pltpu.SemaphoreType.DMA((3 + len(TILES),)),
        ]
    flops = rows * width * (width + 2 * keyed)
    kernel = functools.partial(project_kernel, half)
    limit = LIMIT_B if half else LIMIT_A
    args = [x, wq, wk, wv, *others]
    return call(kernel, outs, scratch, limit, flops, flops // rows, args, [] if half else [pltpu.HBM] * 4)


LIMIT_A = 53.6
LIMIT_B = 16


def own_taps(conv, mine, taps, taps_v):
    half = conv.shape[1] // 2
    slab = half // GROUP
    wide = taps_v.shape[0]
    start = jnp.minimum(slab * mine // LANES * LANES, half - wide)
    inside = pl.multiple_of(slab * mine - start, 32)
    for h in range(2):
        cut = conv[:, pl.ds(pl.multiple_of(half * h + start, LANES), wide)]
        padded = jnp.concatenate([cut, jnp.zeros((8 - CONV, wide), f32)], 0)
        for j in range(wide // LANES):
            rows = slice(j * LANES, (j + 1) * LANES)
            taps_v[rows, :] = padded[:, rows].T
        taps[h * slab : (h + 1) * slab, :] = taps_v[pl.ds(inside, slab), :]


def state_kernel(half, *refs):
    length, p0, p1, p2, p3 = refs[:5]
    if half:
        taps, aug, qk, state, held = refs[5:]
    else:
        conv, aug, qk, state, taps, held, taps_v = refs[5:]
        own_taps(conv, lax.rem(lax.axis_index("blk"), GROUP), taps, taps_v)
    rows = p0.shape[1]
    place = lax.axis_index("blk")
    mine, group = lax.rem(place, GROUP), place // GROUP
    kept = held.shape[1]
    size = kept // LOCAL - 2 * FEAT
    values = LOCAL * size
    tokens = GROUP * rows
    for s, ref in zip(ORDER, (p0, p1, p2, p3)):
        held[mine ^ s] = ref[0:kept, :]
    if half:
        sums = p0[kept:, :].astype(f32) + p1[kept:, :].astype(f32)
        sums += p2[kept:, :].astype(f32) + p3[kept:, :].astype(f32)
        state[LOCAL * (size + REST) :, :] = sums.astype(bf16)
    for b in range(GROUP):
        qk[:, b * rows : (b + 1) * rows] = held[b, values:, :]
    alive = (group * tokens + iota((1, tokens), 1) < length[...]).astype(f32)
    token = iota((FEAT, tokens), 1)
    row = iota((FEAT, tokens), 0)
    marks = (row == 0) | ((row == 1) & (token == 0)) | ((row == 2) & (token == 1))
    marks = jnp.where(marks, alive, 0.0).astype(bf16)
    lane = iota((size, rows), 1)
    last = iota((REST, rows), 0)
    ends = iota((REST, rows), 1)
    ends = ((last == EDGE) & (ends == rows - 1)) | ((last == EDGE + 1) & (ends == rows - 2))
    ends = ends.astype(bf16)
    step = size + REST
    for h in range(LOCAL):
        cut = slice(h * size, (h + 1) * size)
        first = (half * LOCAL + h) * size
        tap = taps[first : first + size, :]
        tap = [jnp.broadcast_to(tap[:, t : t + 1], (size, rows)) for t in range(CONV)]
        before = [jnp.zeros((size, rows), f32)] * 2
        pieces = []
        for b in range(GROUP):
            now = held[b, cut, :].astype(f32)
            rolled = [pltpu.roll(now, 1, 1), pltpu.roll(now, 2, 1)]
            one = jnp.where(lane < 1, before[0], rolled[0])
            two = jnp.where(lane < 2, before[1], rolled[1])
            before = rolled
            mixed = tap[0] * now + tap[1] * one + tap[2] * two
            live = alive[:, b * rows : (b + 1) * rows]
            pieces.append(jnp.where(live > 0, mixed, 0.0).astype(bf16))
        aug_h = jnp.concatenate([jnp.concatenate(pieces, 1), marks], 0)
        aug[h] = aug_h
        y = qk[h * FEAT : (h + 1) * FEAT, :].astype(f32) * FEAT ** (-0.25)
        feats = symmetric(y, 1.0).astype(bf16)
        own = dot(aug_h, feats, NT)
        keys = pltpu.roll(own[size : size + 8, :LANES], KEYS % 8, 0)
        keys = jnp.concatenate([jnp.zeros((KEYS // 8 * 8, LANES), f32), keys], 0)
        edge = dot(ends, held[GROUP - 1, h * size : h * size + LANES, :], NT)
        rest = own[:, LANES:].T + edge + keys
        state[h * step : h * step + size, :] = own[:size, :LANES].astype(bf16)
        state[h * step + size : (h + 1) * step, :] = rest.astype(bf16)


def group_state(half, length, payloads, taps, after):
    total, rows = payloads[0].shape
    tokens = GROUP * rows
    extra = 2 * FEAT if half else 0
    outs = [
        ((LOCAL, LANES, tokens), bf16),
        ((2 * LOCAL * FEAT, tokens), bf16),
        (((total - extra) // LOCAL * LOCAL + extra, LANES), bf16),
    ]
    scratch = [pltpu.VMEM((GROUP, total - extra, rows), bf16)]
    if not half:
        slab = taps.shape[1] // GROUP
        outs.append(((slab, 8), f32))
        scratch.append(pltpu.VMEM(((slab // 2 // LANES + 2) * LANES, 8), f32))
    kernel = functools.partial(state_kernel, half)
    args = [length, *payloads, taps]
    return call(kernel, outs, scratch, 32, 100_000_000, 1_000_000, args, after=after)


def local_kernel(aug, qk, num):
    _, _, tokens = aug.shape
    keyed = LOCAL * FEAT
    half = tokens // 2
    keys = qk[0:keyed, :].astype(f32).T.astype(bf16)
    queries = qk[keyed:, :]
    head = iota((keyed, tokens), 0) // FEAT
    causal = iota((half, half), 0) <= iota((half, half), 1)

    def scores(d):
        return 1.0 + d * (0.25 + d * 0.03125)

    for h in range(LOCAL):
        only = jnp.where(head == h, queries, jnp.zeros_like(queries))
        first = scores(dot(keys[:half], only[:, :half]))
        first = jnp.where(causal, first, 0.0).astype(bf16)
        num[h, :, 0:half] = dot(aug[h, :, 0:half], first)
        lower = scores(dot(keys[half:], only[:, half:]))
        lower = jnp.where(causal, lower, 0.0).astype(bf16)
        upper = scores(dot(keys[:half], only[:, half:])).astype(bf16)
        num[h, :, half:] = dot(aug[h, :, 0:half], upper) + dot(aug[h, :, half:], lower)


def local_part(aug, qk, flops, after):
    _, _, tokens = aug.shape
    return call(local_kernel, [(aug.shape, f32)], [], 32, flops, 1000, [aug, qk], after=after)[0]


def finish_kernel(half, *refs):
    if half:
        slot, *refs = refs
    length, num, own, got, qk, taps = refs[:6]
    refs = refs[6:]
    if half:
        other, *firsts = refs[:5]
        refs = refs[5:]
    r0, r1, r2, r3, route, scr = refs
    _, _, tokens = num.shape
    rows = tokens // GROUP
    size = taps.shape[0] // 2 // LOCAL
    keyed = LOCAL * FEAT
    place = lax.axis_index("blk")
    mine, group = lax.rem(place, GROUP), place // GROUP
    upper = group == 1
    weight = jnp.where(upper, 1.0, 0.0)
    alive = group * tokens + iota((1, tokens), 1) < length[...]
    first = (iota((size, LANES), 1) == 0) & upper
    aux = iota((LANES - size, SYM), 0)
    step = size + REST

    def whole(ref, h):
        rest = ref[h * step + size : (h + 1) * step, :].astype(f32)
        tail = [rest[KEYS : KEYS + 3], jnp.zeros((LANES - size - 3, LANES), f32)]
        main = [ref[h * step : h * step + size, :].astype(f32), *tail]
        return jnp.concatenate([jnp.concatenate(main, 0), rest.T], 1)

    finals = []
    for h in range(LOCAL):
        here, there = whole(own, h), whole(got, h)
        low = jnp.where(upper, there, here)
        high = jnp.where(upper, here, there)
        at = (half * LOCAL + h) * size
        tap = taps[at : at + size, :]
        last, second = low[:size, 153:154], low[:size, 154:155]
        change0 = tap[:, 1:2] * last + tap[:, 2:3] * second
        change1 = tap[:, 2:3] * last
        key0, key1 = high[size + 1 : size + 2, :], high[size + 2 : size + 3, :]
        body = low[:size] + change0 * key0 + change1 * key1
        tail = jnp.where(aux == 2, key1, low[size:])
        prior = jnp.concatenate([body, tail], 0)
        finals.append(jnp.concatenate([body + high[:size], low[size:] + high[size:]], 0))
        y = qk[keyed + h * FEAT : keyed + (h + 1) * FEAT, :].astype(f32) * FEAT ** (-0.25)
        feats = symmetric(y, 0.5).astype(bf16)
        all_num = num[h] + weight * dot(prior.astype(bf16), feats)
        den = jnp.where(alive, all_num[size : size + 1, :], 1.0)
        inverse = jnp.where(alive, 1.0 / den, 0.0)
        top = all_num[:size]
        extra = all_num[size + 2 : size + 3, 0:1]
        edge = top[:, :LANES] - jnp.where(first, change1 * extra, 0.0)
        top = jnp.concatenate([edge, top[:, LANES:]], 1)
        result = (top * inverse).astype(bf16)
        for b in range(GROUP):
            scr[b, h * size : (h + 1) * size, :] = result[:, b * rows : (b + 1) * rows]
    for j, (s, out) in enumerate(zip(RETURN, (r0, r1, r2, r3))):
        if half:
            out[0 : LOCAL * size, :] = firsts[j][...]
        out[half * LOCAL * size :, :] = scr[mine ^ s]
    if not half:
        for c in range(LOCAL):
            route[c * step : c * step + size, :] = finals[c][:size, :LANES].astype(bf16)
            route[c * step + size : (c + 1) * step, :] = finals[c][:, LANES:].T.astype(bf16)
        return
    count = length[...]
    for c in range(LOCAL):
        cut = slice(c * step, c * step + size)
        final = jnp.where(upper, finals[c][:size, :LANES], other[cut, :].astype(f32))
        route[cut, :] = final.astype(bf16)
        cut = slice(c * step + size, (c + 1) * step)
        final = jnp.where(upper, finals[c][:, LANES:].T, other[cut, :].astype(f32))
        if c == 0:
            row, lane = iota(final.shape, 0), iota(final.shape, 1)
            values = (slot[0], lax.shift_right_logical(count, 8), count & 255)
            for at, value in enumerate(values):
                final = jnp.where((row == INFO) & (lane == at), value.astype(f32), final)
        route[cut, :] = final.astype(bf16)
    sums = own[LOCAL * step :, :].astype(f32) + got[LOCAL * step :, :].astype(f32)
    route[LOCAL * step :, :] = sums.astype(bf16)


def finish(half, length, slot, num, own, got, qk, taps, other):
    _, _, tokens = num.shape
    rows = tokens // GROUP
    width = taps.shape[0] // 2
    outs = [(((1 + half) * width, rows), bf16)] * GROUP + [(own.shape, bf16)]
    scratch = [pltpu.VMEM((GROUP, width, rows), bf16)]
    args = [slot] * half + [length, num, own, got, qk, taps] + other
    kernel = functools.partial(finish_kernel, half)
    return call(kernel, outs, scratch, 32, 50_000_000, 20_000_000, args, [pltpu.SMEM] * half)


def place_kernel(r0, r1, r2, r3, mixed, scr, turned, sems):
    width = scr.shape[0]
    mine = lax.rem(lax.axis_index("blk"), GROUP)
    half = width // 2
    slab = half // GROUP
    for s, ref in zip(RETURN, (r0, r1, r2, r3)):
        start = pl.multiple_of(slab * (mine ^ s), 32)
        scr[pl.ds(start, slab), :] = ref[0:slab, :]
        scr[pl.ds(pl.multiple_of(half + start, 32), slab), :] = ref[slab:, :]
    copies = []
    for j in range(width // LANES):
        cut = slice(j * LANES, (j + 1) * LANES)
        turned[:, cut] = scr[cut, :].T
        if j % 2:
            cut = pl.ds((j - 1) * LANES, 2 * LANES)
            copies.append(
                pltpu.make_async_copy(turned.at[:, cut], mixed.at[0, :, cut], sems.at[j // 2])
            )
            copies[-1].start()
    for copy in copies:
        copy.wait()


def place_tokens(results, after):
    part, rows = results[0].shape
    width = part * GROUP

    def kernel(*refs):
        place_kernel(*refs[:GROUP], *refs[GROUP + len(after) :])

    vmem, hbm = (pl.BlockSpec(memory_space=space) for space in (pltpu.VMEM, pl.ANY))
    return pl.pallas_call(
        kernel,
        out_shape=jax.ShapeDtypeStruct((1, rows, width), bf16),
        in_specs=[vmem] * GROUP + [hbm] * len(after),
        out_specs=hbm,
        scratch_shapes=[
            pltpu.VMEM((width, rows), bf16),
            pltpu.VMEM((rows, width), bf16),
            pltpu.SemaphoreType.DMA((width // LANES // 2,)),
        ],
        compiler_params=pltpu.CompilerParams(vmem_limit_bytes=32 * 2**20),
        cost_estimate=pl.CostEstimate(flops=1000, bytes_accessed=1_000_000, transcendentals=0),
    )(*results, *after)


ROUTE = (2, 1)


def hand_on_kernel(own, got, out):
    other = (lax.axis_index("req") ^ ROUTE[1]).astype(f32)
    kept = jnp.zeros(out.shape, f32)
    step = (own.shape[0] - 2 * FEAT) // LOCAL
    for ref in (own, got):
        here = ref[step - FEAT : step, :].astype(f32)[INFO % FEAT :, 0:1] == other
        kept += jnp.where(here, ref[...].astype(f32), 0.0)
    out[...] = kept.astype(bf16)


def hand_on(own, got, after):
    args = [own, got]
    return call(hand_on_kernel, [(own.shape, bf16)], [], 32, 1000, 300_000, args, after=after)[0]


def expand_kernel(c0, c1, c2, spread, state, norm):
    me = lax.axis_index("req").astype(f32)
    kept = jnp.zeros(c0.shape, f32)
    step = (c0.shape[0] - 2 * FEAT) // LOCAL
    at = step - REST + INFO
    for ref in (c0, c1, c2):
        here = ref[step - FEAT : step, :].astype(f32)[INFO % FEAT :, 0:1] == me
        kept += jnp.where(here, ref[...].astype(f32), 0.0)
    size = state.shape[2] // LOCAL
    expand = state.shape[0]
    scale = jnp.where(iota((expand, size), 0) > FEAT, math.sqrt(0.5), 1.0)
    wholes = []
    for c in range(LOCAL):
        main = kept[c * step : c * step + size].astype(bf16)
        rest = kept[c * step + size : (c + 1) * step].astype(bf16)
        whole = dot(spread[:, :LANES], main, NT) + dot(spread[:, LANES:], rest)[:, :size]
        wholes.append(whole * scale)
    state[...] = jnp.concatenate(wholes, 1).reshape(state.shape)
    sums = kept[LOCAL * step :]
    keyed = HEADS * FEAT
    sums = jnp.concatenate([sums[:FEAT], sums[FEAT:]], 1)
    plain = jnp.concatenate([sums[9:], sums[:9]], 0) * FEAT ** (-0.25)
    products = sums * FEAT ** (-0.5)
    b = iota((FEAT, keyed), 0)
    entry = lax.rem(iota((FEAT, keyed), 1), FEAT)
    big = [jnp.where(entry == b, plain, 0.0)]
    for a in range(FEAT):
        mirror = b == (a + 9) % FEAT
        row = jnp.where(mirror, products[a : a + 1], products)
        big.append(jnp.where(entry == jnp.where(mirror, b, a), row, 0.0))
    big = jnp.concatenate(big, 0)
    gather = (iota((keyed, HEADS), 0) // FEAT == iota((keyed, HEADS), 1)).astype(bf16)
    rest = dot(big.astype(bf16), gather)
    rest = rest * jnp.where(iota(rest.shape, 0) >= FEAT, math.sqrt(0.5), 1.0)
    info = kept[at : at + 1]
    count = info[:, 1:2] * 256.0 + info[:, 2:3]
    norm[0] = jnp.concatenate([jnp.broadcast_to(count, (1, HEADS)), rest], 0).T


def spread_rows():
    table = np.zeros((1 + FEAT + FEAT * FEAT, SYM), np.float32)
    table[0, 152] = 1
    for a in range(FEAT):
        table[1 + a, 128 + a] = 1
        for b in range(FEAT):
            o = (b - a) % FEAT
            at = o * FEAT + a if o < 8 else (144 + min(a, b) if o == 8 else (FEAT - o) * FEAT + b)
            table[1 + FEAT + a * FEAT + b, at] = 1
    return table


def expand_state(candidates, columns):
    spread = jnp.asarray(spread_rows(), bf16)
    expand = spread.shape[0]
    outs = [((expand, 1, columns), f32), ((1, HEADS, expand), f32)]
    return call(expand_kernel, outs, [], 32, 40_000_000, 1_000_000, [*candidates, spread])


def across(arrays, order):
    return [swap(array, "blk", s) if s else array for s, array in zip(order, arrays)]


def swap(array, axis, by):
    return lax.ppermute(array, axis, [(i, i ^ by) for i in range(lax.axis_size(axis))])


def two_groups(
    tokens_in, query_weight, key_weight, value_weight, conv_weight, prompt_lengths, decode_map
):
    width = tokens_in.shape[2]
    given = (tokens_in, query_weight, key_weight, value_weight)
    length, slot = prompt_lengths.reshape(1, 1), decode_map
    *parts, early = project(0, *given)
    sent = [across(parts, ORDER)]
    parts = project(1, *given, length, early)
    sent.append(across(parts, ORDER))
    *first, taps = group_state(0, length, sent[0], conv_weight, [])
    second = group_state(1, length, sent[1], taps, [first[2]])
    got = [swap(held[2], "blk", GROUP) for held in (first, second)]
    aug, qk, own = first
    num = local_part(aug, qk, 1000, [second[2]])
    early = finish(0, length, slot, num, own, got[0], qk, taps, [])
    aug, qk, own = second
    num = local_part(aug, qk, 5_000_000_000, [early[4]])
    *parts, total = finish(1, length, slot, num, own, got[1], qk, taps, [early[4], *early[:4]])
    results = across(parts, RETURN)
    beside = swap(total, "req", ROUTE[0])
    theirs = swap(hand_on(total, beside, []), "req", ROUTE[1])
    state, norm = expand_state([total, beside, theirs], width // lax.axis_size("blk"))
    mixed = place_tokens(results, [theirs])
    return (mixed, jnp.swapaxes(state, 0, 1), jnp.swapaxes(norm, 1, 2))


def from_behind(array, axis, by):
    devices = lax.axis_size(axis)
    pairs = [(i, i + by) for i in range(devices) if 0 <= i + by < devices]
    return lax.ppermute(array, axis, pairs)


def entering(part, axis, combine, identity):
    place = lax.axis_index(axis)
    gathered = jax.tree.map(lambda a: lax.all_gather(a, axis), part)
    state = jax.tree.map(lambda a, e: jnp.zeros_like(a) + jnp.asarray(e, a.dtype), part, identity)

    def one(turn, state):
        return combine(
            state, jax.tree.map(lambda a: lax.dynamic_index_in_dim(a, turn, 0, False), gathered)
        )

    return lax.fori_loop(0, place, one, state)


def features_last(x):
    half = x * FEAT ** (-0.25)
    outer = half[:, :, None, :] * half[:, None, :, :]
    flat = outer.reshape(half.shape[0], FEAT * FEAT, half.shape[2]) * math.sqrt(0.5)
    ones = jnp.ones((half.shape[0], 1, half.shape[2]), jnp.float32)
    return jnp.concatenate([ones, half, flat], 1)


def add_pair(earlier, later):
    return (earlier[0] + later[0], earlier[1] + later[1])


def route_slot(pair, decode_map):
    groups = lax.axis_size("req")
    slots = (jnp.arange(groups, dtype=jnp.int32) == decode_map[0]).astype(jnp.float32)
    sent = (slots[:, None, None] * pair[0][None], slots[:, None, None] * pair[1][None])
    got = (
        lax.all_to_all(sent[0], "req", split_axis=0, concat_axis=0, tiled=True),
        lax.all_to_all(sent[1], "req", split_axis=0, concat_axis=0, tiled=True),
    )
    return (jnp.sum(got[0], 0), jnp.sum(got[1], 0))


def reduce_blocks(pair):
    return (
        lax.psum_scatter(pair[0], "blk", scatter_dimension=1, tiled=True),
        lax.psum_scatter(pair[1], "blk", scatter_dimension=1, tiled=True),
    )


def any_blocks(
    tokens_in, query_weight, key_weight, value_weight, conv_weight, prompt_lengths, decode_map
):
    rows = tokens_in.shape[1]
    width = tokens_in.shape[2]
    blocks = lax.axis_size("blk")
    head_size = width // HEADS
    hi = lax.Precision.HIGHEST
    inputs = tokens_in[0]
    queries = jnp.einsum(
        "dk,td->kt", query_weight, inputs, preferred_element_type=jnp.float32
    ).reshape(HEADS, FEAT, rows)
    keys = jnp.einsum("dk,td->kt", key_weight, inputs, preferred_element_type=jnp.float32).reshape(
        HEADS, FEAT, rows
    )
    values = jnp.dot(inputs, value_weight, preferred_element_type=jnp.float32).astype(jnp.bfloat16)
    earlier = from_behind(values[rows - (CONV - 1) :], "blk", 1)
    extended = jnp.concatenate([earlier, values], 0).astype(jnp.float32)
    conv = jnp.zeros((rows, width), jnp.float32)
    for tap in range(CONV):
        conv = conv + conv_weight[tap][None, :] * extended[CONV - 1 - tap : CONV - 1 - tap + rows]
    conv_t = conv.astype(jnp.bfloat16).astype(jnp.float32).T.reshape(HEADS, head_size, rows)
    start = lax.axis_index("blk") * rows
    live = (start + jnp.arange(rows, dtype=jnp.int32) < prompt_lengths[0]).astype(jnp.float32)
    feat_q = features_last(queries)
    feat_k = features_last(keys) * live[None, None, :]
    own_state = jnp.einsum("hft,hct->hfc", feat_k, conv_t, precision=hi)
    own_norm = jnp.sum(feat_k, 2)
    zero_state = jnp.zeros_like(own_state)
    zero_norm = jnp.zeros_like(own_norm)
    prior_state, prior_norm = entering(
        (own_state, own_norm), "blk", add_pair, (zero_state, zero_norm)
    )
    causal = (jnp.arange(rows)[:, None] >= jnp.arange(rows)[None, :]).astype(jnp.float32)
    scores = jnp.einsum("hft,hfs->hts", feat_q, feat_k, precision=hi) * causal[None]
    num = jnp.einsum("hts,hcs->hct", scores, conv_t, precision=hi) + jnp.einsum(
        "hft,hfc->hct", feat_q, prior_state, precision=hi
    )
    den = (
        jnp.sum(scores, -1)
        + jnp.einsum("hft,hf->ht", feat_q, prior_norm, precision=hi)
        + (1.0 - live)[None, :]
    )
    result = jnp.where(live[None, None, :] > 0, num / den[:, None, :], 0.0)
    mixed = result.reshape(width, rows).T.reshape(1, rows, width).astype(jnp.bfloat16)
    state_flat = jnp.transpose(own_state, (1, 0, 2)).reshape(own_state.shape[1], width)
    pair = (state_flat, jnp.tile(own_norm.T, (1, blocks)))
    final = route_slot(reduce_blocks(pair), decode_map)
    return (mixed, final[0][None], final[1][None])


def solution(mesh):
    def on_device(*args):
        rows = args[0].shape[1]
        if mesh.shape["blk"] == 2 * GROUP and mesh.shape["req"] == 4 and rows == LANES:
            return two_groups(*args)
        return any_blocks(*args)

    return jax.shard_map(
        on_device,
        mesh=mesh,
        in_specs=(P("req", "blk", None), P(), P(), P(), P(), P("req"), P("req")),
        out_specs=(P("req", "blk", None), P("req", None, "blk"), P("req", None, None)),
        check_vma=False,
    )
```

```python
import functools
import math

import jax
import jax.numpy as jnp
import numpy as np
from jax import lax
from jax.experimental import pallas as pl
from jax.experimental.pallas import tpu as pltpu
from jax.sharding import PartitionSpec as P

HEADS = 16
FEAT = 16
CONV = 3

GROUP = 4
SYM = 160
LANES = 128
REST = SYM - LANES
EDGE, KEYS = 25, 27
INFO = 31
LOCAL = HEADS // GROUP // 2
ORDER = (0, 3, 2, 1)
RETURN = (0, 3, 1, 2)
f32 = jnp.float32
bf16 = jnp.bfloat16
NT = (((1,), (1,)), ((), ()))
NN = (((1,), (0,)), ((), ()))


def dot(a, b, dims=NN):
    return lax.dot_general(a, b, dims, preferred_element_type=f32)


def iota(shape, axis):
    return lax.broadcasted_iota(jnp.int32, shape, axis)


def symmetric(y, scale_square):
    twice = jnp.concatenate([y, y], 0)
    rows = [y * y * scale_square] + [y * twice[o : o + FEAT] for o in range(1, 8)]
    rest = jnp.where(iota((8, y.shape[1]), 0) == 0, 1.0, 0.0)
    return jnp.concatenate(rows + [y, y[:8] * y[8:], rest], 0)


def call(kernel, outs, scratch, limit, flops, moved, args, spaces=(), after=()):
    vmem = pl.BlockSpec(memory_space=pltpu.VMEM)
    given = [pl.BlockSpec(memory_space=space) for space in spaces]
    if after:
        body, plain = kernel, len(args)

        def kernel(*refs):
            body(*refs[:plain], *refs[plain + len(after) :])

    return pl.pallas_call(
        kernel,
        out_shape=[jax.ShapeDtypeStruct(shape, dtype) for shape, dtype in outs],
        in_specs=given
        + [vmem] * (len(args) - len(given))
        + [pl.BlockSpec(memory_space=pl.ANY)] * len(after),
        out_specs=[vmem] * len(outs),
        scratch_shapes=scratch,
        compiler_params=pltpu.CompilerParams(vmem_limit_bytes=int(limit * 2**20)),
        cost_estimate=pl.CostEstimate(flops=flops, bytes_accessed=moved, transcendentals=0),
    )(*args, *after)


TILES = (384, 512)
TILES_B = (896,)


def key_sums(keys):
    keyed, rows = keys.shape
    gram = dot(keys, keys, NT)
    same = iota((keyed, keyed), 0) // FEAT == iota((keyed, keyed), 1) // FEAT
    entry, lane = iota((FEAT, keyed), 0), iota((FEAT, keyed), 1)
    pick = (lax.rem(lane, FEAT) == entry).astype(bf16)
    folded = dot(pick, jnp.where(same, gram, 0.0).astype(bf16))
    plain = dot(jnp.ones((8, rows), bf16), keys, NT)
    mirror = lax.rem(entry - lax.rem(lane, FEAT) + FEAT, FEAT) == 9
    return jnp.where(mirror, plain[0:1], folded).astype(bf16)


def project_kernel(half, *refs):
    x, wq, wk, wv = refs[:4]
    refs = refs[4:]
    if half:
        length, early, conv, o0, o1, o2, o3, taps = refs[:8]
        refs = refs[8:]
    else:
        o0, o1, o2, o3, early, x_v = refs[:6]
        refs = refs[6:]
    rows = early.shape[1]
    width = wv.shape[1] // 2
    keyed = wq.shape[1] // 2
    place = lax.axis_index("blk")
    mine = lax.rem(place, GROUP)
    slab = width // GROUP
    if half:
        vt, qkt, taps_v = refs
        inputs = x[...]
        own_taps(conv, mine, taps, taps_v)
        both = jnp.concatenate([wk[:, keyed:], wq[:, keyed:]], 1)
        qkt[...] = dot(inputs, both).T.astype(bf16)
        at = 0
        for tile in TILES_B:
            weights = wv[:, width + at : width + at + tile]
            vt[at : at + tile, :] = dot(inputs, weights).T.astype(bf16)
            at += tile
    else:
        vt, qkt, wqk_v, wv_v, sems = refs
        first, second = pl.ds(0, keyed), pl.ds(keyed, keyed)
        needed = [
            pltpu.make_async_copy(x.at[0], x_v, sems.at[0]),
            pltpu.make_async_copy(wk.at[:, first], wqk_v.at[:, first], sems.at[1]),
            pltpu.make_async_copy(wq.at[:, first], wqk_v.at[:, second], sems.at[2]),
        ]
        copies, at = [], 0
        for j, tile in enumerate(TILES):
            cut = pl.ds(at, tile)
            copies.append(pltpu.make_async_copy(wv.at[:, cut], wv_v.at[:, cut], sems.at[3 + j]))
            at += tile
        for copy in (*needed, *copies):
            copy.start()
        for copy in needed:
            copy.wait()
        inputs = x_v[...]
        qkt[...] = dot(inputs, wqk_v[...]).T.astype(bf16)
        at = 0
        for tile, copy in zip(TILES, copies):
            copy.wait()
            vt[at : at + tile, :] = dot(inputs, wv_v[:, at : at + tile]).T.astype(bf16)
            at += tile
    part = keyed // GROUP
    for s, out in zip(ORDER, (o0, o1, o2, o3)):
        dest = mine ^ s
        out[0:slab, :] = vt[pl.ds(pl.multiple_of(slab * dest, 32), slab), :]
        for base, at in ((0, slab), (keyed, slab + part)):
            start = pl.multiple_of(base + part * dest, 32)
            out[at : at + part, :] = qkt[pl.ds(start, part), :]
    if not half:
        early[...] = qkt[0:keyed, :]
        return
    alive = place * rows + iota((1, rows), 1) < length[...]
    alive = jnp.where(alive, 1.0, 0.0).astype(bf16)
    sums = [key_sums(early[...] * alive), key_sums(qkt[0:keyed, :] * alive)]
    for out in (o0, o1, o2, o3):
        out[slab + 2 * part :, :] = jnp.concatenate(sums, 0)


def project(half, x, wq, wk, wv, *others):
    rows, width = x.shape[-2:]
    keyed = wq.shape[1]
    total = (width + 2 * keyed) // GROUP // 2 + (2 * FEAT if half else 0)
    outs = [((total, rows), bf16)] * GROUP
    scratch = [pltpu.VMEM((width // 2, rows), bf16), pltpu.VMEM((keyed, rows), bf16)]
    if half:
        slab = width // GROUP
        outs.append(((slab, 8), f32))
        scratch.append(pltpu.VMEM(((slab // 2 // LANES + 2) * LANES, 8), f32))
    else:
        outs += [((keyed // 2, rows), bf16), ((rows, width), bf16)]
        scratch += [
            pltpu.VMEM((width, keyed), bf16),
            pltpu.VMEM((width, width // 2), bf16),
            pltpu.SemaphoreType.DMA((3 + len(TILES),)),
        ]
    flops = rows * width * (width + 2 * keyed)
    kernel = functools.partial(project_kernel, half)
    limit = LIMIT_B if half else LIMIT_A
    args = [x, wq, wk, wv, *others]
    return call(kernel, outs, scratch, limit, flops, flops // rows, args, [] if half else [pltpu.HBM] * 4)


LIMIT_A = 53.1
LIMIT_B = 16


def own_taps(conv, mine, taps, taps_v):
    half = conv.shape[1] // 2
    slab = half // GROUP
    wide = taps_v.shape[0]
    start = jnp.minimum(slab * mine // LANES * LANES, half - wide)
    inside = pl.multiple_of(slab * mine - start, 32)
    for h in range(2):
        cut = conv[:, pl.ds(pl.multiple_of(half * h + start, LANES), wide)]
        padded = jnp.concatenate([cut, jnp.zeros((8 - CONV, wide), f32)], 0)
        for j in range(wide // LANES):
            rows = slice(j * LANES, (j + 1) * LANES)
            taps_v[rows, :] = padded[:, rows].T
        taps[h * slab : (h + 1) * slab, :] = taps_v[pl.ds(inside, slab), :]


def state_kernel(half, *refs):
    length, p0, p1, p2, p3 = refs[:5]
    taps, aug, qk, state, held = refs[5:]
    rows = p0.shape[1]
    place = lax.axis_index("blk")
    mine, group = lax.rem(place, GROUP), place // GROUP
    kept = held.shape[1]
    size = kept // LOCAL - 2 * FEAT
    values = LOCAL * size
    tokens = GROUP * rows
    for s, ref in zip(ORDER, (p0, p1, p2, p3)):
        held[mine ^ s] = ref[0:kept, :]
    if half:
        sums = p0[kept:, :].astype(f32) + p1[kept:, :].astype(f32)
        sums += p2[kept:, :].astype(f32) + p3[kept:, :].astype(f32)
        state[LOCAL * (size + REST) :, :] = sums.astype(bf16)
    for b in range(GROUP):
        qk[:, b * rows : (b + 1) * rows] = held[b, values:, :]
    alive = (group * tokens + iota((1, tokens), 1) < length[...]).astype(f32)
    token = iota((FEAT, tokens), 1)
    row = iota((FEAT, tokens), 0)
    marks = (row == 0) | ((row == 1) & (token == 0)) | ((row == 2) & (token == 1))
    marks = jnp.where(marks, alive, 0.0).astype(bf16)
    lane = iota((size, rows), 1)
    last = iota((REST, rows), 0)
    ends = iota((REST, rows), 1)
    ends = ((last == EDGE) & (ends == rows - 1)) | ((last == EDGE + 1) & (ends == rows - 2))
    ends = ends.astype(bf16)
    step = size + REST
    for h in range(LOCAL):
        cut = slice(h * size, (h + 1) * size)
        first = (half * LOCAL + h) * size
        tap = taps[first : first + size, :]
        tap = [jnp.broadcast_to(tap[:, t : t + 1], (size, rows)) for t in range(CONV)]
        before = [jnp.zeros((size, rows), f32)] * 2
        pieces = []
        for b in range(GROUP):
            now = held[b, cut, :].astype(f32)
            rolled = [pltpu.roll(now, 1, 1), pltpu.roll(now, 2, 1)]
            one = jnp.where(lane < 1, before[0], rolled[0])
            two = jnp.where(lane < 2, before[1], rolled[1])
            before = rolled
            mixed = tap[0] * now + tap[1] * one + tap[2] * two
            live = alive[:, b * rows : (b + 1) * rows]
            pieces.append(jnp.where(live > 0, mixed, 0.0).astype(bf16))
        aug_h = jnp.concatenate([jnp.concatenate(pieces, 1), marks], 0)
        aug[h] = aug_h
        y = qk[h * FEAT : (h + 1) * FEAT, :].astype(f32) * FEAT ** (-0.25)
        feats = symmetric(y, 1.0).astype(bf16)
        own = dot(aug_h, feats, NT)
        keys = pltpu.roll(own[size : size + 8, :LANES], KEYS % 8, 0)
        keys = jnp.concatenate([jnp.zeros((KEYS // 8 * 8, LANES), f32), keys], 0)
        edge = dot(ends, held[GROUP - 1, h * size : h * size + LANES, :], NT)
        rest = own[:, LANES:].T + edge + keys
        state[h * step : h * step + size, :] = own[:size, :LANES].astype(bf16)
        state[h * step + size : (h + 1) * step, :] = rest.astype(bf16)


def group_state(half, length, payloads, taps, after):
    total, rows = payloads[0].shape
    tokens = GROUP * rows
    extra = 2 * FEAT if half else 0
    outs = [
        ((LOCAL, LANES, tokens), bf16),
        ((2 * LOCAL * FEAT, tokens), bf16),
        (((total - extra) // LOCAL * LOCAL + extra, LANES), bf16),
    ]
    scratch = [pltpu.VMEM((GROUP, total - extra, rows), bf16)]
    kernel = functools.partial(state_kernel, half)
    args = [length, *payloads, taps]
    return call(kernel, outs, scratch, 32, 100_000_000, 1_000_000, args, after=after)


def local_kernel(aug, qk, num):
    _, _, tokens = aug.shape
    keyed = LOCAL * FEAT
    half = tokens // 2
    keys = qk[0:keyed, :].astype(f32).T.astype(bf16)
    queries = qk[keyed:, :]
    head = iota((keyed, tokens), 0) // FEAT
    causal = iota((half, half), 0) <= iota((half, half), 1)

    def scores(d):
        return 1.0 + d * (0.25 + d * 0.03125)

    for h in range(LOCAL):
        only = jnp.where(head == h, queries, jnp.zeros_like(queries))
        first = scores(dot(keys[:half], only[:, :half]))
        first = jnp.where(causal, first, 0.0).astype(bf16)
        num[h, :, 0:half] = dot(aug[h, :, 0:half], first)
        lower = scores(dot(keys[half:], only[:, half:]))
        lower = jnp.where(causal, lower, 0.0).astype(bf16)
        upper = scores(dot(keys[:half], only[:, half:])).astype(bf16)
        num[h, :, half:] = dot(aug[h, :, 0:half], upper) + dot(aug[h, :, half:], lower)


def local_part(aug, qk, flops, after):
    _, _, tokens = aug.shape
    return call(local_kernel, [(aug.shape, f32)], [], 32, flops, 1000, [aug, qk], after=after)[0]


def finish_kernel(half, *refs):
    if half:
        slot, *refs = refs
    length, num, own, got, qk, taps = refs[:6]
    refs = refs[6:]
    if half:
        other, *firsts = refs[:5]
        refs = refs[5:]
    r0, r1, r2, r3, route, scr = refs
    _, _, tokens = num.shape
    rows = tokens // GROUP
    size = taps.shape[0] // 2 // LOCAL
    keyed = LOCAL * FEAT
    place = lax.axis_index("blk")
    mine, group = lax.rem(place, GROUP), place // GROUP
    upper = group == 1
    weight = jnp.where(upper, 1.0, 0.0)
    alive = group * tokens + iota((1, tokens), 1) < length[...]
    first = (iota((size, LANES), 1) == 0) & upper
    aux = iota((LANES - size, SYM), 0)
    step = size + REST

    def whole(ref, h):
        rest = ref[h * step + size : (h + 1) * step, :].astype(f32)
        tail = [rest[KEYS : KEYS + 3], jnp.zeros((LANES - size - 3, LANES), f32)]
        main = [ref[h * step : h * step + size, :].astype(f32), *tail]
        return jnp.concatenate([jnp.concatenate(main, 0), rest.T], 1)

    finals = []
    for h in range(LOCAL):
        here, there = whole(own, h), whole(got, h)
        low = jnp.where(upper, there, here)
        high = jnp.where(upper, here, there)
        at = (half * LOCAL + h) * size
        tap = taps[at : at + size, :]
        last, second = low[:size, 153:154], low[:size, 154:155]
        change0 = tap[:, 1:2] * last + tap[:, 2:3] * second
        change1 = tap[:, 2:3] * last
        key0, key1 = high[size + 1 : size + 2, :], high[size + 2 : size + 3, :]
        body = low[:size] + change0 * key0 + change1 * key1
        tail = jnp.where(aux == 2, key1, low[size:])
        prior = jnp.concatenate([body, tail], 0)
        finals.append(jnp.concatenate([body + high[:size], low[size:] + high[size:]], 0))
        y = qk[keyed + h * FEAT : keyed + (h + 1) * FEAT, :].astype(f32) * FEAT ** (-0.25)
        feats = symmetric(y, 0.5).astype(bf16)
        all_num = num[h] + weight * dot(prior.astype(bf16), feats)
        den = jnp.where(alive, all_num[size : size + 1, :], 1.0)
        inverse = jnp.where(alive, 1.0 / den, 0.0)
        top = all_num[:size]
        extra = all_num[size + 2 : size + 3, 0:1]
        edge = top[:, :LANES] - jnp.where(first, change1 * extra, 0.0)
        top = jnp.concatenate([edge, top[:, LANES:]], 1)
        result = (top * inverse).astype(bf16)
        for b in range(GROUP):
            scr[b, h * size : (h + 1) * size, :] = result[:, b * rows : (b + 1) * rows]
    for j, (s, out) in enumerate(zip(RETURN, (r0, r1, r2, r3))):
        if half:
            out[0 : LOCAL * size, :] = firsts[j][...]
        out[half * LOCAL * size :, :] = scr[mine ^ s]
    if not half:
        for c in range(LOCAL):
            route[c * step : c * step + size, :] = finals[c][:size, :LANES].astype(bf16)
            route[c * step + size : (c + 1) * step, :] = finals[c][:, LANES:].T.astype(bf16)
        return
    count = length[...]
    for c in range(LOCAL):
        cut = slice(c * step, c * step + size)
        final = jnp.where(upper, finals[c][:size, :LANES], other[cut, :].astype(f32))
        route[cut, :] = final.astype(bf16)
        cut = slice(c * step + size, (c + 1) * step)
        final = jnp.where(upper, finals[c][:, LANES:].T, other[cut, :].astype(f32))
        if c == 0:
            row, lane = iota(final.shape, 0), iota(final.shape, 1)
            values = (slot[0], lax.shift_right_logical(count, 8), count & 255)
            for at, value in enumerate(values):
                final = jnp.where((row == INFO) & (lane == at), value.astype(f32), final)
        route[cut, :] = final.astype(bf16)
    sums = own[LOCAL * step :, :].astype(f32) + got[LOCAL * step :, :].astype(f32)
    route[LOCAL * step :, :] = sums.astype(bf16)


def finish(half, length, slot, num, own, got, qk, taps, other):
    _, _, tokens = num.shape
    rows = tokens // GROUP
    width = taps.shape[0] // 2
    outs = [(((1 + half) * width, rows), bf16)] * GROUP + [(own.shape, bf16)]
    scratch = [pltpu.VMEM((GROUP, width, rows), bf16)]
    args = [slot] * half + [length, num, own, got, qk, taps] + other
    kernel = functools.partial(finish_kernel, half)
    return call(kernel, outs, scratch, 32, 50_000_000, 20_000_000, args, [pltpu.SMEM] * half)


def place_kernel(r0, r1, r2, r3, mixed, scr, turned, sems):
    width = scr.shape[0]
    mine = lax.rem(lax.axis_index("blk"), GROUP)
    half = width // 2
    slab = half // GROUP
    for s, ref in zip(RETURN, (r0, r1, r2, r3)):
        start = pl.multiple_of(slab * (mine ^ s), 32)
        scr[pl.ds(start, slab), :] = ref[0:slab, :]
        scr[pl.ds(pl.multiple_of(half + start, 32), slab), :] = ref[slab:, :]
    copies = []
    for j in range(width // LANES):
        cut = slice(j * LANES, (j + 1) * LANES)
        turned[:, cut] = scr[cut, :].T
        if j % 2:
            cut = pl.ds((j - 1) * LANES, 2 * LANES)
            copies.append(
                pltpu.make_async_copy(turned.at[:, cut], mixed.at[0, :, cut], sems.at[j // 2])
            )
            copies[-1].start()
    for copy in copies:
        copy.wait()


def place_tokens(results, after):
    part, rows = results[0].shape
    width = part * GROUP

    def kernel(*refs):
        place_kernel(*refs[:GROUP], *refs[GROUP + len(after) :])

    vmem, hbm = (pl.BlockSpec(memory_space=space) for space in (pltpu.VMEM, pl.ANY))
    return pl.pallas_call(
        kernel,
        out_shape=jax.ShapeDtypeStruct((1, rows, width), bf16),
        in_specs=[vmem] * GROUP + [hbm] * len(after),
        out_specs=hbm,
        scratch_shapes=[
            pltpu.VMEM((width, rows), bf16),
            pltpu.VMEM((rows, width), bf16),
            pltpu.SemaphoreType.DMA((width // LANES // 2,)),
        ],
        compiler_params=pltpu.CompilerParams(vmem_limit_bytes=32 * 2**20),
        cost_estimate=pl.CostEstimate(flops=1000, bytes_accessed=1_000_000, transcendentals=0),
    )(*results, *after)


ROUTE = (2, 1)


def hand_on_kernel(own, got, out):
    other = (lax.axis_index("req") ^ ROUTE[1]).astype(f32)
    kept = jnp.zeros(out.shape, f32)
    step = (own.shape[0] - 2 * FEAT) // LOCAL
    for ref in (own, got):
        here = ref[step - FEAT : step, :].astype(f32)[INFO % FEAT :, 0:1] == other
        kept += jnp.where(here, ref[...].astype(f32), 0.0)
    out[...] = kept.astype(bf16)


def hand_on(own, got, after):
    args = [own, got]
    return call(hand_on_kernel, [(own.shape, bf16)], [], 32, 1000, 300_000, args, after=after)[0]


def expand_kernel(c0, c1, c2, spread, state, norm):
    me = lax.axis_index("req").astype(f32)
    kept = jnp.zeros(c0.shape, f32)
    step = (c0.shape[0] - 2 * FEAT) // LOCAL
    at = step - REST + INFO
    for ref in (c0, c1, c2):
        here = ref[step - FEAT : step, :].astype(f32)[INFO % FEAT :, 0:1] == me
        kept += jnp.where(here, ref[...].astype(f32), 0.0)
    size = state.shape[2] // LOCAL
    expand = state.shape[0]
    scale = jnp.where(iota((expand, size), 0) > FEAT, math.sqrt(0.5), 1.0)
    wholes = []
    for c in range(LOCAL):
        main = kept[c * step : c * step + size].astype(bf16)
        rest = kept[c * step + size : (c + 1) * step].astype(bf16)
        whole = dot(spread[:, :LANES], main, NT) + dot(spread[:, LANES:], rest)[:, :size]
        wholes.append(whole * scale)
    state[...] = jnp.concatenate(wholes, 1).reshape(state.shape)
    sums = kept[LOCAL * step :]
    keyed = HEADS * FEAT
    sums = jnp.concatenate([sums[:FEAT], sums[FEAT:]], 1)
    plain = jnp.concatenate([sums[9:], sums[:9]], 0) * FEAT ** (-0.25)
    products = sums * FEAT ** (-0.5)
    b = iota((FEAT, keyed), 0)
    entry = lax.rem(iota((FEAT, keyed), 1), FEAT)
    big = [jnp.where(entry == b, plain, 0.0)]
    for a in range(FEAT):
        mirror = b == (a + 9) % FEAT
        row = jnp.where(mirror, products[a : a + 1], products)
        big.append(jnp.where(entry == jnp.where(mirror, b, a), row, 0.0))
    big = jnp.concatenate(big, 0)
    gather = (iota((keyed, HEADS), 0) // FEAT == iota((keyed, HEADS), 1)).astype(bf16)
    rest = dot(big.astype(bf16), gather)
    rest = rest * jnp.where(iota(rest.shape, 0) >= FEAT, math.sqrt(0.5), 1.0)
    info = kept[at : at + 1]
    count = info[:, 1:2] * 256.0 + info[:, 2:3]
    norm[0] = jnp.concatenate([jnp.broadcast_to(count, (1, HEADS)), rest], 0).T


def spread_rows():
    table = np.zeros((1 + FEAT + FEAT * FEAT, SYM), np.float32)
    table[0, 152] = 1
    for a in range(FEAT):
        table[1 + a, 128 + a] = 1
        for b in range(FEAT):
            o = (b - a) % FEAT
            at = o * FEAT + a if o < 8 else (144 + min(a, b) if o == 8 else (FEAT - o) * FEAT + b)
            table[1 + FEAT + a * FEAT + b, at] = 1
    return table


def expand_state(candidates, columns):
    spread = jnp.asarray(spread_rows(), bf16)
    expand = spread.shape[0]
    outs = [((expand, 1, columns), f32), ((1, HEADS, expand), f32)]
    return call(expand_kernel, outs, [], 32, 40_000_000, 1_000_000, [*candidates, spread])


def across(arrays, order):
    return [swap(array, "blk", s) if s else array for s, array in zip(order, arrays)]


def swap(array, axis, by):
    return lax.ppermute(array, axis, [(i, i ^ by) for i in range(lax.axis_size(axis))])


def two_groups(
    tokens_in, query_weight, key_weight, value_weight, conv_weight, prompt_lengths, decode_map
):
    width = tokens_in.shape[2]
    given = (tokens_in, query_weight, key_weight, value_weight)
    length, slot = prompt_lengths.reshape(1, 1), decode_map
    *parts, early, inputs = project(0, *given)
    sent = [across(parts, ORDER)]
    *parts, taps = project(1, inputs, *given[1:], length, early, conv_weight)
    sent.append(across(parts, ORDER))
    first = group_state(0, length, sent[0], taps, [])
    second = group_state(1, length, sent[1], taps, [first[2]])
    got = [swap(held[2], "blk", GROUP) for held in (first, second)]
    aug, qk, own = first
    num = local_part(aug, qk, 1000, [second[2]])
    early = finish(0, length, slot, num, own, got[0], qk, taps, [])
    aug, qk, own = second
    num = local_part(aug, qk, 5_000_000_000, [early[4]])
    *parts, total = finish(1, length, slot, num, own, got[1], qk, taps, [early[4], *early[:4]])
    results = across(parts, RETURN)
    beside = swap(total, "req", ROUTE[0])
    theirs = swap(hand_on(total, beside, []), "req", ROUTE[1])
    state, norm = expand_state([total, beside, theirs], width // lax.axis_size("blk"))
    mixed = place_tokens(results, [theirs])
    return (mixed, jnp.swapaxes(state, 0, 1), jnp.swapaxes(norm, 1, 2))


def from_behind(array, axis, by):
    devices = lax.axis_size(axis)
    pairs = [(i, i + by) for i in range(devices) if 0 <= i + by < devices]
    return lax.ppermute(array, axis, pairs)


def entering(part, axis, combine, identity):
    place = lax.axis_index(axis)
    gathered = jax.tree.map(lambda a: lax.all_gather(a, axis), part)
    state = jax.tree.map(lambda a, e: jnp.zeros_like(a) + jnp.asarray(e, a.dtype), part, identity)

    def one(turn, state):
        return combine(
            state, jax.tree.map(lambda a: lax.dynamic_index_in_dim(a, turn, 0, False), gathered)
        )

    return lax.fori_loop(0, place, one, state)


def features_last(x):
    half = x * FEAT ** (-0.25)
    outer = half[:, :, None, :] * half[:, None, :, :]
    flat = outer.reshape(half.shape[0], FEAT * FEAT, half.shape[2]) * math.sqrt(0.5)
    ones = jnp.ones((half.shape[0], 1, half.shape[2]), jnp.float32)
    return jnp.concatenate([ones, half, flat], 1)


def add_pair(earlier, later):
    return (earlier[0] + later[0], earlier[1] + later[1])


def route_slot(pair, decode_map):
    groups = lax.axis_size("req")
    slots = (jnp.arange(groups, dtype=jnp.int32) == decode_map[0]).astype(jnp.float32)
    sent = (slots[:, None, None] * pair[0][None], slots[:, None, None] * pair[1][None])
    got = (
        lax.all_to_all(sent[0], "req", split_axis=0, concat_axis=0, tiled=True),
        lax.all_to_all(sent[1], "req", split_axis=0, concat_axis=0, tiled=True),
    )
    return (jnp.sum(got[0], 0), jnp.sum(got[1], 0))


def reduce_blocks(pair):
    return (
        lax.psum_scatter(pair[0], "blk", scatter_dimension=1, tiled=True),
        lax.psum_scatter(pair[1], "blk", scatter_dimension=1, tiled=True),
    )


def any_blocks(
    tokens_in, query_weight, key_weight, value_weight, conv_weight, prompt_lengths, decode_map
):
    rows = tokens_in.shape[1]
    width = tokens_in.shape[2]
    blocks = lax.axis_size("blk")
    head_size = width // HEADS
    hi = lax.Precision.HIGHEST
    inputs = tokens_in[0]
    queries = jnp.einsum(
        "dk,td->kt", query_weight, inputs, preferred_element_type=jnp.float32
    ).reshape(HEADS, FEAT, rows)
    keys = jnp.einsum("dk,td->kt", key_weight, inputs, preferred_element_type=jnp.float32).reshape(
        HEADS, FEAT, rows
    )
    values = jnp.dot(inputs, value_weight, preferred_element_type=jnp.float32).astype(jnp.bfloat16)
    earlier = from_behind(values[rows - (CONV - 1) :], "blk", 1)
    extended = jnp.concatenate([earlier, values], 0).astype(jnp.float32)
    conv = jnp.zeros((rows, width), jnp.float32)
    for tap in range(CONV):
        conv = conv + conv_weight[tap][None, :] * extended[CONV - 1 - tap : CONV - 1 - tap + rows]
    conv_t = conv.astype(jnp.bfloat16).astype(jnp.float32).T.reshape(HEADS, head_size, rows)
    start = lax.axis_index("blk") * rows
    live = (start + jnp.arange(rows, dtype=jnp.int32) < prompt_lengths[0]).astype(jnp.float32)
    feat_q = features_last(queries)
    feat_k = features_last(keys) * live[None, None, :]
    own_state = jnp.einsum("hft,hct->hfc", feat_k, conv_t, precision=hi)
    own_norm = jnp.sum(feat_k, 2)
    zero_state = jnp.zeros_like(own_state)
    zero_norm = jnp.zeros_like(own_norm)
    prior_state, prior_norm = entering(
        (own_state, own_norm), "blk", add_pair, (zero_state, zero_norm)
    )
    causal = (jnp.arange(rows)[:, None] >= jnp.arange(rows)[None, :]).astype(jnp.float32)
    scores = jnp.einsum("hft,hfs->hts", feat_q, feat_k, precision=hi) * causal[None]
    num = jnp.einsum("hts,hcs->hct", scores, conv_t, precision=hi) + jnp.einsum(
        "hft,hfc->hct", feat_q, prior_state, precision=hi
    )
    den = (
        jnp.sum(scores, -1)
        + jnp.einsum("hft,hf->ht", feat_q, prior_norm, precision=hi)
        + (1.0 - live)[None, :]
    )
    result = jnp.where(live[None, None, :] > 0, num / den[:, None, :], 0.0)
    mixed = result.reshape(width, rows).T.reshape(1, rows, width).astype(jnp.bfloat16)
    state_flat = jnp.transpose(own_state, (1, 0, 2)).reshape(own_state.shape[1], width)
    pair = (state_flat, jnp.tile(own_norm.T, (1, blocks)))
    final = route_slot(reduce_blocks(pair), decode_map)
    return (mixed, final[0][None], final[1][None])


def solution(mesh):
    def on_device(*args):
        rows = args[0].shape[1]
        if mesh.shape["blk"] == 2 * GROUP and mesh.shape["req"] == 4 and rows == LANES:
            return two_groups(*args)
        return any_blocks(*args)

    return jax.shard_map(
        on_device,
        mesh=mesh,
        in_specs=(P("req", "blk", None), P(), P(), P(), P(), P("req"), P("req")),
        out_specs=(P("req", "blk", None), P("req", None, "blk"), P("req", None, None)),
        check_vma=False,
    )
```

```python
import functools
import math

import jax
import jax.numpy as jnp
import numpy as np
from jax import lax
from jax.experimental import pallas as pl
from jax.experimental.pallas import tpu as pltpu
from jax.sharding import PartitionSpec as P

HEADS = 16
FEAT = 16
CONV = 3

GROUP = 4
SYM = 160
LANES = 128
REST = SYM - LANES
EDGE, KEYS = 25, 27
INFO = 31
LOCAL = HEADS // GROUP // 2
ORDER = (0, 3, 2, 1)
RETURN = (0, 3, 2, 1)
f32 = jnp.float32
bf16 = jnp.bfloat16
NT = (((1,), (1,)), ((), ()))
NN = (((1,), (0,)), ((), ()))


def dot(a, b, dims=NN):
    return lax.dot_general(a, b, dims, preferred_element_type=f32)


def iota(shape, axis):
    return lax.broadcasted_iota(jnp.int32, shape, axis)


def symmetric(y, scale_square):
    twice = jnp.concatenate([y, y], 0)
    rows = [y * y * scale_square] + [y * twice[o : o + FEAT] for o in range(1, 8)]
    rest = jnp.where(iota((8, y.shape[1]), 0) == 0, 1.0, 0.0)
    return jnp.concatenate(rows + [y, y[:8] * y[8:], rest], 0)


def call(kernel, outs, scratch, limit, flops, moved, args, spaces=(), after=()):
    vmem = pl.BlockSpec(memory_space=pltpu.VMEM)
    given = [pl.BlockSpec(memory_space=space) for space in spaces]
    if after:
        body, plain = kernel, len(args)

        def kernel(*refs):
            body(*refs[:plain], *refs[plain + len(after) :])

    return pl.pallas_call(
        kernel,
        out_shape=[jax.ShapeDtypeStruct(shape, dtype) for shape, dtype in outs],
        in_specs=given
        + [vmem] * (len(args) - len(given))
        + [pl.BlockSpec(memory_space=pl.ANY)] * len(after),
        out_specs=[vmem] * len(outs),
        scratch_shapes=scratch,
        compiler_params=pltpu.CompilerParams(vmem_limit_bytes=int(limit * 2**20)),
        cost_estimate=pl.CostEstimate(flops=flops, bytes_accessed=moved, transcendentals=0),
    )(*args, *after)


TILES = (384, 512)
TILES_B = (896,)


def key_sums(keys):
    keyed, rows = keys.shape
    gram = dot(keys, keys, NT)
    same = iota((keyed, keyed), 0) // FEAT == iota((keyed, keyed), 1) // FEAT
    entry, lane = iota((FEAT, keyed), 0), iota((FEAT, keyed), 1)
    pick = (lax.rem(lane, FEAT) == entry).astype(bf16)
    folded = dot(pick, jnp.where(same, gram, 0.0).astype(bf16))
    plain = dot(jnp.ones((8, rows), bf16), keys, NT)
    mirror = lax.rem(entry - lax.rem(lane, FEAT) + FEAT, FEAT) == 9
    return jnp.where(mirror, plain[0:1], folded).astype(bf16)


def project_kernel(half, *refs):
    x, wq, wk, wv = refs[:4]
    refs = refs[4:]
    if half:
        length, early, conv, o0, o1, o2, o3, taps = refs[:8]
        refs = refs[8:]
    else:
        o0, o1, o2, o3, early, x_v = refs[:6]
        refs = refs[6:]
    rows = early.shape[1]
    width = wv.shape[1] // 2
    keyed = wq.shape[1] // 2
    place = lax.axis_index("blk")
    mine = lax.rem(place, GROUP)
    slab = width // GROUP
    if half:
        vt, qkt, taps_v = refs
        inputs = x[...]
        own_taps(conv, mine, taps, taps_v)
        both = jnp.concatenate([wk[:, keyed:], wq[:, keyed:]], 1)
        qkt[...] = dot(inputs, both).T.astype(bf16)
        at = 0
        for tile in TILES_B:
            weights = wv[:, width + at : width + at + tile]
            vt[at : at + tile, :] = dot(inputs, weights).T.astype(bf16)
            at += tile
    else:
        vt, qkt, wqk_v, wv_v, sems = refs
        first, second = pl.ds(0, keyed), pl.ds(keyed, keyed)
        needed = [
            pltpu.make_async_copy(x.at[0], x_v, sems.at[0]),
            pltpu.make_async_copy(wk.at[:, first], wqk_v.at[:, first], sems.at[1]),
            pltpu.make_async_copy(wq.at[:, first], wqk_v.at[:, second], sems.at[2]),
        ]
        copies, at = [], 0
        for j, tile in enumerate(TILES):
            cut = pl.ds(at, tile)
            copies.append(pltpu.make_async_copy(wv.at[:, cut], wv_v.at[:, cut], sems.at[3 + j]))
            at += tile
        for copy in (*needed, *copies):
            copy.start()
        for copy in needed:
            copy.wait()
        inputs = x_v[...]
        qkt[...] = dot(inputs, wqk_v[...]).T.astype(bf16)
        at = 0
        for tile, copy in zip(TILES, copies):
            copy.wait()
            vt[at : at + tile, :] = dot(inputs, wv_v[:, at : at + tile]).T.astype(bf16)
            at += tile
    part = keyed // GROUP
    for s, out in zip(ORDER, (o0, o1, o2, o3)):
        dest = mine ^ s
        out[0:slab, :] = vt[pl.ds(pl.multiple_of(slab * dest, 32), slab), :]
        for base, at in ((0, slab), (keyed, slab + part)):
            start = pl.multiple_of(base + part * dest, 32)
            out[at : at + part, :] = qkt[pl.ds(start, part), :]
    if not half:
        early[...] = qkt[0:keyed, :]
        return
    alive = place * rows + iota((1, rows), 1) < length[...]
    alive = jnp.where(alive, 1.0, 0.0).astype(bf16)
    sums = [key_sums(early[...] * alive), key_sums(qkt[0:keyed, :] * alive)]
    for out in (o0, o1, o2, o3):
        out[slab + 2 * part :, :] = jnp.concatenate(sums, 0)


def project(half, x, wq, wk, wv, *others):
    rows, width = x.shape[-2:]
    keyed = wq.shape[1]
    total = (width + 2 * keyed) // GROUP // 2 + (2 * FEAT if half else 0)
    outs = [((total, rows), bf16)] * GROUP
    scratch = [pltpu.VMEM((width // 2, rows), bf16), pltpu.VMEM((keyed, rows), bf16)]
    if half:
        slab = width // GROUP
        outs.append(((slab, 8), f32))
        scratch.append(pltpu.VMEM(((slab // 2 // LANES + 2) * LANES, 8), f32))
    else:
        outs += [((keyed // 2, rows), bf16), ((rows, width), bf16)]
        scratch += [
            pltpu.VMEM((width, keyed), bf16),
            pltpu.VMEM((width, width // 2), bf16),
            pltpu.SemaphoreType.DMA((3 + len(TILES),)),
        ]
    flops = rows * width * (width + 2 * keyed)
    kernel = functools.partial(project_kernel, half)
    limit = LIMIT_B if half else LIMIT_A
    args = [x, wq, wk, wv, *others]
    return call(kernel, outs, scratch, limit, flops, flops // rows, args, [] if half else [pltpu.HBM] * 4)


LIMIT_A = 53.1
LIMIT_B = 16


def own_taps(conv, mine, taps, taps_v):
    half = conv.shape[1] // 2
    slab = half // GROUP
    wide = taps_v.shape[0]
    start = jnp.minimum(slab * mine // LANES * LANES, half - wide)
    inside = pl.multiple_of(slab * mine - start, 32)
    for h in range(2):
        cut = conv[:, pl.ds(pl.multiple_of(half * h + start, LANES), wide)]
        padded = jnp.concatenate([cut, jnp.zeros((8 - CONV, wide), f32)], 0)
        for j in range(wide // LANES):
            rows = slice(j * LANES, (j + 1) * LANES)
            taps_v[rows, :] = padded[:, rows].T
        taps[h * slab : (h + 1) * slab, :] = taps_v[pl.ds(inside, slab), :]


def state_kernel(half, *refs):
    length, p0, p1, p2, p3 = refs[:5]
    taps, aug, qk, state, held = refs[5:]
    rows = p0.shape[1]
    place = lax.axis_index("blk")
    mine, group = lax.rem(place, GROUP), place // GROUP
    kept = held.shape[1]
    size = kept // LOCAL - 2 * FEAT
    values = LOCAL * size
    tokens = GROUP * rows
    for s, ref in zip(ORDER, (p0, p1, p2, p3)):
        held[mine ^ s] = ref[0:kept, :]
    if half:
        sums = p0[kept:, :].astype(f32) + p1[kept:, :].astype(f32)
        sums += p2[kept:, :].astype(f32) + p3[kept:, :].astype(f32)
        state[LOCAL * (size + REST) :, :] = sums.astype(bf16)
    for b in range(GROUP):
        qk[:, b * rows : (b + 1) * rows] = held[b, values:, :]
    alive = (group * tokens + iota((1, tokens), 1) < length[...]).astype(f32)
    token = iota((FEAT, tokens), 1)
    row = iota((FEAT, tokens), 0)
    marks = (row == 0) | ((row == 1) & (token == 0)) | ((row == 2) & (token == 1))
    marks = jnp.where(marks, alive, 0.0).astype(bf16)
    lane = iota((size, rows), 1)
    last = iota((REST, rows), 0)
    ends = iota((REST, rows), 1)
    ends = ((last == EDGE) & (ends == rows - 1)) | ((last == EDGE + 1) & (ends == rows - 2))
    ends = ends.astype(bf16)
    step = size + REST
    for h in range(LOCAL):
        cut = slice(h * size, (h + 1) * size)
        first = (half * LOCAL + h) * size
        tap = taps[first : first + size, :]
        tap = [jnp.broadcast_to(tap[:, t : t + 1], (size, rows)) for t in range(CONV)]
        before = [jnp.zeros((size, rows), f32)] * 2
        pieces = []
        for b in range(GROUP):
            now = held[b, cut, :].astype(f32)
            rolled = [pltpu.roll(now, 1, 1), pltpu.roll(now, 2, 1)]
            one = jnp.where(lane < 1, before[0], rolled[0])
            two = jnp.where(lane < 2, before[1], rolled[1])
            before = rolled
            mixed = tap[0] * now + tap[1] * one + tap[2] * two
            live = alive[:, b * rows : (b + 1) * rows]
            pieces.append(jnp.where(live > 0, mixed, 0.0).astype(bf16))
        aug_h = jnp.concatenate([jnp.concatenate(pieces, 1), marks], 0)
        aug[h] = aug_h
        y = qk[h * FEAT : (h + 1) * FEAT, :].astype(f32) * FEAT ** (-0.25)
        feats = symmetric(y, 1.0).astype(bf16)
        own = dot(aug_h, feats, NT)
        keys = pltpu.roll(own[size : size + 8, :LANES], KEYS % 8, 0)
        keys = jnp.concatenate([jnp.zeros((KEYS // 8 * 8, LANES), f32), keys], 0)
        edge = dot(ends, held[GROUP - 1, h * size : h * size + LANES, :], NT)
        rest = own[:, LANES:].T + edge + keys
        state[h * step : h * step + size, :] = own[:size, :LANES].astype(bf16)
        state[h * step + size : (h + 1) * step, :] = rest.astype(bf16)


def group_state(half, length, payloads, taps, after):
    total, rows = payloads[0].shape
    tokens = GROUP * rows
    extra = 2 * FEAT if half else 0
    outs = [
        ((LOCAL, LANES, tokens), bf16),
        ((2 * LOCAL * FEAT, tokens), bf16),
        (((total - extra) // LOCAL * LOCAL + extra, LANES), bf16),
    ]
    scratch = [pltpu.VMEM((GROUP, total - extra, rows), bf16)]
    kernel = functools.partial(state_kernel, half)
    args = [length, *payloads, taps]
    return call(kernel, outs, scratch, 32, 100_000_000, 1_000_000, args, after=after)


def local_kernel(aug, qk, num):
    _, _, tokens = aug.shape
    keyed = LOCAL * FEAT
    half = tokens // 2
    keys = qk[0:keyed, :].astype(f32).T.astype(bf16)
    queries = qk[keyed:, :]
    head = iota((keyed, tokens), 0) // FEAT
    causal = iota((half, half), 0) <= iota((half, half), 1)

    def scores(d):
        return 1.0 + d * (0.25 + d * 0.03125)

    for h in range(LOCAL):
        only = jnp.where(head == h, queries, jnp.zeros_like(queries))
        first = scores(dot(keys[:half], only[:, :half]))
        first = jnp.where(causal, first, 0.0).astype(bf16)
        num[h, :, 0:half] = dot(aug[h, :, 0:half], first)
        lower = scores(dot(keys[half:], only[:, half:]))
        lower = jnp.where(causal, lower, 0.0).astype(bf16)
        upper = scores(dot(keys[:half], only[:, half:])).astype(bf16)
        num[h, :, half:] = dot(aug[h, :, 0:half], upper) + dot(aug[h, :, half:], lower)


def local_part(aug, qk, flops, after):
    _, _, tokens = aug.shape
    return call(local_kernel, [(aug.shape, f32)], [], 32, flops, 1000, [aug, qk], after=after)[0]


def finish_kernel(half, *refs):
    if half:
        slot, *refs = refs
    length, num, own, got, qk, taps = refs[:6]
    refs = refs[6:]
    if half:
        other, *firsts = refs[:5]
        refs = refs[5:]
    r0, r1, r2, r3, route, scr = refs
    _, _, tokens = num.shape
    rows = tokens // GROUP
    size = taps.shape[0] // 2 // LOCAL
    keyed = LOCAL * FEAT
    place = lax.axis_index("blk")
    mine, group = lax.rem(place, GROUP), place // GROUP
    upper = group == 1
    weight = jnp.where(upper, 1.0, 0.0)
    alive = group * tokens + iota((1, tokens), 1) < length[...]
    first = (iota((size, LANES), 1) == 0) & upper
    aux = iota((LANES - size, SYM), 0)
    step = size + REST

    def whole(ref, h):
        rest = ref[h * step + size : (h + 1) * step, :].astype(f32)
        tail = [rest[KEYS : KEYS + 3], jnp.zeros((LANES - size - 3, LANES), f32)]
        main = [ref[h * step : h * step + size, :].astype(f32), *tail]
        return jnp.concatenate([jnp.concatenate(main, 0), rest.T], 1)

    finals = []
    for h in range(LOCAL):
        here, there = whole(own, h), whole(got, h)
        low = jnp.where(upper, there, here)
        high = jnp.where(upper, here, there)
        at = (half * LOCAL + h) * size
        tap = taps[at : at + size, :]
        last, second = low[:size, 153:154], low[:size, 154:155]
        change0 = tap[:, 1:2] * last + tap[:, 2:3] * second
        change1 = tap[:, 2:3] * last
        key0, key1 = high[size + 1 : size + 2, :], high[size + 2 : size + 3, :]
        body = low[:size] + change0 * key0 + change1 * key1
        tail = jnp.where(aux == 2, key1, low[size:])
        prior = jnp.concatenate([body, tail], 0)
        finals.append(jnp.concatenate([body + high[:size], low[size:] + high[size:]], 0))
        y = qk[keyed + h * FEAT : keyed + (h + 1) * FEAT, :].astype(f32) * FEAT ** (-0.25)
        feats = symmetric(y, 0.5).astype(bf16)
        all_num = num[h] + weight * dot(prior.astype(bf16), feats)
        den = jnp.where(alive, all_num[size : size + 1, :], 1.0)
        inverse = jnp.where(alive, 1.0 / den, 0.0)
        top = all_num[:size]
        extra = all_num[size + 2 : size + 3, 0:1]
        edge = top[:, :LANES] - jnp.where(first, change1 * extra, 0.0)
        top = jnp.concatenate([edge, top[:, LANES:]], 1)
        result = (top * inverse).astype(bf16)
        for b in range(GROUP):
            scr[b, h * size : (h + 1) * size, :] = result[:, b * rows : (b + 1) * rows]
    for j, (s, out) in enumerate(zip(RETURN, (r0, r1, r2, r3))):
        if half:
            out[0 : LOCAL * size, :] = firsts[j][...]
        out[half * LOCAL * size :, :] = scr[mine ^ s]
    if not half:
        for c in range(LOCAL):
            route[c * step : c * step + size, :] = finals[c][:size, :LANES].astype(bf16)
            route[c * step + size : (c + 1) * step, :] = finals[c][:, LANES:].T.astype(bf16)
        return
    count = length[...]
    for c in range(LOCAL):
        cut = slice(c * step, c * step + size)
        final = jnp.where(upper, finals[c][:size, :LANES], other[cut, :].astype(f32))
        route[cut, :] = final.astype(bf16)
        cut = slice(c * step + size, (c + 1) * step)
        final = jnp.where(upper, finals[c][:, LANES:].T, other[cut, :].astype(f32))
        if c == 0:
            row, lane = iota(final.shape, 0), iota(final.shape, 1)
            values = (slot[0], lax.shift_right_logical(count, 8), count & 255)
            for at, value in enumerate(values):
                final = jnp.where((row == INFO) & (lane == at), value.astype(f32), final)
        route[cut, :] = final.astype(bf16)
    sums = own[LOCAL * step :, :].astype(f32) + got[LOCAL * step :, :].astype(f32)
    route[LOCAL * step :, :] = sums.astype(bf16)


def finish(half, length, slot, num, own, got, qk, taps, other):
    _, _, tokens = num.shape
    rows = tokens // GROUP
    width = taps.shape[0] // 2
    outs = [(((1 + half) * width, rows), bf16)] * GROUP + [(own.shape, bf16)]
    scratch = [pltpu.VMEM((GROUP, width, rows), bf16)]
    args = [slot] * half + [length, num, own, got, qk, taps] + other
    kernel = functools.partial(finish_kernel, half)
    return call(kernel, outs, scratch, 32, 50_000_000, 20_000_000, args, [pltpu.SMEM] * half)


def place_kernel(r0, r1, r2, r3, mixed, scr, turned, sems):
    width = scr.shape[0]
    mine = lax.rem(lax.axis_index("blk"), GROUP)
    half = width // 2
    slab = half // GROUP
    for s, ref in zip(RETURN, (r0, r1, r2, r3)):
        start = pl.multiple_of(slab * (mine ^ s), 32)
        scr[pl.ds(start, slab), :] = ref[0:slab, :]
        scr[pl.ds(pl.multiple_of(half + start, 32), slab), :] = ref[slab:, :]
    copies = []
    for j in range(width // LANES):
        cut = slice(j * LANES, (j + 1) * LANES)
        turned[:, cut] = scr[cut, :].T
        if j % 2:
            cut = pl.ds((j - 1) * LANES, 2 * LANES)
            copies.append(
                pltpu.make_async_copy(turned.at[:, cut], mixed.at[0, :, cut], sems.at[j // 2])
            )
            copies[-1].start()
    for copy in copies:
        copy.wait()


def place_tokens(results, after):
    part, rows = results[0].shape
    width = part * GROUP

    def kernel(*refs):
        place_kernel(*refs[:GROUP], *refs[GROUP + len(after) :])

    vmem, hbm = (pl.BlockSpec(memory_space=space) for space in (pltpu.VMEM, pl.ANY))
    return pl.pallas_call(
        kernel,
        out_shape=jax.ShapeDtypeStruct((1, rows, width), bf16),
        in_specs=[vmem] * GROUP + [hbm] * len(after),
        out_specs=hbm,
        scratch_shapes=[
            pltpu.VMEM((width, rows), bf16),
            pltpu.VMEM((rows, width), bf16),
            pltpu.SemaphoreType.DMA((width // LANES // 2,)),
        ],
        compiler_params=pltpu.CompilerParams(vmem_limit_bytes=32 * 2**20),
        cost_estimate=pl.CostEstimate(flops=1000, bytes_accessed=1_000_000, transcendentals=0),
    )(*results, *after)


ROUTE = (2, 1)


def hand_on_kernel(own, got, out):
    other = (lax.axis_index("req") ^ ROUTE[1]).astype(f32)
    kept = jnp.zeros(out.shape, f32)
    step = (own.shape[0] - 2 * FEAT) // LOCAL
    for ref in (own, got):
        here = ref[step - FEAT : step, :].astype(f32)[INFO % FEAT :, 0:1] == other
        kept += jnp.where(here, ref[...].astype(f32), 0.0)
    out[...] = kept.astype(bf16)


def hand_on(own, got, after):
    args = [own, got]
    return call(hand_on_kernel, [(own.shape, bf16)], [], 32, 1000, 300_000, args, after=after)[0]


def expand_kernel(c0, c1, c2, spread, state, norm):
    me = lax.axis_index("req").astype(f32)
    kept = jnp.zeros(c0.shape, f32)
    step = (c0.shape[0] - 2 * FEAT) // LOCAL
    at = step - REST + INFO
    for ref in (c0, c1, c2):
        here = ref[step - FEAT : step, :].astype(f32)[INFO % FEAT :, 0:1] == me
        kept += jnp.where(here, ref[...].astype(f32), 0.0)
    size = state.shape[2] // LOCAL
    expand = state.shape[0]
    scale = jnp.where(iota((expand, size), 0) > FEAT, math.sqrt(0.5), 1.0)
    wholes = []
    for c in range(LOCAL):
        main = kept[c * step : c * step + size].astype(bf16)
        rest = kept[c * step + size : (c + 1) * step].astype(bf16)
        whole = dot(spread[:, :LANES], main, NT) + dot(spread[:, LANES:], rest)[:, :size]
        wholes.append(whole * scale)
    state[...] = jnp.concatenate(wholes, 1).reshape(state.shape)
    sums = kept[LOCAL * step :]
    keyed = HEADS * FEAT
    sums = jnp.concatenate([sums[:FEAT], sums[FEAT:]], 1)
    plain = jnp.concatenate([sums[9:], sums[:9]], 0) * FEAT ** (-0.25)
    products = sums * FEAT ** (-0.5)
    b = iota((FEAT, keyed), 0)
    entry = lax.rem(iota((FEAT, keyed), 1), FEAT)
    big = [jnp.where(entry == b, plain, 0.0)]
    for a in range(FEAT):
        mirror = b == (a + 9) % FEAT
        row = jnp.where(mirror, products[a : a + 1], products)
        big.append(jnp.where(entry == jnp.where(mirror, b, a), row, 0.0))
    big = jnp.concatenate(big, 0)
    gather = (iota((keyed, HEADS), 0) // FEAT == iota((keyed, HEADS), 1)).astype(bf16)
    rest = dot(big.astype(bf16), gather)
    rest = rest * jnp.where(iota(rest.shape, 0) >= FEAT, math.sqrt(0.5), 1.0)
    info = kept[at : at + 1]
    count = info[:, 1:2] * 256.0 + info[:, 2:3]
    norm[0] = jnp.concatenate([jnp.broadcast_to(count, (1, HEADS)), rest], 0).T


def spread_rows():
    table = np.zeros((1 + FEAT + FEAT * FEAT, SYM), np.float32)
    table[0, 152] = 1
    for a in range(FEAT):
        table[1 + a, 128 + a] = 1
        for b in range(FEAT):
            o = (b - a) % FEAT
            at = o * FEAT + a if o < 8 else (144 + min(a, b) if o == 8 else (FEAT - o) * FEAT + b)
            table[1 + FEAT + a * FEAT + b, at] = 1
    return table


def expand_state(candidates, columns):
    spread = jnp.asarray(spread_rows(), bf16)
    expand = spread.shape[0]
    outs = [((expand, 1, columns), f32), ((1, HEADS, expand), f32)]
    return call(expand_kernel, outs, [], 32, 40_000_000, 1_000_000, [*candidates, spread])


def across(arrays, order):
    return [swap(array, "blk", s) if s else array for s, array in zip(order, arrays)]


def swap(array, axis, by):
    return lax.ppermute(array, axis, [(i, i ^ by) for i in range(lax.axis_size(axis))])


def two_groups(
    tokens_in, query_weight, key_weight, value_weight, conv_weight, prompt_lengths, decode_map
):
    width = tokens_in.shape[2]
    given = (tokens_in, query_weight, key_weight, value_weight)
    length, slot = prompt_lengths.reshape(1, 1), decode_map
    *parts, early, inputs = project(0, *given)
    sent = [across(parts, ORDER)]
    *parts, taps = project(1, inputs, *given[1:], length, early, conv_weight)
    sent.append(across(parts, ORDER))
    first = group_state(0, length, sent[0], taps, [])
    second = group_state(1, length, sent[1], taps, [first[2]])
    got = [swap(held[2], "blk", GROUP) for held in (first, second)]
    aug, qk, own = first
    num = local_part(aug, qk, 1000, [second[2]])
    early = finish(0, length, slot, num, own, got[0], qk, taps, [])
    aug, qk, own = second
    num = local_part(aug, qk, 5_000_000_000, [early[4]])
    *parts, total = finish(1, length, slot, num, own, got[1], qk, taps, [early[4], *early[:4]])
    results = across(parts, RETURN)
    beside = swap(total, "req", ROUTE[0])
    theirs = swap(hand_on(total, beside, []), "req", ROUTE[1])
    state, norm = expand_state([total, beside, theirs], width // lax.axis_size("blk"))
    mixed = place_tokens(results, [theirs])
    return (mixed, jnp.swapaxes(state, 0, 1), jnp.swapaxes(norm, 1, 2))


def from_behind(array, axis, by):
    devices = lax.axis_size(axis)
    pairs = [(i, i + by) for i in range(devices) if 0 <= i + by < devices]
    return lax.ppermute(array, axis, pairs)


def entering(part, axis, combine, identity):
    place = lax.axis_index(axis)
    gathered = jax.tree.map(lambda a: lax.all_gather(a, axis), part)
    state = jax.tree.map(lambda a, e: jnp.zeros_like(a) + jnp.asarray(e, a.dtype), part, identity)

    def one(turn, state):
        return combine(
            state, jax.tree.map(lambda a: lax.dynamic_index_in_dim(a, turn, 0, False), gathered)
        )

    return lax.fori_loop(0, place, one, state)


def features_last(x):
    half = x * FEAT ** (-0.25)
    outer = half[:, :, None, :] * half[:, None, :, :]
    flat = outer.reshape(half.shape[0], FEAT * FEAT, half.shape[2]) * math.sqrt(0.5)
    ones = jnp.ones((half.shape[0], 1, half.shape[2]), jnp.float32)
    return jnp.concatenate([ones, half, flat], 1)


def add_pair(earlier, later):
    return (earlier[0] + later[0], earlier[1] + later[1])


def route_slot(pair, decode_map):
    groups = lax.axis_size("req")
    slots = (jnp.arange(groups, dtype=jnp.int32) == decode_map[0]).astype(jnp.float32)
    sent = (slots[:, None, None] * pair[0][None], slots[:, None, None] * pair[1][None])
    got = (
        lax.all_to_all(sent[0], "req", split_axis=0, concat_axis=0, tiled=True),
        lax.all_to_all(sent[1], "req", split_axis=0, concat_axis=0, tiled=True),
    )
    return (jnp.sum(got[0], 0), jnp.sum(got[1], 0))


def reduce_blocks(pair):
    return (
        lax.psum_scatter(pair[0], "blk", scatter_dimension=1, tiled=True),
        lax.psum_scatter(pair[1], "blk", scatter_dimension=1, tiled=True),
    )


def any_blocks(
    tokens_in, query_weight, key_weight, value_weight, conv_weight, prompt_lengths, decode_map
):
    rows = tokens_in.shape[1]
    width = tokens_in.shape[2]
    blocks = lax.axis_size("blk")
    head_size = width // HEADS
    hi = lax.Precision.HIGHEST
    inputs = tokens_in[0]
    queries = jnp.einsum(
        "dk,td->kt", query_weight, inputs, preferred_element_type=jnp.float32
    ).reshape(HEADS, FEAT, rows)
    keys = jnp.einsum("dk,td->kt", key_weight, inputs, preferred_element_type=jnp.float32).reshape(
        HEADS, FEAT, rows
    )
    values = jnp.dot(inputs, value_weight, preferred_element_type=jnp.float32).astype(jnp.bfloat16)
    earlier = from_behind(values[rows - (CONV - 1) :], "blk", 1)
    extended = jnp.concatenate([earlier, values], 0).astype(jnp.float32)
    conv = jnp.zeros((rows, width), jnp.float32)
    for tap in range(CONV):
        conv = conv + conv_weight[tap][None, :] * extended[CONV - 1 - tap : CONV - 1 - tap + rows]
    conv_t = conv.astype(jnp.bfloat16).astype(jnp.float32).T.reshape(HEADS, head_size, rows)
    start = lax.axis_index("blk") * rows
    live = (start + jnp.arange(rows, dtype=jnp.int32) < prompt_lengths[0]).astype(jnp.float32)
    feat_q = features_last(queries)
    feat_k = features_last(keys) * live[None, None, :]
    own_state = jnp.einsum("hft,hct->hfc", feat_k, conv_t, precision=hi)
    own_norm = jnp.sum(feat_k, 2)
    zero_state = jnp.zeros_like(own_state)
    zero_norm = jnp.zeros_like(own_norm)
    prior_state, prior_norm = entering(
        (own_state, own_norm), "blk", add_pair, (zero_state, zero_norm)
    )
    causal = (jnp.arange(rows)[:, None] >= jnp.arange(rows)[None, :]).astype(jnp.float32)
    scores = jnp.einsum("hft,hfs->hts", feat_q, feat_k, precision=hi) * causal[None]
    num = jnp.einsum("hts,hcs->hct", scores, conv_t, precision=hi) + jnp.einsum(
        "hft,hfc->hct", feat_q, prior_state, precision=hi
    )
    den = (
        jnp.sum(scores, -1)
        + jnp.einsum("hft,hf->ht", feat_q, prior_norm, precision=hi)
        + (1.0 - live)[None, :]
    )
    result = jnp.where(live[None, None, :] > 0, num / den[:, None, :], 0.0)
    mixed = result.reshape(width, rows).T.reshape(1, rows, width).astype(jnp.bfloat16)
    state_flat = jnp.transpose(own_state, (1, 0, 2)).reshape(own_state.shape[1], width)
    pair = (state_flat, jnp.tile(own_norm.T, (1, blocks)))
    final = route_slot(reduce_blocks(pair), decode_map)
    return (mixed, final[0][None], final[1][None])


def solution(mesh):
    def on_device(*args):
        rows = args[0].shape[1]
        if mesh.shape["blk"] == 2 * GROUP and mesh.shape["req"] == 4 and rows == LANES:
            return two_groups(*args)
        return any_blocks(*args)

    return jax.shard_map(
        on_device,
        mesh=mesh,
        in_specs=(P("req", "blk", None), P(), P(), P(), P(), P("req"), P("req")),
        out_specs=(P("req", "blk", None), P("req", None, "blk"), P("req", None, None)),
        check_vma=False,
    )
```
